32 devices in a mesh: grp: 4 (over x, core), exp: 8 (over z, y).
Axes of the slice: x: 2, y: 2, z: 4, core: 2. Of those that a mesh axis runs over, the one named last changes fastest.
Arguments:
- tokens: bfloat16 [8192, 2048], P(('grp', 'exp')), may hold values from -6 to 6
- expert_ids: int32 [8192, 1], P(('grp', 'exp')), may hold values from 0 to 7; in each aligned block of 256 rows (0 to 255, 256 to 511, ...) at most 64 rows name the same one
- gate_up_weight: bfloat16 [8, 2048, 1408], P('exp'), may hold values from -0.125 to 0.125
- down_weight: bfloat16 [8, 704, 2048], P('exp'), may hold values from -0.21875 to 0.21875
- grad_out: bfloat16 [8192, 2048], P(('grp', 'exp')), may hold values from -6 to 6
Outputs:
- mixed_out: bfloat16 [8192, 2048], P(('grp', 'exp'))
- grad_tokens: bfloat16 [8192, 2048], P(('grp', 'exp'))
- grad_gate_up: float32 [8, 2048, 1408], P('exp', 'grp')
- grad_down: float32 [8, 704, 2048], P('exp', None, 'grp')
The draws below stay inside these ranges and needn't reach their ends.
Inputs may be any that keep to these rules, and one draw needn't show every extreme that they name: `expert_ids`: among the 256 rows of one device (aligned blocks of rows), no expert is named more than 64 times; some device names one expert exactly 64 times.
All inputs are finite; a program needn't handle non-finite values.
Results may differ from the reference program's by a relative error of at most 0.0053.
Values may be sent and summed in bfloat16 or wider, within the bound.
No kernel may reach another device: no remote copies, remote signals or barrier semaphores. Data moves between devices by JAX's collectives and lax.ppermute only.
A program may use at most 128 MiB of HBM per device.

```python
import math
import jax
import jax.numpy as jnp
import numpy as np
from jax import lax

D = 2048
FF = 704
TOK_DEV = 256
EXPERTS = 8
CAPACITY = 64
TOKENS = 8192


def levels(key, shape, split, smallest, top_value):
    loudness, own = 1.0, jax.random.fold_in(key, 6)
    for axis_at, shards_of in split:
        draws = jnp.exp(jax.random.uniform(jax.random.fold_in(own, axis_at), (shards_of,), jnp.float32, smallest / len(split), top_value / len(split)))
        loudness = loudness * jnp.repeat(draws, shape[axis_at] // shards_of).reshape([-1 if axis == axis_at else 1 for axis in range(len(shape))])
    return loudness


def shared_out(stream_key, own, number, rows, number_of, top, most, skew):
    sequence = jax.random.permutation(stream_key, number_of)
    heavy_load, usual = portions_of(number_of, rows * top, most, skew, True), portions_of(number_of, rows * top, most, skew, False)
    places = jnp.arange(number_of)

    def named(lengths, rotation):
        used = int((lengths > 0).sum())
        fixed = max(1, used // 4)
        shifted = fixed + (places - fixed + rotation * (used - fixed)) % max(1, number_of - fixed)
        return jnp.zeros((number_of,), jnp.int32).at[sequence[jnp.where(places < fixed, places, shifted)]].set(jnp.asarray(lengths, jnp.int32))

    lengths = jnp.where(number % 4 == 0, named(heavy_load, number // 4), named(usual, number - number // 4 - 1))
    mixed = jax.random.permutation(jax.random.fold_in(own, 3), number_of)
    source_of, receiver = mixed[0:number_of // 2 * 2:2], mixed[1:number_of // 2 * 2:2]
    margin = jnp.minimum(lengths[source_of] - 1, most - lengths[receiver]) // 2
    margin = jnp.where((source_of == sequence[0]) | (receiver == sequence[0]) | (lengths[receiver] == 0), 0, jnp.maximum(margin, 0))
    shifted = jax.random.randint(jax.random.fold_in(own, 4), (number_of // 2,), 0, 1 << 20) % (margin + 1)
    lengths = lengths.at[source_of].add(-shifted).at[receiver].add(shifted)
    members = jnp.searchsorted(jnp.cumsum(lengths), jnp.arange(rows * top), side="right").astype(jnp.int32)
    listing = members.reshape(top, rows).T
    listing = listing[jax.random.permutation(jax.random.fold_in(own, 1), rows)]
    rotation = jax.random.randint(jax.random.fold_in(own, 2), (rows, 1), 0, top)
    return jnp.take_along_axis(listing, (jnp.arange(top)[None, :] + rotation) % top, axis=1)


def portions_of(count, total, most, lean, full):
    loads = [(1 << 20) // math.isqrt(standing ** lean) + 1 for standing in range(1, count + 1)]
    largest = most if full else min(most, max(-(-total // count), total * loads[0] // sum(loads)))
    least = 1 if total - largest >= count - 1 else 0
    holding, surplus = [largest] + [least] * (count - 1), total - largest - least * (count - 1)
    while surplus > 0:
        movable = [i for i in range(1, count) if holding[i] < largest] or [i for i in range(1, count) if holding[i] < most]
        mass, left = sum([loads[i] for i in movable]), surplus
        for i in movable:
            extra = min(most - holding[i], max(1, left * loads[i] // mass), surplus)
            holding[i] = holding[i] + extra
            surplus = surplus - extra
    return np.array(holding)


def bell_draw(own_key, shape, scale, limit, pieces=(), kind=jnp.bfloat16):
    result = scale * jax.random.normal(own_key, shape, jnp.float32)
    if pieces:
        result = result * levels(own_key, shape, pieces, -0.22, 0.18)
    return jnp.clip(result, -limit, limit).astype(kind)


def setup_inputs(seed: int = 0) -> dict:
    splits = jax.random.split(jax.random.key(seed), 6)
    tokens = bell_draw(splits[0], (TOKENS, D), 1.0, 6.0, ((0, 32),))
    expert_ids_keys = jax.random.split(jax.random.fold_in(splits[1], 1), TOKENS // TOK_DEV)
    expert_ids_turns = jax.random.permutation(jax.random.fold_in(splits[1], 3), TOKENS // TOK_DEV)
    expert_ids = jax.vmap(lambda own, number: shared_out(jax.random.fold_in(splits[1], 2), own, number, TOK_DEV, EXPERTS, 1, CAPACITY, 2))(expert_ids_keys, expert_ids_turns).reshape((TOKENS, 1))
    gate_up_weight = bell_draw(splits[2], (EXPERTS, D, 2 * FF), D ** -0.5, 0.125, ((0, 8),))
    down_weight = bell_draw(splits[3], (EXPERTS, FF, D), FF ** -0.5, 0.21875, ((0, 8),))
    grad_out = bell_draw(splits[4], (TOKENS, D), 1.0, 6.0, ((0, 32),))
    return {"tokens": tokens, "expert_ids": expert_ids, "gate_up_weight": gate_up_weight, "down_weight": down_weight, "grad_out": grad_out}


def reference(tokens, expert_ids, gate_up_weight, down_weight, grad_out):
    tile = 128
    count_rows, width = tokens.shape
    experts = gate_up_weight.shape[0]
    hidden_width = down_weight.shape[1]
    route = expert_ids[:, 0].astype(jnp.int32)
    onehot = (route[:, None] == jnp.arange(experts, dtype=jnp.int32)[None, :]).astype(jnp.int32)
    counts = jnp.sum(onehot, axis=0).astype(jnp.int32)
    padded = ((counts + tile - 1) // tile * tile).astype(jnp.int32)
    offsets = (jnp.cumsum(padded) - padded).astype(jnp.int32)
    ranks = jnp.sum((jnp.cumsum(onehot, axis=0).astype(jnp.int32) - 1) * onehot, axis=1).astype(jnp.int32)
    dest = (offsets[route] + ranks).astype(jnp.int32)
    total = count_rows + experts * tile
    tiles = total // tile
    sorted_x = jnp.zeros((total, width), jnp.bfloat16).at[dest].set(tokens)
    sorted_dy = jnp.zeros((total, width), jnp.bfloat16).at[dest].set(grad_out)
    ends = offsets + padded
    starts = (jnp.arange(tiles, dtype=jnp.int32) * tile).astype(jnp.int32)
    owner = jnp.minimum(jnp.sum((ends[None, :] <= starts[:, None]).astype(jnp.int32), axis=1), experts - 1).astype(jnp.int32)

    def step(carry, index):
        acc_gate_up, acc_down = carry
        expert = owner[index]
        first = (index * tile).astype(jnp.int32)
        rows_x = lax.dynamic_slice_in_dim(sorted_x, first, tile, 0)
        rows_dy = lax.dynamic_slice_in_dim(sorted_dy, first, tile, 0)
        weight_one = lax.dynamic_index_in_dim(gate_up_weight, expert, 0, keepdims=False)
        weight_two = lax.dynamic_index_in_dim(down_weight, expert, 0, keepdims=False)
        proj = jnp.dot(rows_x, weight_one, preferred_element_type=jnp.float32)
        gate = proj[:, :hidden_width]
        upper = proj[:, hidden_width:]
        sig = jax.nn.sigmoid(gate)
        silu_gate = gate * sig
        hidden = (silu_gate * upper).astype(jnp.bfloat16)
        branch = jnp.dot(hidden, weight_two, preferred_element_type=jnp.float32).astype(jnp.bfloat16)
        grad_hidden = jnp.dot(rows_dy, weight_two.T, preferred_element_type=jnp.float32)
        grad_proj = jnp.concatenate([grad_hidden * upper * sig * (1.0 + gate * (1.0 - sig)), grad_hidden * silu_gate], axis=1).astype(jnp.bfloat16)
        grad_branch = jnp.dot(grad_proj, weight_one.T, preferred_element_type=jnp.float32).astype(jnp.bfloat16)
        part_one = jnp.dot(rows_x.T, grad_proj, preferred_element_type=jnp.float32)
        part_two = jnp.dot(hidden.T, rows_dy, preferred_element_type=jnp.float32)
        acc_gate_up = acc_gate_up.at[expert].add(part_one)
        acc_down = acc_down.at[expert].add(part_two)
        return (acc_gate_up, acc_down), (branch, grad_branch)

    init = (jnp.zeros(gate_up_weight.shape, jnp.float32), jnp.zeros(down_weight.shape, jnp.float32))
    (grad_gate_up, grad_down), (branches, grad_branches) = lax.scan(step, init, jnp.arange(tiles, dtype=jnp.int32))
    branches = branches.reshape(total, width)
    grad_branches = grad_branches.reshape(total, width)
    mixed_out = (tokens.astype(jnp.float32) + branches[dest].astype(jnp.float32)).astype(jnp.bfloat16)
    grad_tokens = (grad_out.astype(jnp.float32) + grad_branches[dest].astype(jnp.float32)).astype(jnp.bfloat16)
    return (mixed_out, grad_tokens, grad_gate_up, grad_down)
```

```python
import jax
import jax.numpy as jnp
from jax import lax
from jax.experimental import pallas as pl
from jax.experimental.pallas import tpu as pltpu
from jax.sharding import PartitionSpec as P

VMEM_BYTES = 48 * 1024 * 1024


def dot(left, right, dims):
    return lax.dot_general(left, right, (dims, ((), ())), preferred_element_type=jnp.float32)


def route_kernel(experts, cap, rel_ref, data_ref, place_ref, *block_refs):
    rows = rel_ref.shape[0]
    slots = experts * cap

    @pl.when(pl.program_id(0) == 0)
    def _():
        rel = rel_ref[...]
        onehot = lax.broadcasted_iota(jnp.int32, (rows, 128), 1) == rel
        before = lax.broadcasted_iota(jnp.int32, (rows, rows), 1) < lax.broadcasted_iota(jnp.int32, (rows, rows), 0)
        ranks = dot(before.astype(jnp.bfloat16), onehot.astype(jnp.bfloat16), ((1,), (0,)))
        rank = jnp.sum(jnp.where(onehot, ranks, 0.0), axis=1, keepdims=True).astype(jnp.int32)
        target = rel * cap + rank
        place_ref[...] = (lax.broadcasted_iota(jnp.int32, (rows, slots), 1) == target).astype(jnp.bfloat16)

    place_kernel(experts, cap, place_ref, data_ref, *block_refs)


def place_kernel(experts, cap, place_ref, data_ref, *block_refs):
    moved = dot(place_ref[...], data_ref[...], ((0,), (0,))).astype(jnp.bfloat16)
    for index in range(experts):
        block_refs[index][...] = moved[index * cap : (index + 1) * cap]


def combine_kernel(place_ref, data_ref, *refs):
    back = jnp.concatenate([ref[...] for ref in refs[:-1]], axis=0)
    total = data_ref[...].astype(jnp.float32) + dot(place_ref[...], back, ((1,), (0,)))
    refs[-1][...] = total.astype(jnp.bfloat16)


def params():
    return pltpu.CompilerParams(vmem_limit_bytes=VMEM_BYTES, dimension_semantics=("arbitrary",))


def cost(rows, slots, width):
    return pl.CostEstimate(
        flops=2 * rows * slots * width, bytes_accessed=2 * (rows + slots) * width, transcendentals=0
    )


def route_and_place(rel, data, experts, cap):
    rows, width = data.shape
    slots = experts * cap
    step = width // 4
    return pl.pallas_call(
        lambda *refs: route_kernel(experts, cap, *refs),
        grid=(width // step,),
        in_specs=[pl.BlockSpec((rows, 1), lambda i: (0, 0)), pl.BlockSpec((rows, step), lambda i: (0, i))],
        out_specs=[pl.BlockSpec((rows, slots), lambda i: (0, 0))]
        + [pl.BlockSpec((cap, step), lambda i: (0, i))] * experts,
        out_shape=[jax.ShapeDtypeStruct((rows, slots), jnp.bfloat16)]
        + [jax.ShapeDtypeStruct((cap, width), jnp.bfloat16)] * experts,
        compiler_params=params(),
        cost_estimate=cost(rows, slots, width),
        name="route_and_place",
    )(rel, data)


def place(placing, data, experts, cap):
    rows, width = data.shape
    slots = experts * cap
    step = width // 4
    return pl.pallas_call(
        lambda *refs: place_kernel(experts, cap, *refs),
        grid=(width // step,),
        in_specs=[pl.BlockSpec((rows, slots), lambda i: (0, 0)), pl.BlockSpec((rows, step), lambda i: (0, i))],
        out_specs=[pl.BlockSpec((cap, step), lambda i: (0, i))] * experts,
        out_shape=[jax.ShapeDtypeStruct((cap, width), jnp.bfloat16)] * experts,
        compiler_params=params(),
        cost_estimate=cost(rows, slots, width),
        name="place",
    )(placing, data)


def combine(placing, data, blocks):
    rows, width = data.shape
    cap = blocks[0].shape[0]
    slots = placing.shape[1]
    step = width // 4
    return pl.pallas_call(
        combine_kernel,
        grid=(width // step,),
        in_specs=[pl.BlockSpec((rows, slots), lambda i: (0, 0)), pl.BlockSpec((rows, step), lambda i: (0, i))]
        + [pl.BlockSpec((cap, step), lambda i: (0, i))] * len(blocks),
        out_specs=pl.BlockSpec((rows, step), lambda i: (0, i)),
        out_shape=jax.ShapeDtypeStruct((rows, width), jnp.bfloat16),
        compiler_params=params(),
        cost_estimate=cost(rows, slots, width),
        name="combine",
    )(placing, data, *blocks)


def exchange(blocks):
    experts = len(blocks)
    moved = {0: blocks[0]}
    for mask in range(experts - 1, 0, -1):
        moved[mask] = lax.ppermute(blocks[mask], "exp", [(i, i ^ mask) for i in range(experts)])
    return [moved[mask] for mask in range(experts)]


def halving_sum(parts):
    count = len(parts)
    bit = 1
    while bit < count:
        pairs = [(i, i ^ bit) for i in range(count)]
        for q in range(count - 2 * bit, -1, -2 * bit):
            got = [lax.ppermute(part.astype(jnp.bfloat16), "grp", pairs) for part in parts[q | bit]]
            parts[q] = [part + piece.astype(jnp.float32) for part, piece in zip(parts[q], got)]
        bit *= 2
    return parts[0]


def body(tokens, expert_ids, gate_up_weight, down_weight, grad_out):
    rows, width = tokens.shape
    experts = lax.axis_size("exp")
    groups = lax.axis_size("grp")
    cap = 2 * rows // experts
    rel = expert_ids ^ lax.axis_index("exp").astype(jnp.int32)
    placing, *sent_x = route_and_place(rel, tokens, experts, cap)
    sent_dy = place(placing, grad_out, experts, cap)
    slot_x = jnp.concatenate(exchange(sent_x), axis=0)
    slot_dy = jnp.concatenate(exchange(sent_dy), axis=0)
    weight_one = gate_up_weight[0]
    weight_two = down_weight[0]
    hidden_width = weight_two.shape[0]

    proj = dot(slot_x, weight_one, ((1,), (0,)))
    gate = proj[:, :hidden_width]
    upper = proj[:, hidden_width:]
    sigma = jax.nn.sigmoid(gate)
    silu_gate = gate * sigma
    hidden = (silu_gate * upper).astype(jnp.bfloat16)
    branch = dot(hidden, weight_two, ((1,), (0,))).astype(jnp.bfloat16)
    back_out = exchange([branch[i * cap : (i + 1) * cap] for i in range(experts)])

    grad_hidden = dot(slot_dy, weight_two, ((1,), (1,)))
    grad_proj = jnp.concatenate(
        [grad_hidden * upper * sigma * (1.0 + gate * (1.0 - sigma)), grad_hidden * silu_gate], axis=1
    ).astype(jnp.bfloat16)
    grad_branch = dot(grad_proj, weight_one, ((1,), (1,))).astype(jnp.bfloat16)
    back_grad = exchange([grad_branch[i * cap : (i + 1) * cap] for i in range(experts)])

    group = lax.axis_index("grp").astype(jnp.int32)
    share = width // groups
    parts = []
    for q in range(groups):
        start = (group ^ q) * share
        part_x = lax.dynamic_slice_in_dim(slot_x, start, share, 1)
        part_dy = lax.dynamic_slice_in_dim(slot_dy, start, share, 1)
        parts.append([dot(part_x, grad_proj, ((0,), (0,))), dot(hidden, part_dy, ((0,), (0,)))])
    grad_gate_up, grad_down = halving_sum(parts)

    mixed_out = combine(placing, tokens, back_out)
    grad_tokens = combine(placing, grad_out, back_grad)
    return (mixed_out, grad_tokens, grad_gate_up[None], grad_down[None])


def solution(mesh):
    in_specs = (
        P(("grp", "exp"), None),
        P(("grp", "exp"), None),
        P("exp", None, None),
        P("exp", None, None),
        P(("grp", "exp"), None),
    )
    out_specs = (
        P(("grp", "exp"), None),
        P(("grp", "exp"), None),
        P("exp", "grp", None),
        P("exp", None, "grp"),
    )
    return jax.shard_map(body, mesh=mesh, in_specs=in_specs, out_specs=out_specs, check_vma=False)
```

```python
import jax
import jax.numpy as jnp
from jax import lax
from jax.experimental import pallas as pl
from jax.experimental.pallas import tpu as pltpu
from jax.sharding import PartitionSpec as P

VMEM_BYTES = 48 * 1024 * 1024
SMALL = pl.CostEstimate(flops=1024, bytes_accessed=1024, transcendentals=0)
ROWS = 256


def dot(left, right, dims):
    return lax.dot_general(left, right, (dims, ((), ())), preferred_element_type=jnp.float32)


def params(grid=True):
    return pltpu.CompilerParams(
        vmem_limit_bytes=VMEM_BYTES, dimension_semantics=("arbitrary",) if grid else None
    )


def like(shape, dtype=jnp.bfloat16):
    return jax.ShapeDtypeStruct(shape, dtype)


def route_kernel(experts, cap, rel_ref, data_ref, place_ref, *block_refs):
    rows = rel_ref.shape[0]
    slots = experts * cap

    @pl.when(pl.program_id(0) == 0)
    def _():
        rel = rel_ref[...]
        onehot = lax.broadcasted_iota(jnp.int32, (rows, 128), 1) == rel
        before = lax.broadcasted_iota(jnp.int32, (rows, rows), 1) < lax.broadcasted_iota(jnp.int32, (rows, rows), 0)
        ranks = dot(before.astype(jnp.bfloat16), onehot.astype(jnp.bfloat16), ((1,), (0,)))
        rank = jnp.sum(jnp.where(onehot, ranks, 0.0), axis=1, keepdims=True).astype(jnp.int32)
        target = rel * cap + rank
        place_ref[...] = (lax.broadcasted_iota(jnp.int32, (rows, slots), 1) == target).astype(jnp.bfloat16)

    place_kernel(experts, cap, place_ref, data_ref, *block_refs)


def place_kernel(experts, cap, place_ref, data_ref, *block_refs):
    moved = dot(place_ref[...], data_ref[...], ((0,), (0,))).astype(jnp.bfloat16)
    for index in range(experts):
        block_refs[index][...] = moved[index * cap : (index + 1) * cap]


def combine_kernel(place_ref, data_ref, *refs):
    back = jnp.concatenate([ref[...] for ref in refs[:-1]], axis=0)
    total = data_ref[...].astype(jnp.float32) + dot(place_ref[...], back, ((1,), (0,)))
    refs[-1][...] = total.astype(jnp.bfloat16)


def join_rows(block_refs, out_ref):
    cap = block_refs[0].shape[0]
    for index, block_ref in enumerate(block_refs):
        out_ref[index * cap : (index + 1) * cap] = block_ref[...]


def split_rows(left_ref, right_ref, dims, outs):
    cap = outs[0].shape[0]
    each = max(1, ROWS // cap)
    for first in range(0, len(outs), each):
        result = dot(left_ref[first * cap : (first + each) * cap], right_ref[...], dims).astype(jnp.bfloat16)
        for index in range(each):
            outs[first + index][...] = result[index * cap : (index + 1) * cap]


def forward_kernel(*refs):
    count = (len(refs) - 6) // 2
    one_ref, two_ref, slot_ref, hidden_ref, upper_ref, silu_ref = refs[count : count + 6]
    wide = two_ref.shape[0]
    join_rows(refs[:count], slot_ref)

    @pl.loop(0, slot_ref.shape[0] // ROWS)
    def _(step):
        here = pl.ds(pl.multiple_of(step * ROWS, ROWS), ROWS)
        proj = dot(slot_ref[here], one_ref[...], ((1,), (0,)))
        gate = proj[:, :wide]
        upper = proj[:, wide:]
        sigma = 1.0 / (1.0 + jnp.exp(-gate))
        silu = gate * sigma
        hidden_ref[here] = (silu * upper).astype(jnp.bfloat16)
        upper_ref[here] = upper * sigma * (1.0 + gate * (1.0 - sigma))
        silu_ref[here] = silu

    split_rows(hidden_ref, two_ref, ((1,), (0,)), refs[count + 6 :])


def grad_proj_kernel(*refs):
    two_ref, upper_ref, silu_ref, slot_ref, out_ref = refs[-5:]
    join_rows(refs[:-5], slot_ref)

    @pl.loop(0, slot_ref.shape[0] // ROWS)
    def _(step):
        here = pl.ds(pl.multiple_of(step * ROWS, ROWS), ROWS)
        grad_hidden = dot(slot_ref[here], two_ref[...], ((1,), (1,)))
        both = jnp.concatenate([grad_hidden * upper_ref[here], grad_hidden * silu_ref[here]], axis=1)
        out_ref[here] = both.astype(jnp.bfloat16)


def grad_branch_kernel(grad_ref, one_ref, *outs):
    split_rows(grad_ref, one_ref, ((1,), (1,)), outs)


def weight_kernel(number_ref, x_ref, dy_ref, grad_ref, hidden_ref, *refs):
    up_ref, down_ref = refs[-2:]
    up = dot(x_ref[...], grad_ref[...], ((0,), (0,)))
    down = dot(hidden_ref[...], dy_ref[...], ((0,), (0,)))
    for index in range(0, len(refs) - 2, 2):
        up = up + refs[index][...].astype(jnp.float32)
        down = down + refs[index + 1][...].astype(jnp.float32)
    up_ref[...] = up.astype(up_ref.dtype)
    down_ref[...] = down.astype(down_ref.dtype)


def route_and_place(rel, data, experts, cap):
    rows, width = data.shape
    slots = experts * cap
    step = width // 4
    return pl.pallas_call(
        lambda *refs: route_kernel(experts, cap, *refs),
        grid=(width // step,),
        in_specs=[pl.BlockSpec((rows, 1), lambda i: (0, 0)), pl.BlockSpec((rows, step), lambda i: (0, i))],
        out_specs=[pl.BlockSpec((rows, slots), lambda i: (0, 0))]
        + [pl.BlockSpec((cap, step), lambda i: (0, i))] * experts,
        out_shape=[like((rows, slots))] + [like((cap, width))] * experts,
        compiler_params=params(),
        cost_estimate=SMALL,
        name="route_and_place",
    )(rel, data)


def place(placing, data, experts, cap):
    rows, width = data.shape
    slots = experts * cap
    step = width // 4
    return pl.pallas_call(
        lambda *refs: place_kernel(experts, cap, *refs),
        grid=(width // step,),
        in_specs=[pl.BlockSpec((rows, slots), lambda i: (0, 0)), pl.BlockSpec((rows, step), lambda i: (0, i))],
        out_specs=[pl.BlockSpec((cap, step), lambda i: (0, i))] * experts,
        out_shape=[like((cap, width))] * experts,
        compiler_params=params(),
        cost_estimate=SMALL,
        name="place",
    )(placing, data)


def combine(placing, data, blocks):
    rows, width = data.shape
    cap = blocks[0].shape[0]
    slots = placing.shape[1]
    step = width // 4
    return pl.pallas_call(
        combine_kernel,
        grid=(width // step,),
        in_specs=[pl.BlockSpec((rows, slots), lambda i: (0, 0)), pl.BlockSpec((rows, step), lambda i: (0, i))]
        + [pl.BlockSpec((cap, step), lambda i: (0, i))] * len(blocks),
        out_specs=pl.BlockSpec((rows, step), lambda i: (0, i)),
        out_shape=like((rows, width)),
        compiler_params=params(),
        cost_estimate=SMALL,
        name="combine",
    )(placing, data, *blocks)


def forward(blocks, weight_one, weight_two):
    slots = len(blocks) * blocks[0].shape[0]
    wide, width = weight_two.shape
    return pl.pallas_call(
        forward_kernel,
        out_shape=[
            like((slots, width)),
            like((slots, wide)),
            like((slots, wide), jnp.float32),
            like((slots, wide), jnp.float32),
        ]
        + [like(blocks[0].shape)] * len(blocks),
        compiler_params=params(False),
        cost_estimate=SMALL,
        name="forward",
    )(*blocks, weight_one, weight_two)


def grad_of_proj(blocks, weight_two, upper, silu):
    slots = len(blocks) * blocks[0].shape[0]
    wide, width = weight_two.shape
    return pl.pallas_call(
        grad_proj_kernel,
        out_shape=[like((slots, width)), like((slots, 2 * wide))],
        compiler_params=params(False),
        cost_estimate=SMALL,
        name="grad_proj",
    )(*blocks, weight_two, upper, silu)


def grad_of_branch(grad_proj, weight_one, experts, cap):
    return pl.pallas_call(
        grad_branch_kernel,
        out_shape=[like((cap, weight_one.shape[0]))] * experts,
        compiler_params=params(False),
        cost_estimate=SMALL,
        name="grad_branch",
    )(grad_proj, weight_one)


def weight_part(number, groups, slot_x, slot_dy, grad_proj, hidden, received, dtype):
    slots, width = slot_x.shape
    share = width // groups
    wide = hidden.shape[1]
    outs = [like((share, 2 * wide), dtype), like((wide, share), dtype)]

    def whole(array):
        return pl.BlockSpec(array.shape, lambda i, number_ref: (0, 0))

    column = pl.BlockSpec((slots, share), lambda i, number_ref: (0, number_ref[0]))
    return pl.pallas_call(
        weight_kernel,
        grid_spec=pltpu.PrefetchScalarGridSpec(
            num_scalar_prefetch=1,
            grid=(1,),
            in_specs=[column, column, whole(grad_proj), whole(hidden)] + [whole(piece) for piece in received],
            out_specs=[whole(out) for out in outs],
        ),
        out_shape=outs,
        compiler_params=params(),
        cost_estimate=SMALL,
        name="weight_part",
    )(number, slot_x, slot_dy, grad_proj, hidden, *received)


def after(value, *earlier):
    return lax.optimization_barrier((value, *earlier))[0]


class Lane:
    def __init__(self, window):
        self.window = window
        self.done = []

    def send(self, value, axis, pairs, *earlier):
        if len(self.done) >= self.window:
            earlier = (self.done[-self.window], *earlier)
        if earlier:
            value = after(value, *earlier)
        self.done.append(lax.ppermute(value, axis, pairs))
        return self.done[-1]


def exchange(blocks, far, held={}):
    experts = len(blocks)
    half = experts // 2
    moved = {0: blocks[0]}
    for mask in range(half - 1, -1, -1):
        pairs = [(i, i ^ (mask + half)) for i in range(experts)]
        moved[mask + half] = far.send(blocks[mask + half], "exp", pairs, *held.get(mask, ()))
        if mask:
            pairs = [(i, i ^ mask) for i in range(experts)]
            moved[mask] = lax.ppermute(after(blocks[mask], far.done[-1]), "exp", pairs)
    return [moved[mask] for mask in range(experts)]


def body(tokens, expert_ids, gate_up_weight, down_weight, grad_out):
    rows, width = tokens.shape
    experts = lax.axis_size("exp")
    groups = lax.axis_size("grp")
    cap = 2 * rows // experts
    weight_one = gate_up_weight[0]
    weight_two = down_weight[0]
    far = Lane(2)
    rel = expert_ids ^ lax.axis_index("exp").astype(jnp.int32)
    group = lax.axis_index("grp").astype(jnp.int32)

    placing, *sent_x = route_and_place(rel, tokens, experts, cap)
    sent_dy = place(placing, grad_out, experts, cap)
    blocks_x = exchange(sent_x, far)
    slot_x, hidden, upper, silu, *branch = forward(blocks_x, weight_one, weight_two)

    blocks_dy = exchange(sent_dy, far, {1: (hidden,)})
    slot_dy, grad_proj = grad_of_proj(blocks_dy, weight_two, upper, silu)
    grad_branch = grad_of_branch(grad_proj, weight_one, experts, cap)

    count = len(far.done)
    lanes = {}
    made = {}

    def weight_sum(q, bit):
        received = []
        low = bit // 2
        while low:
            pairs = [(i, i ^ low) for i in range(groups)]
            lane = lanes.setdefault(low, Lane(1))
            received += [lane.send(piece, "grp", pairs) for piece in weight_sum(q | low, low)]
            low //= 2
        dtype = jnp.float32 if bit == groups else jnp.bfloat16
        grad = grad_proj if made else after(grad_proj, first_out)
        made[q] = weight_part((group ^ q)[None], groups, slot_x, slot_dy, grad, hidden, received, dtype)
        return made[q]

    back_out = exchange(branch, far, {1: (grad_proj,), 0: (grad_branch[0],)})
    first_out = far.done[count]
    mixed_out = combine(placing, tokens, back_out)
    grad_gate_up, grad_down = weight_sum(0, groups)
    back_grad = exchange(grad_branch, far, {0: (mixed_out,)})
    back_grad[0] = after(back_grad[0], grad_gate_up)
    grad_tokens = combine(placing, grad_out, back_grad)
    return (mixed_out, grad_tokens, grad_gate_up[None], grad_down[None])


def solution(mesh):
    in_specs = (
        P(("grp", "exp"), None),
        P(("grp", "exp"), None),
        P("exp", None, None),
        P("exp", None, None),
        P(("grp", "exp"), None),
    )
    out_specs = (
        P(("grp", "exp"), None),
        P(("grp", "exp"), None),
        P("exp", "grp", None),
        P("exp", None, "grp"),
    )
    return jax.shard_map(body, mesh=mesh, in_specs=in_specs, out_specs=out_specs, check_vma=False)
```

```python
import jax
import jax.numpy as jnp
from jax import lax
from jax.experimental import pallas as pl
from jax.experimental.pallas import tpu as pltpu
from jax.sharding import PartitionSpec as P

SMALL = pl.CostEstimate(flops=1024, bytes_accessed=1024, transcendentals=0)
ROWS = 256


def dot(left, right, dims):
    return lax.dot_general(left, right, (dims, ((), ())), preferred_element_type=jnp.float32)


def params(mebibytes):
    return pltpu.CompilerParams(vmem_limit_bytes=mebibytes * 1024 * 1024, dimension_semantics=("arbitrary",))


def whole(array):
    return pl.BlockSpec(array.shape, lambda *index: (0,) * len(array.shape), pipeline_mode=pl.Buffered(1))


def like(shape, dtype=jnp.bfloat16):
    return jax.ShapeDtypeStruct(shape, dtype)


def route_kernel(experts, cap, rel_ref, data_ref, place_ref, *block_refs):
    rows = rel_ref.shape[1]
    slots = experts * cap

    @pl.when(pl.program_id(0) == 0)
    def _():
        rel = rel_ref[...]
        onehot = lax.broadcasted_iota(jnp.int32, (max(experts, 16), rows), 0) == rel
        before = lax.broadcasted_iota(jnp.int32, (rows, rows), 0) < lax.broadcasted_iota(jnp.int32, (rows, rows), 1)
        ranks = dot(onehot.astype(jnp.bfloat16), before.astype(jnp.bfloat16), ((1,), (0,)))
        rank = jnp.sum(jnp.where(onehot, ranks, 0.0), axis=0, keepdims=True).astype(jnp.int32)
        target = rel * cap + rank
        place_ref[...] = (lax.broadcasted_iota(jnp.int32, (slots, rows), 0) == target).astype(jnp.bfloat16)

    place_kernel(cap, place_ref, data_ref, *block_refs)


def place_kernel(cap, place_ref, data_ref, *block_refs):
    moved = dot(place_ref[...], data_ref[...], ((1,), (0,))).astype(jnp.bfloat16)
    for index, block_ref in enumerate(block_refs):
        block_ref[...] = moved[index * cap : (index + 1) * cap]


def combine_kernel(place_ref, data_ref, *refs):
    back = jnp.concatenate([ref[...] for ref in refs[:-1]], axis=0)
    total = data_ref[...].astype(jnp.float32) + dot(place_ref[...], back, ((0,), (0,)))
    refs[-1][...] = total.astype(jnp.bfloat16)


def join_rows(block_refs, out_ref):
    cap = block_refs[0].shape[0]
    for index, block_ref in enumerate(block_refs):
        out_ref[index * cap : (index + 1) * cap] = block_ref[...]


def split_rows(left_ref, right_ref, dims, outs):
    cap = outs[0].shape[0]
    each = max(1, ROWS // cap)
    for first in range(0, len(outs), each):
        result = dot(left_ref[first * cap : (first + each) * cap], right_ref[...], dims).astype(jnp.bfloat16)
        for index in range(each):
            outs[first + index][...] = result[index * cap : (index + 1) * cap]


def forward_kernel(*refs):
    count = (len(refs) - 6) // 2
    one_ref, two_ref, slot_ref, hidden_ref, upper_ref, silu_ref = refs[count : count + 6]
    wide = two_ref.shape[0]
    join_rows(refs[:count], slot_ref)

    @pl.loop(0, slot_ref.shape[0] // ROWS)
    def _(step):
        here = pl.ds(pl.multiple_of(step * ROWS, ROWS), ROWS)
        proj = dot(slot_ref[here], one_ref[...], ((1,), (0,)))
        gate = proj[:, :wide]
        upper = proj[:, wide:]
        sigma = 1.0 / (1.0 + jnp.exp(-gate))
        silu = gate * sigma
        hidden_ref[here] = (silu * upper).astype(jnp.bfloat16)
        upper_ref[here] = upper * sigma * (1.0 + gate * (1.0 - sigma))
        silu_ref[here] = silu

    split_rows(hidden_ref, two_ref, ((1,), (0,)), refs[count + 6 :])


def grad_proj_kernel(*refs):
    two_ref, upper_ref, silu_ref, slot_ref, out_ref = refs[-5:]
    join_rows(refs[:-5], slot_ref)

    @pl.loop(0, slot_ref.shape[0] // ROWS)
    def _(step):
        here = pl.ds(pl.multiple_of(step * ROWS, ROWS), ROWS)
        grad_hidden = dot(slot_ref[here], two_ref[...], ((1,), (1,)))
        both = jnp.concatenate([grad_hidden * upper_ref[here], grad_hidden * silu_ref[here]], axis=1)
        out_ref[here] = both.astype(jnp.bfloat16)


def grad_branch_kernel(grad_ref, one_ref, *outs):
    split_rows(grad_ref, one_ref, ((1,), (1,)), outs)


def weight_kernel(number_ref, x_ref, dy_ref, grad_ref, hidden_ref, *refs):
    out_ref = refs[-1]
    wide, half = grad_ref.shape[1], hidden_ref.shape[1]
    up = dot(x_ref[...], grad_ref[...], ((0,), (0,)))
    down = dot(dy_ref[...], hidden_ref[...], ((0,), (0,)))
    for ref in refs[:-1]:
        up = up + ref[:, :wide].astype(jnp.float32)
        down = down + ref[:, wide : wide + half].astype(jnp.float32)
    out_ref[:, :wide] = up.astype(jnp.bfloat16)
    out_ref[:, wide : wide + half] = down.astype(jnp.bfloat16)


def weight_end_kernel(number_ref, x_ref, dy_ref, grad_ref, hidden_ref, *refs):
    up_ref, down_ref = refs[-2:]
    share, wide = up_ref.shape
    up = dot(x_ref[...], grad_ref[...], ((0,), (0,)))
    down = dot(hidden_ref[...], dy_ref[...], ((0,), (0,)))
    row = lax.broadcasted_iota(jnp.int32, (share, share), 0)
    unit = (row == lax.broadcasted_iota(jnp.int32, (share, share), 1)).astype(jnp.bfloat16)
    for ref in refs[:-2]:
        up = up + ref[:, :wide].astype(jnp.float32)
        down = down + dot(ref[:, wide : wide + down.shape[0]], unit, ((0,), (0,)))
    up_ref[...] = up
    down_ref[...] = down


def route_and_place(rel, data, experts, cap):
    rows, width = data.shape
    slots = experts * cap
    step = width // 4
    return pl.pallas_call(
        lambda *refs: route_kernel(experts, cap, *refs),
        grid=(width // step,),
        in_specs=[whole(rel), pl.BlockSpec((rows, step), lambda i: (0, i))],
        out_specs=[pl.BlockSpec((slots, rows), lambda i: (0, 0))]
        + [pl.BlockSpec((cap, step), lambda i: (0, i))] * experts,
        out_shape=[like((slots, rows))] + [like((cap, width))] * experts,
        compiler_params=params(8),
        cost_estimate=SMALL,
        name="route_and_place",
    )(rel, data)


def place(placing, data, experts, cap):
    rows, width = data.shape
    step = width // 4
    return pl.pallas_call(
        lambda *refs: place_kernel(cap, *refs),
        grid=(width // step,),
        in_specs=[whole(placing), pl.BlockSpec((rows, step), lambda i: (0, i))],
        out_specs=[pl.BlockSpec((cap, step), lambda i: (0, i))] * experts,
        out_shape=[like((cap, width))] * experts,
        compiler_params=params(8),
        cost_estimate=SMALL,
        name="place",
    )(placing, data)


def combine(placing, data, blocks):
    rows, width = data.shape
    cap = blocks[0].shape[0]
    step = width // 4
    return pl.pallas_call(
        combine_kernel,
        grid=(width // step,),
        in_specs=[whole(placing), pl.BlockSpec((rows, step), lambda i: (0, i))]
        + [pl.BlockSpec((cap, step), lambda i: (0, i))] * len(blocks),
        out_specs=pl.BlockSpec((rows, step), lambda i: (0, i)),
        out_shape=like((rows, width)),
        compiler_params=params(8),
        cost_estimate=SMALL,
        name="combine",
    )(placing, data, *blocks)


def call(kernel, name, mebibytes, outs, *arrays):
    return pl.pallas_call(
        kernel,
        grid=(1,),
        in_specs=[whole(array) for array in arrays],
        out_specs=[whole(out) for out in outs],
        out_shape=outs,
        compiler_params=params(mebibytes),
        cost_estimate=SMALL,
        name=name,
    )(*arrays)


def weight_part(number, groups, slot_x, slot_dy, grad_proj, hidden, received, end):
    slots, width = slot_x.shape
    share = width // groups
    wide = hidden.shape[1]
    outs = [like((share, pl.cdiv(3 * wide, 128) * 128))]
    if end:
        outs = [like((share, 2 * wide), jnp.float32), like((wide, share), jnp.float32)]
    column = pl.BlockSpec((slots, share), lambda i, number_ref: (0, number_ref[0]), pipeline_mode=pl.Buffered(1))
    return pl.pallas_call(
        weight_end_kernel if end else weight_kernel,
        grid_spec=pltpu.PrefetchScalarGridSpec(
            num_scalar_prefetch=1,
            grid=(1,),
            in_specs=[column, column, whole(grad_proj), whole(hidden)] + [whole(piece) for piece in received],
            out_specs=[whole(out) for out in outs],
        ),
        out_shape=outs,
        compiler_params=params(20),
        cost_estimate=SMALL,
        name="weight_part",
    )(number, slot_x, slot_dy, grad_proj, hidden, *received)


def after(value, *earlier):
    if not earlier:
        return value
    return lax.optimization_barrier((value, *earlier))[0]


class Lane:
    def __init__(self, window):
        self.window = window
        self.done = []

    def send(self, value, axis, pairs, *earlier):
        if len(self.done) >= self.window:
            earlier = (self.done[-self.window], *earlier)
        self.done.append(lax.ppermute(after(value, *earlier), axis, pairs))
        return self.done[-1]


def exchange(blocks, far, held={}):
    experts = len(blocks)
    half = experts // 2
    moved = {0: blocks[0]}
    for mask in range(half - 1, -1, -1):
        pairs = [(i, i ^ (mask + half)) for i in range(experts)]
        moved[mask + half] = far.send(blocks[mask + half], "exp", pairs, *held.get(mask, ()))
        if mask:
            pairs = [(i, i ^ mask) for i in range(experts)]
            moved[mask] = lax.ppermute(after(blocks[mask], far.done[-1]), "exp", pairs)
    return [moved[mask] for mask in range(experts)]


def body(tokens, expert_ids, gate_up_weight, down_weight, grad_out):
    rows, width = tokens.shape
    experts = lax.axis_size("exp")
    groups = lax.axis_size("grp")
    cap = 2 * rows // experts
    weight_one = gate_up_weight[0]
    weight_two = down_weight[0]
    wide = weight_two.shape[0]
    slots = experts * cap
    block = like((cap, width))
    far = Lane(3)
    rel = expert_ids.reshape(1, rows) ^ lax.axis_index("exp").astype(jnp.int32)
    group = lax.axis_index("grp").astype(jnp.int32)

    placing, *sent_x = route_and_place(rel, tokens, experts, cap)
    sent_dy = place(placing, grad_out, experts, cap)
    blocks_x = exchange(sent_x, far)
    outs = [like((slots, width)), like((slots, wide))] + [like((slots, wide), jnp.float32)] * 2 + [block] * experts
    slot_x, hidden, upper, silu, *branch = call(forward_kernel, "forward", 26, outs, *blocks_x, weight_one, weight_two)

    blocks_dy = exchange(sent_dy, far, {0: (hidden,)})
    outs = [like((slots, width)), like((slots, 2 * wide))]
    slot_dy, grad_proj = call(grad_proj_kernel, "grad_proj", 16, outs, *blocks_dy, weight_two, upper, silu)
    grad_branch = call(grad_branch_kernel, "grad_branch", 14, [block] * experts, grad_proj, weight_one)

    first_out = len(far.done)
    back_out = exchange(branch, far, {0: (grad_proj,)})
    lanes = {}
    far_out = far.done[first_out:]
    near_out = back_out[experts // 2 - 1 : 0 : -1]
    gates = iter([far_out[:2], [far_out[2], near_out[0], grad_branch[0]], [far_out[3], near_out[1]]])

    def weight_sum(q, bit):
        received = []
        low = bit // 2
        while low:
            pairs = [(i, i ^ low) for i in range(groups)]
            (piece,) = weight_sum(q | low, low)
            received.append(lanes.setdefault(low, Lane(1)).send(piece, "grp", pairs))
            low //= 2
        grad = after(grad_proj, *([] if bit == groups else next(gates, [])))
        return weight_part((group ^ q)[None], groups, slot_x, slot_dy, grad, hidden, received, bit == groups)

    grad_gate_up, grad_down = weight_sum(0, groups)
    mixed_out = combine(placing, tokens, back_out)
    back_grad = exchange(grad_branch, far, {0: (mixed_out,)})
    back_grad[0] = after(back_grad[0], grad_gate_up)
    grad_tokens = combine(placing, grad_out, back_grad)
    return (mixed_out, grad_tokens, grad_gate_up[None], grad_down[None])


def solution(mesh):
    in_specs = (
        P(("grp", "exp"), None),
        P(("grp", "exp"), None),
        P("exp", None, None),
        P("exp", None, None),
        P(("grp", "exp"), None),
    )
    out_specs = (
        P(("grp", "exp"), None),
        P(("grp", "exp"), None),
        P("exp", "grp", None),
        P("exp", None, "grp"),
    )
    return jax.shard_map(body, mesh=mesh, in_specs=in_specs, out_specs=out_specs, check_vma=False)
```

```python
import jax
import jax.numpy as jnp
from jax import lax
from jax.experimental import pallas as pl
from jax.experimental.pallas import tpu as pltpu
from jax.sharding import PartitionSpec as P

SMALL = pl.CostEstimate(flops=1024, bytes_accessed=1024, transcendentals=0)
BF16 = jnp.bfloat16
F32 = jnp.float32
ROWS = ((0,), (0,))
COLS = ((1,), (1,))
PLAIN = ((1,), (0,))


def dot(left, right, dims):
    return lax.dot_general(left, right, (dims, ((), ())), preferred_element_type=F32)


def like(shape, dtype=BF16):
    return jax.ShapeDtypeStruct(shape, dtype)


def call(kernel, name, mebibytes, outs, scratch, arrays, small=(), scalars=()):
    hbm = pl.BlockSpec(memory_space=pltpu.HBM)
    return pl.pallas_call(
        kernel,
        in_specs=[pl.BlockSpec(memory_space=pltpu.SMEM)] * len(scalars)
        + [pl.BlockSpec(memory_space=pltpu.VMEM)] * len(small)
        + [hbm] * len(arrays),
        out_specs=[hbm] * len(outs),
        out_shape=outs,
        scratch_shapes=scratch,
        compiler_params=pltpu.CompilerParams(vmem_limit_bytes=mebibytes * 1024 * 1024),
        cost_estimate=SMALL,
        name=name,
    )(*scalars, *small, *arrays)


class Copies:
    def __init__(self, sems):
        self.sems = sems
        self.used = 0

    def start(self, source, target):
        copy = pltpu.make_async_copy(source, target, self.sems.at[self.used])
        self.used += 1
        copy.start()
        return copy


def wait(copies):
    for copy in copies:
        copy.wait()


def place_kernel(part, cap, rel_ref, tokens_ref, grad_ref, *refs):
    blocks, (data, moved, sems) = refs[:-3], refs[-3:]
    experts = len(blocks)
    rows, width = tokens_ref.shape
    copies = Copies(sems)
    loads = [copies.start(ref, data.at[:, side * width : (side + 1) * width]) for side, ref in enumerate((tokens_ref, grad_ref))]
    placing = placing_of(rel_ref[...], experts, part, cap)
    stores = []
    for side in range(2):
        here = slice(side * width, (side + 1) * width)
        loads[side].wait()
        moved[:, here] = dot(placing, data[:, here], PLAIN).astype(BF16)
        for index, block in enumerate(blocks):
            stores.append(copies.start(moved.at[index * cap : (index + 1) * cap, here], block.at[:, here]))
    wait(stores)


def placing_of(rel, experts, part, cap):
    rows = rel.shape[1]
    onehot = lax.broadcasted_iota(jnp.int32, (max(experts, 16), rows), 0) == rel
    before = lax.broadcasted_iota(jnp.int32, (rows, rows), 0) < lax.broadcasted_iota(jnp.int32, (rows, rows), 1)
    ranks = dot(onehot.astype(BF16), before.astype(BF16), PLAIN)
    rank = jnp.sum(jnp.where(onehot, ranks, 0.0), axis=0, keepdims=True).astype(jnp.int32) - part * cap
    target = jnp.where((rank >= 0) & (rank < cap), rel * cap + rank, -1)
    return (lax.broadcasted_iota(jnp.int32, (experts * cap, rows), 0) == target).astype(BF16)


def expert_kernel(*refs):
    count = (len(refs) - 12) // 2
    blocks, (one_ref, two_ref), outs = refs[:count], refs[count : count + 2], refs[count + 2 : 2 * count + 2]
    slot_out, proj_out, hidden_out, slot, one, two, back, proj, hidden, sems = refs[2 * count + 2 :]
    cap = blocks[0].shape[0]
    wide, width = two.shape
    copies = Copies(sems)
    loads = [copies.start(block, slot.at[index * cap : (index + 1) * cap]) for index, block in enumerate(blocks)]
    one_load = copies.start(one_ref, one)
    two_load = copies.start(two_ref, two)
    wait(loads)
    stores = [copies.start(slot, slot_out)]
    one_load.wait()
    both = dot(slot[:, :width], one[...], PLAIN)
    gate, upper = both[:, :wide], both[:, wide:]
    sigma = 1.0 / (1.0 + jnp.exp(-gate))
    silu = gate * sigma
    hidden[...] = (silu * upper).astype(BF16)
    stores.append(copies.start(hidden, hidden_out))
    two_load.wait()
    grad_hidden = dot(slot[:, width:], two[...], COLS)
    proj[...] = jnp.concatenate(
        [grad_hidden * upper * sigma * (1.0 + gate * (1.0 - sigma)), grad_hidden * silu], axis=1
    ).astype(BF16)
    stores.append(copies.start(proj, proj_out))
    back[:, :width] = dot(hidden[...], two[...], PLAIN).astype(BF16)
    back[:, width:] = dot(proj[...], one[...], COLS).astype(BF16)
    stores += [copies.start(back.at[index * cap : (index + 1) * cap], out) for index, out in enumerate(outs)]
    wait(stores)


def weight_kernel(end, parts, pieces, number_ref, *refs):
    sources, refs = refs[: 3 * parts], refs[3 * parts :]
    more, refs = refs[: sum(pieces)], refs[sum(pieces) :]
    results, sems = refs[-3 if end else -2 : -1], refs[-1]
    outs, (x, dy, proj, hidden, received) = refs[: -6 - len(results)], refs[-6 - len(results) : -1 - len(results)]
    cap = x.shape[0] // parts
    share, wide = x.shape[1], hidden.shape[1]
    width = sources[0].shape[1] // 2
    first = pl.multiple_of(number_ref[0] * share, share)
    copies = Copies(sems)
    loads = []
    for part in range(parts):
        slot_ref, proj_ref, hidden_ref = sources[3 * part : 3 * part + 3]
        here = slice(part * cap, (part + 1) * cap)
        loads.append(copies.start(slot_ref.at[:, pl.ds(first, share)], x.at[here]))
        loads.append(copies.start(slot_ref.at[:, pl.ds(pl.multiple_of(first + width, share), share)], dy.at[here]))
        loads.append(copies.start(proj_ref, proj.at[here]))
        loads.append(copies.start(hidden_ref, hidden.at[here]))
    more_loads = []
    for index, number in enumerate(pieces):
        row = 0
        for ref in more[:number]:
            more_loads.append(copies.start(ref, received.at[index, row : row + ref.shape[0]]))
            row += ref.shape[0]
        more = more[number:]
    wait(loads)
    up = dot(x[...], proj[...], ROWS)
    down = dot(hidden[...], dy[...], ROWS) if end else dot(dy[...], hidden[...], ROWS)
    wait(more_loads)
    for index in range(len(pieces)):
        up = up + received[index, :, : 2 * wide].astype(F32)
        extra = received[index, :, 2 * wide : 3 * wide]
        if end:
            row = lax.broadcasted_iota(jnp.int32, (share, share), 0)
            unit = (row == lax.broadcasted_iota(jnp.int32, (share, share), 1)).astype(BF16)
            down = down + dot(extra, unit, ROWS)
        else:
            down = down + extra.astype(F32)
    if end:
        results[0][...] = up
        results[1][...] = down
        wait([copies.start(result, out) for result, out in zip(results, outs)])
        return
    results[0][:, : 2 * wide] = up.astype(BF16)
    results[0][:, 2 * wide : 3 * wide] = down.astype(BF16)
    stores, row = [], 0
    for out in outs:
        stores.append(copies.start(results[0].at[row : row + out.shape[0]], out))
        row += out.shape[0]
    wait(stores)


def combine_kernel(part, cap, rel_ref, tokens_ref, grad_ref, *refs):
    blocks, (mixed_out, grad_out, data, back, sems) = refs[:-5], refs[-5:]
    width = tokens_ref.shape[1]
    copies = Copies(sems)
    loads = [copies.start(ref, data.at[:, side * width : (side + 1) * width]) for side, ref in enumerate((tokens_ref, grad_ref))]
    loads += [copies.start(block, back.at[index * cap : (index + 1) * cap]) for index, block in enumerate(blocks)]
    placing = placing_of(rel_ref[...], len(blocks), part, cap)
    wait(loads)
    stores = []
    for side, out in enumerate((mixed_out, grad_out)):
        here = slice(side * width, (side + 1) * width)
        data[:, here] = (data[:, here].astype(F32) + dot(placing, back[:, here], ROWS)).astype(BF16)
        stores.append(copies.start(data.at[:, here], out))
    wait(stores)


def after(value, *earlier):
    if not earlier:
        return value
    return lax.optimization_barrier((value, *earlier))[0]


class Lane:
    def __init__(self, window):
        self.window = window
        self.done = []

    def send(self, value, axis, pairs, *earlier):
        if len(self.done) >= self.window:
            earlier = (self.done[-self.window], *earlier)
        self.done.append(lax.ppermute(after(value, *earlier), axis, pairs))
        return self.done[-1]


def exchange(blocks, far, held={}):
    experts = len(blocks)
    half = experts // 2
    moved = {0: blocks[0]}
    for mask in range(half - 1, -1, -1):
        pairs = [(i, i ^ (mask + half)) for i in range(experts)]
        moved[mask + half] = far.send(blocks[mask + half], "exp", pairs, *held.get(mask, ()))
        if mask:
            pairs = [(i, i ^ mask) for i in range(experts)]
            moved[mask] = lax.ppermute(after(blocks[mask], far.done[-1]), "exp", pairs)
    return [moved[mask] for mask in range(experts)]


def body(tokens, expert_ids, gate_up_weight, down_weight, grad_out):
    rows, width = tokens.shape
    experts = lax.axis_size("exp")
    groups = lax.axis_size("grp")
    capacity = 2 * rows // experts
    parts = 2 if capacity % 32 == 0 else 1
    cap = capacity // parts
    slots = experts * cap
    weight_one = gate_up_weight[0]
    weight_two = down_weight[0]
    wide = weight_two.shape[0]
    share = width // groups
    pair = like((cap, 2 * width))
    sems = pltpu.SemaphoreType.DMA
    far = Lane(3)
    rel = expert_ids.reshape(1, rows) ^ lax.axis_index("exp").astype(jnp.int32)
    group = lax.axis_index("grp").astype(jnp.int32)

    def place(part):
        return call(
            lambda *refs: place_kernel(part, cap, *refs),
            "place",
            20,
            [pair] * experts,
            [pltpu.VMEM((rows, 2 * width), BF16), pltpu.VMEM((slots, 2 * width), BF16), sems((2 + 2 * experts,))],
            [tokens, grad_out],
            [rel],
        )

    def expert(blocks):
        shapes = [(slots, 2 * width), (slots, 2 * wide), (slots, wide)]
        back = [pltpu.VMEM(shape, BF16) for shape in shapes]
        scratch = [back[0], pltpu.VMEM(weight_one.shape, BF16), pltpu.VMEM(weight_two.shape, BF16)]
        outs = call(
            expert_kernel,
            "expert",
            44,
            [pair] * experts + [like(shape) for shape in shapes],
            scratch + back + [sems((5 + 2 * experts,))],
            [*blocks, weight_one, weight_two],
        )
        return outs[:experts], outs[experts:]

    def weight_part(number, kept, received, end, heads):
        shape = (share, pl.cdiv(3 * wide, 128) * 128)
        finals = [like((share, 2 * wide), F32), like((wide, share), F32)]
        rows_of = [heads, share - heads] if heads else [share]
        outs = finals if end else [like((count, shape[1])) for count in rows_of]
        total = parts * slots
        scratch = [pltpu.VMEM((total, width), BF16) for width in (share, share, 2 * wide, wide)]
        scratch.append(pltpu.VMEM((max(1, len(received)), *shape), BF16))
        scratch += [pltpu.VMEM(out.shape, out.dtype) for out in (finals if end else [like(shape)])]
        sources = [array for arrays in kept + received for array in arrays]
        scratch.append(sems((len(sources) + parts + len(outs),)))
        pieces = [len(arrays) for arrays in received]
        return call(
            lambda *refs: weight_kernel(end, parts, pieces, *refs),
            "weight_part",
            32,
            outs,
            scratch,
            sources,
            scalars=[number[None]],
        )

    def combine(part, first, second, blocks):
        return call(
            lambda *refs: combine_kernel(part, cap, *refs),
            "combine",
            20,
            [like((rows, width))] * 2,
            [pltpu.VMEM((rows, 2 * width), BF16), pltpu.VMEM((slots, 2 * width), BF16), sems((4 + experts,))],
            [first, second, *blocks],
            [rel],
        )

    sent = [place(part) for part in range(parts)]
    results = []
    for part in range(parts):
        held = {0: (results[-1][0][0],)} if results else {}
        results.append(expert(exchange(sent[part], far, held)))
    kept = [result[1] for result in results]

    count = len(far.done)
    back = [exchange(results[0][0], far)]
    far_out = far.done[count:]
    near_out = back[0][experts // 2 - 1 : 0 : -1]
    gates = iter([[], far_out[2:3] + near_out[:1], far_out[3:] + near_out[1:2]])
    lanes = {}

    def weight_sum(q, bit):
        received = []
        low = bit // 2
        while low:
            pairs = [(i, i ^ low) for i in range(groups)]
            lane = lanes.setdefault(low, Lane(1))
            head, *rest = weight_sum(q | low, low)
            head = lane.send(head, "grp", pairs)
            received.append([head] + [lane.send(piece, "grp", pairs, *far_out[:2]) for piece in rest])
            low //= 2
        first = after(kept[0][0], *([] if bit == groups else next(gates, [])))
        heads = 16 if q == groups - 1 else 0
        return weight_part(group ^ q, [[first, *kept[0][1:]], *kept[1:]], received, bit == groups, heads)

    grad_gate_up, grad_down = weight_sum(0, groups)
    mixed, grad = tokens, grad_out
    for part in range(1, parts):
        mixed, grad = combine(part - 1, mixed, grad, back[-1])
        back.append(exchange(results[part][0], far, {0: (mixed,)}))
    back[-1][0] = after(back[-1][0], grad_gate_up)
    mixed, grad = combine(parts - 1, mixed, grad, back[-1])
    return (mixed, grad, grad_gate_up[None], grad_down[None])


def solution(mesh):
    in_specs = (
        P(("grp", "exp"), None),
        P(("grp", "exp"), None),
        P("exp", None, None),
        P("exp", None, None),
        P(("grp", "exp"), None),
    )
    out_specs = (
        P(("grp", "exp"), None),
        P(("grp", "exp"), None),
        P("exp", "grp", None),
        P("exp", None, "grp"),
    )
    return jax.shard_map(body, mesh=mesh, in_specs=in_specs, out_specs=out_specs, check_vma=False)
```

```python
import jax
import jax.numpy as jnp
from jax import lax
from jax.experimental import pallas as pl
from jax.experimental.pallas import tpu as pltpu
from jax.sharding import PartitionSpec as P

SMALL = pl.CostEstimate(flops=1024, bytes_accessed=1024, transcendentals=0)
BF16 = jnp.bfloat16
F32 = jnp.float32
ROWS = ((0,), (0,))
COLS = ((1,), (1,))
PLAIN = ((1,), (0,))


def dot(left, right, dims):
    return lax.dot_general(left, right, (dims, ((), ())), preferred_element_type=F32)


def like(shape, dtype=BF16):
    return jax.ShapeDtypeStruct(shape, dtype)


def call(kernel, name, mebibytes, outs, scratch, arrays, small=(), scalars=()):
    hbm = pl.BlockSpec(memory_space=pltpu.HBM)
    return pl.pallas_call(
        kernel,
        in_specs=[pl.BlockSpec(memory_space=pltpu.SMEM)] * len(scalars)
        + [pl.BlockSpec(memory_space=pltpu.VMEM)] * len(small)
        + [hbm] * len(arrays),
        out_specs=[hbm] * len(outs),
        out_shape=outs,
        scratch_shapes=scratch,
        compiler_params=pltpu.CompilerParams(vmem_limit_bytes=mebibytes * 1024 * 1024),
        cost_estimate=SMALL,
        name=name,
    )(*scalars, *small, *arrays)


class Copies:
    def __init__(self, sems):
        self.sems = sems
        self.used = 0

    def start(self, source, target):
        copy = pltpu.make_async_copy(source, target, self.sems.at[self.used])
        self.used += 1
        copy.start()
        return copy


def wait(copies):
    for copy in copies:
        copy.wait()


def place_kernel(part, cap, rel_ref, tokens_ref, grad_ref, *refs):
    blocks, (data, moved, sems) = refs[:-3], refs[-3:]
    experts = len(blocks)
    rows, width = tokens_ref.shape
    copies = Copies(sems)
    loads = [copies.start(ref, data.at[:, side * width : (side + 1) * width]) for side, ref in enumerate((tokens_ref, grad_ref))]
    placing = placing_of(rel_ref[...], experts, part, cap)
    stores = []
    for side in range(2):
        here = slice(side * width, (side + 1) * width)
        loads[side].wait()
        moved[:, here] = dot(placing, data[:, here], PLAIN).astype(BF16)
        for index, block in enumerate(blocks):
            stores.append(copies.start(moved.at[index * cap : (index + 1) * cap, here], block.at[:, here]))
    wait(stores)


def placing_of(rel, experts, part, cap):
    rows = rel.shape[1]
    onehot = lax.broadcasted_iota(jnp.int32, (max(experts, 16), rows), 0) == rel
    before = lax.broadcasted_iota(jnp.int32, (rows, rows), 0) < lax.broadcasted_iota(jnp.int32, (rows, rows), 1)
    ranks = dot(onehot.astype(BF16), before.astype(BF16), PLAIN)
    rank = jnp.sum(jnp.where(onehot, ranks, 0.0), axis=0, keepdims=True).astype(jnp.int32) - part * cap
    target = jnp.where((rank >= 0) & (rank < cap), rel * cap + rank, -1)
    return (lax.broadcasted_iota(jnp.int32, (experts * cap, rows), 0) == target).astype(BF16)


def expert_kernel(*refs):
    count = (len(refs) - 12) // 2
    blocks, (one_ref, two_ref), outs = refs[:count], refs[count : count + 2], refs[count + 2 : 2 * count + 2]
    slot_out, proj_out, hidden_out, slot, one, two, back, proj, hidden, sems = refs[2 * count + 2 :]
    cap = blocks[0].shape[0]
    wide, width = two.shape
    copies = Copies(sems)
    loads = [copies.start(block, slot.at[index * cap : (index + 1) * cap]) for index, block in enumerate(blocks)]
    one_load = copies.start(one_ref, one)
    two_load = copies.start(two_ref, two)
    wait(loads)
    stores = [copies.start(slot, slot_out)]
    one_load.wait()
    both = dot(slot[:, :width], one[...], PLAIN)
    gate, upper = both[:, :wide], both[:, wide:]
    sigma = 1.0 / (1.0 + jnp.exp(-gate))
    silu = gate * sigma
    hidden[...] = (silu * upper).astype(BF16)
    stores.append(copies.start(hidden, hidden_out))
    two_load.wait()
    grad_hidden = dot(slot[:, width:], two[...], COLS)
    proj[...] = jnp.concatenate(
        [grad_hidden * upper * sigma * (1.0 + gate * (1.0 - sigma)), grad_hidden * silu], axis=1
    ).astype(BF16)
    stores.append(copies.start(proj, proj_out))
    back[:, :width] = dot(hidden[...], two[...], PLAIN).astype(BF16)
    back[:, width:] = dot(proj[...], one[...], COLS).astype(BF16)
    stores += [copies.start(back.at[index * cap : (index + 1) * cap], out) for index, out in enumerate(outs)]
    wait(stores)


def weight_kernel(end, parts, pieces, number_ref, *refs):
    sources, refs = refs[: 3 * parts], refs[3 * parts :]
    more, refs = refs[: sum(pieces)], refs[sum(pieces) :]
    results, sems = refs[-3 if end else -2 : -1], refs[-1]
    outs, (x, dy, proj, hidden, received) = refs[: -6 - len(results)], refs[-6 - len(results) : -1 - len(results)]
    cap = x.shape[0] // parts
    share, wide = x.shape[1], hidden.shape[1]
    width = sources[0].shape[1] // 2
    first = pl.multiple_of(number_ref[0] * share, share)
    copies = Copies(sems)
    loads = []
    for part in range(parts):
        slot_ref, proj_ref, hidden_ref = sources[3 * part : 3 * part + 3]
        here = slice(part * cap, (part + 1) * cap)
        loads.append(copies.start(slot_ref.at[:, pl.ds(first, share)], x.at[here]))
        loads.append(copies.start(slot_ref.at[:, pl.ds(pl.multiple_of(first + width, share), share)], dy.at[here]))
        loads.append(copies.start(proj_ref, proj.at[here]))
        loads.append(copies.start(hidden_ref, hidden.at[here]))
    more_loads = []
    for index, number in enumerate(pieces):
        row = 0
        for ref in more[:number]:
            more_loads.append(copies.start(ref, received.at[index, row : row + ref.shape[0]]))
            row += ref.shape[0]
        more = more[number:]
    wait(loads)
    up = dot(x[...], proj[...], ROWS)
    down = dot(hidden[...], dy[...], ROWS) if end else dot(dy[...], hidden[...], ROWS)
    wait(more_loads)
    for index in range(len(pieces)):
        up = up + received[index, :, : 2 * wide].astype(F32)
        extra = received[index, :, 2 * wide : 3 * wide]
        if end:
            row = lax.broadcasted_iota(jnp.int32, (share, share), 0)
            unit = (row == lax.broadcasted_iota(jnp.int32, (share, share), 1)).astype(BF16)
            down = down + dot(extra, unit, ROWS)
        else:
            down = down + extra.astype(F32)
    if end:
        results[0][...] = up
        results[1][...] = down
        wait([copies.start(result, out) for result, out in zip(results, outs)])
        return
    results[0][:, : 2 * wide] = up.astype(BF16)
    results[0][:, 2 * wide : 3 * wide] = down.astype(BF16)
    stores, row = [], 0
    for out in outs:
        stores.append(copies.start(results[0].at[row : row + out.shape[0]], out))
        row += out.shape[0]
    wait(stores)


def combine_kernel(part, cap, rel_ref, tokens_ref, grad_ref, *refs):
    blocks, (mixed_out, grad_out, data, back, sems) = refs[:-5], refs[-5:]
    width = tokens_ref.shape[1]
    copies = Copies(sems)
    loads = [copies.start(ref, data.at[:, side * width : (side + 1) * width]) for side, ref in enumerate((tokens_ref, grad_ref))]
    loads += [copies.start(block, back.at[index * cap : (index + 1) * cap]) for index, block in enumerate(blocks)]
    placing = placing_of(rel_ref[...], len(blocks), part, cap)
    wait(loads)
    stores = []
    for side, out in enumerate((mixed_out, grad_out)):
        here = slice(side * width, (side + 1) * width)
        data[:, here] = (data[:, here].astype(F32) + dot(placing, back[:, here], ROWS)).astype(BF16)
        stores.append(copies.start(data.at[:, here], out))
    wait(stores)


def after(value, *earlier):
    if not earlier:
        return value
    return lax.optimization_barrier((value, *earlier))[0]


class Lane:
    def __init__(self, window):
        self.window = window
        self.done = []

    def send(self, value, axis, pairs, *earlier):
        if len(self.done) >= self.window:
            earlier = (self.done[-self.window], *earlier)
        self.done.append(lax.ppermute(after(value, *earlier), axis, pairs))
        return self.done[-1]


def exchange(blocks, far, held={}):
    experts = len(blocks)
    half = experts // 2
    moved = {0: blocks[0]}
    earlier = far.done[-1:]
    for mask in range(half - 1, -1, -1):
        pairs = [(i, i ^ (mask + half)) for i in range(experts)]
        moved[mask + half] = far.send(blocks[mask + half], "exp", pairs, *held.get(mask, ()))
    for mask in range(half - 1, 0, -1):
        pairs = [(i, i ^ mask) for i in range(experts)]
        moved[mask] = lax.ppermute(after(blocks[mask], *earlier), "exp", pairs)
    return [moved[mask] for mask in range(experts)]


def body(tokens, expert_ids, gate_up_weight, down_weight, grad_out):
    rows, width = tokens.shape
    experts = lax.axis_size("exp")
    groups = lax.axis_size("grp")
    capacity = 2 * rows // experts
    parts = 2 if capacity % 32 == 0 else 1
    cap = capacity // parts
    slots = experts * cap
    weight_one = gate_up_weight[0]
    weight_two = down_weight[0]
    wide = weight_two.shape[0]
    share = width // groups
    pair = like((cap, 2 * width))
    sems = pltpu.SemaphoreType.DMA
    far = Lane(2)
    rel = expert_ids.reshape(1, rows) ^ lax.axis_index("exp").astype(jnp.int32)
    group = lax.axis_index("grp").astype(jnp.int32)

    def place(part):
        return call(
            lambda *refs: place_kernel(part, cap, *refs),
            "place",
            slots * 5 // 128,
            [pair] * experts,
            [pltpu.VMEM((rows, 2 * width), BF16), pltpu.VMEM((slots, 2 * width), BF16), sems((2 + 2 * experts,))],
            [tokens, grad_out],
            [rel],
        )

    def expert(blocks):
        shapes = [(slots, 2 * width), (slots, 2 * wide), (slots, wide)]
        back = [pltpu.VMEM(shape, BF16) for shape in shapes]
        scratch = [back[0], pltpu.VMEM(weight_one.shape, BF16), pltpu.VMEM(weight_two.shape, BF16)]
        outs = call(
            expert_kernel,
            "expert",
            2 + slots * 5 // 64,
            [pair] * experts + [like(shape) for shape in shapes],
            scratch + back + [sems((5 + 2 * experts,))],
            [*blocks, weight_one, weight_two],
        )
        return outs[:experts], outs[experts:]

    def weight_part(number, kept, received, end, heads):
        shape = (share, pl.cdiv(3 * wide, 128) * 128)
        finals = [like((share, 2 * wide), F32), like((wide, share), F32)]
        rows_of = [heads, share - heads] if heads else [share]
        outs = finals if end else [like((count, shape[1])) for count in rows_of]
        total = parts * slots
        scratch = [pltpu.VMEM((total, width), BF16) for width in (share, share, 2 * wide, wide)]
        scratch.append(pltpu.VMEM((max(1, len(received)), *shape), BF16))
        scratch += [pltpu.VMEM(out.shape, out.dtype) for out in (finals if end else [like(shape)])]
        sources = [array for arrays in kept + received for array in arrays]
        scratch.append(sems((len(sources) + parts + len(outs),)))
        pieces = [len(arrays) for arrays in received]
        return call(
            lambda *refs: weight_kernel(end, parts, pieces, *refs),
            "weight_part",
            18,
            outs,
            scratch,
            sources,
            scalars=[number[None]],
        )

    def combine(part, first, second, blocks):
        return call(
            lambda *refs: combine_kernel(part, cap, *refs),
            "combine",
            slots * 5 // 128,
            [like((rows, width))] * 2,
            [pltpu.VMEM((rows, 2 * width), BF16), pltpu.VMEM((slots, 2 * width), BF16), sems((4 + experts,))],
            [first, second, *blocks],
            [rel],
        )

    sent = [place(part) for part in range(parts)]
    results = []
    for part in range(parts):
        held = {0: (results[-1][0][0],)} if results else {}
        results.append(expert(exchange(sent[part], far, held)))
    kept = [result[1] for result in results]

    count = len(far.done)
    back = [exchange(results[0][0], far)]
    far_out = far.done[count:]
    near_out = back[0][experts // 2 - 1 : 0 : -1]

    received = {q: [] for q in range(groups)}
    sums = kept[0][0]
    for q in sorted(range(1, groups), key=lambda q: (q & -q, -q)):
        low = q & -q
        first_of_all = q == groups - 1
        if low == 2 and received[q ^ low]:
            sums = after(sums, *far_out[2:3], *near_out[:1])
        sent = weight_part(group ^ q, [[sums, *kept[0][1:]], *kept[1:]], received[q], False, 16 if first_of_all else 0)
        sums = after(sums, sent[0])
        lane = Lane(1)
        pairs = [(i, i ^ low) for i in range(groups)]
        received[q ^ low].append([lane.send(piece, "grp", pairs, *(far_out[:2] if index else ())) for index, piece in enumerate(sent)])

    mixed, grad = tokens, grad_out
    for part in range(1, parts):
        mixed, grad = combine(part - 1, mixed, grad, back[-1])
        back.append(exchange(results[part][0], far, {0: (mixed, *received[0][-1])}))
    grad_gate_up, grad_down = weight_part(group, [[sums, *kept[0][1:]], *kept[1:]], received[0], True, 0)
    back[-1][0] = after(back[-1][0], grad_gate_up)
    mixed, grad = combine(parts - 1, mixed, grad, back[-1])
    return (mixed, grad, grad_gate_up[None], grad_down[None])


def solution(mesh):
    in_specs = (
        P(("grp", "exp"), None),
        P(("grp", "exp"), None),
        P("exp", None, None),
        P("exp", None, None),
        P(("grp", "exp"), None),
    )
    out_specs = (
        P(("grp", "exp"), None),
        P(("grp", "exp"), None),
        P("exp", "grp", None),
        P("exp", None, "grp"),
    )
    return jax.shard_map(body, mesh=mesh, in_specs=in_specs, out_specs=out_specs, check_vma=False)
```

```python
import jax
import jax.numpy as jnp
from jax import lax
from jax.experimental import pallas as pl
from jax.experimental.pallas import tpu as pltpu
from jax.sharding import PartitionSpec as P

VMEM_BYTES = 64 * 1024 * 1024
SMALL = pl.CostEstimate(flops=1024, bytes_accessed=1024, transcendentals=0)
BF16 = jnp.bfloat16
F32 = jnp.float32
ROWS = ((0,), (0,))
COLS = ((1,), (1,))
PLAIN = ((1,), (0,))


def dot(left, right, dims):
    return lax.dot_general(left, right, (dims, ((), ())), preferred_element_type=F32)


def like(shape, dtype=BF16):
    return jax.ShapeDtypeStruct(shape, dtype)


def call(kernel, name, outs, scratch, arrays, small=(), scalars=()):
    hbm = pl.BlockSpec(memory_space=pltpu.HBM)
    return pl.pallas_call(
        kernel,
        in_specs=[pl.BlockSpec(memory_space=pltpu.SMEM)] * len(scalars)
        + [pl.BlockSpec(memory_space=pltpu.VMEM)] * len(small)
        + [hbm] * len(arrays),
        out_specs=[hbm] * len(outs),
        out_shape=outs,
        scratch_shapes=scratch,
        compiler_params=pltpu.CompilerParams(vmem_limit_bytes=VMEM_BYTES),
        cost_estimate=SMALL,
        name=name,
    )(*scalars, *small, *arrays)


class Copies:
    def __init__(self, sems):
        self.sems = sems
        self.used = 0

    def start(self, source, target):
        copy = pltpu.make_async_copy(source, target, self.sems.at[self.used])
        self.used += 1
        copy.start()
        return copy


def wait(copies):
    for copy in copies:
        copy.wait()


def place_kernel(part, cap, rel_ref, tokens_ref, grad_ref, *refs):
    blocks, (data, moved, sems) = refs[:-3], refs[-3:]
    experts = len(blocks)
    rows, width = tokens_ref.shape
    copies = Copies(sems)
    loads = [copies.start(ref, data.at[:, side * width : (side + 1) * width]) for side, ref in enumerate((tokens_ref, grad_ref))]
    placing = placing_of(rel_ref[...], experts, part, cap)
    stores = []
    for side in range(2):
        here = slice(side * width, (side + 1) * width)
        loads[side].wait()
        moved[:, here] = dot(placing, data[:, here], PLAIN).astype(BF16)
        for index, block in enumerate(blocks):
            stores.append(copies.start(moved.at[index * cap : (index + 1) * cap, here], block.at[:, here]))
    wait(stores)


def placing_of(rel, experts, part, cap):
    rows = rel.shape[1]
    onehot = lax.broadcasted_iota(jnp.int32, (max(experts, 16), rows), 0) == rel
    before = lax.broadcasted_iota(jnp.int32, (rows, rows), 0) < lax.broadcasted_iota(jnp.int32, (rows, rows), 1)
    ranks = dot(onehot.astype(BF16), before.astype(BF16), PLAIN)
    rank = jnp.sum(jnp.where(onehot, ranks, 0.0), axis=0, keepdims=True).astype(jnp.int32) - part * cap
    target = jnp.where((rank >= 0) & (rank < cap), rel * cap + rank, -1)
    return (lax.broadcasted_iota(jnp.int32, (experts * cap, rows), 0) == target).astype(BF16)


def expert_kernel(*refs):
    count = (len(refs) - 12) // 2
    blocks, (one_ref, two_ref), outs = refs[:count], refs[count : count + 2], refs[count + 2 : 2 * count + 2]
    slot_out, proj_out, hidden_out, slot, one, two, back, proj, hidden, sems = refs[2 * count + 2 :]
    cap = blocks[0].shape[0]
    wide, width = two.shape
    copies = Copies(sems)
    loads = [copies.start(block, slot.at[index * cap : (index + 1) * cap]) for index, block in enumerate(blocks)]
    one_load = copies.start(one_ref, one)
    two_load = copies.start(two_ref, two)
    wait(loads)
    stores = [copies.start(slot, slot_out)]
    one_load.wait()
    both = dot(slot[:, :width], one[...], PLAIN)
    gate, upper = both[:, :wide], both[:, wide:]
    sigma = 1.0 / (1.0 + jnp.exp(-gate))
    silu = gate * sigma
    hidden[...] = (silu * upper).astype(BF16)
    stores.append(copies.start(hidden, hidden_out))
    two_load.wait()
    grad_hidden = dot(slot[:, width:], two[...], COLS)
    proj[...] = jnp.concatenate(
        [grad_hidden * upper * sigma * (1.0 + gate * (1.0 - sigma)), grad_hidden * silu], axis=1
    ).astype(BF16)
    stores.append(copies.start(proj, proj_out))
    back[:, :width] = dot(hidden[...], two[...], PLAIN).astype(BF16)
    back[:, width:] = dot(proj[...], one[...], COLS).astype(BF16)
    stores += [copies.start(back.at[index * cap : (index + 1) * cap], out) for index, out in enumerate(outs)]
    wait(stores)


def weight_kernel(end, parts, pieces, number_ref, *refs):
    sources, refs = refs[: 3 * parts], refs[3 * parts :]
    more, refs = refs[: sum(pieces)], refs[sum(pieces) :]
    results, sems = refs[-3 if end else -2 : -1], refs[-1]
    outs, (x, dy, proj, hidden, received) = refs[: -6 - len(results)], refs[-6 - len(results) : -1 - len(results)]
    cap = x.shape[0] // parts
    share, wide = x.shape[1], hidden.shape[1]
    width = sources[0].shape[1] // 2
    first = pl.multiple_of(number_ref[0] * share, share)
    copies = Copies(sems)
    loads = []
    for part in range(parts):
        slot_ref, proj_ref, hidden_ref = sources[3 * part : 3 * part + 3]
        here = slice(part * cap, (part + 1) * cap)
        loads.append(copies.start(slot_ref.at[:, pl.ds(first, share)], x.at[here]))
        loads.append(copies.start(slot_ref.at[:, pl.ds(pl.multiple_of(first + width, share), share)], dy.at[here]))
        loads.append(copies.start(proj_ref, proj.at[here]))
        loads.append(copies.start(hidden_ref, hidden.at[here]))
    more_loads = []
    for index, number in enumerate(pieces):
        row = 0
        for ref in more[:number]:
            more_loads.append(copies.start(ref, received.at[index, row : row + ref.shape[0]]))
            row += ref.shape[0]
        more = more[number:]
    wait(loads)
    up = dot(x[...], proj[...], ROWS)
    down = dot(hidden[...], dy[...], ROWS) if end else dot(dy[...], hidden[...], ROWS)
    wait(more_loads)
    for index in range(len(pieces)):
        up = up + received[index, :, : 2 * wide].astype(F32)
        extra = received[index, :, 2 * wide : 3 * wide]
        if end:
            row = lax.broadcasted_iota(jnp.int32, (share, share), 0)
            unit = (row == lax.broadcasted_iota(jnp.int32, (share, share), 1)).astype(BF16)
            down = down + dot(extra, unit, ROWS)
        else:
            down = down + extra.astype(F32)
    if end:
        results[0][...] = up
        results[1][...] = down
        wait([copies.start(result, out) for result, out in zip(results, outs)])
        return
    results[0][:, : 2 * wide] = up.astype(BF16)
    results[0][:, 2 * wide : 3 * wide] = down.astype(BF16)
    stores, row = [], 0
    for out in outs:
        stores.append(copies.start(results[0].at[row : row + out.shape[0]], out))
        row += out.shape[0]
    wait(stores)


def combine_kernel(part, cap, rel_ref, tokens_ref, grad_ref, *refs):
    blocks, (mixed_out, grad_out, data, back, sems) = refs[:-5], refs[-5:]
    width = tokens_ref.shape[1]
    copies = Copies(sems)
    loads = [copies.start(ref, data.at[:, side * width : (side + 1) * width]) for side, ref in enumerate((tokens_ref, grad_ref))]
    loads += [copies.start(block, back.at[index * cap : (index + 1) * cap]) for index, block in enumerate(blocks)]
    placing = placing_of(rel_ref[...], len(blocks), part, cap)
    wait(loads)
    stores = []
    for side, out in enumerate((mixed_out, grad_out)):
        here = slice(side * width, (side + 1) * width)
        data[:, here] = (data[:, here].astype(F32) + dot(placing, back[:, here], ROWS)).astype(BF16)
        stores.append(copies.start(data.at[:, here], out))
    wait(stores)


def after(value, *earlier):
    if not earlier:
        return value
    return lax.optimization_barrier((value, *earlier))[0]


class Lane:
    def __init__(self, window):
        self.window = window
        self.done = []

    def send(self, value, axis, pairs, *earlier):
        if len(self.done) >= self.window:
            earlier = (self.done[-self.window], *earlier)
        self.done.append(lax.ppermute(after(value, *earlier), axis, pairs))
        return self.done[-1]


def exchange(blocks, far, held={}):
    experts = len(blocks)
    half = experts // 2
    moved = {0: blocks[0]}
    earlier = far.done[-1:]
    for mask in range(half - 1, -1, -1):
        pairs = [(i, i ^ (mask + half)) for i in range(experts)]
        moved[mask + half] = far.send(blocks[mask + half], "exp", pairs, *held.get(mask, ()))
    for mask in range(half - 1, 0, -1):
        pairs = [(i, i ^ mask) for i in range(experts)]
        moved[mask] = lax.ppermute(after(blocks[mask], *earlier), "exp", pairs)
    return [moved[mask] for mask in range(experts)]


def body(tokens, expert_ids, gate_up_weight, down_weight, grad_out):
    rows, width = tokens.shape
    experts = lax.axis_size("exp")
    groups = lax.axis_size("grp")
    capacity = 2 * rows // experts
    parts = 2 if capacity % 32 == 0 else 1
    cap = capacity // parts
    slots = experts * cap
    weight_one = gate_up_weight[0]
    weight_two = down_weight[0]
    wide = weight_two.shape[0]
    share = width // groups
    pair = like((cap, 2 * width))
    sems = pltpu.SemaphoreType.DMA
    far = Lane(2)
    rel = expert_ids.reshape(1, rows) ^ lax.axis_index("exp").astype(jnp.int32)
    group = lax.axis_index("grp").astype(jnp.int32)

    def place(part):
        return call(
            lambda *refs: place_kernel(part, cap, *refs),
            "place",
            [pair] * experts,
            [pltpu.VMEM((rows, 2 * width), BF16), pltpu.VMEM((slots, 2 * width), BF16), sems((2 + 2 * experts,))],
            [tokens, grad_out],
            [rel],
        )

    def expert(blocks):
        shapes = [(slots, 2 * width), (slots, 2 * wide), (slots, wide)]
        back = [pltpu.VMEM(shape, BF16) for shape in shapes]
        scratch = [back[0], pltpu.VMEM(weight_one.shape, BF16), pltpu.VMEM(weight_two.shape, BF16)]
        outs = call(
            expert_kernel,
            "expert",
            [pair] * experts + [like(shape) for shape in shapes],
            scratch + back + [sems((5 + 2 * experts,))],
            [*blocks, weight_one, weight_two],
        )
        return outs[:experts], outs[experts:]

    def weight_part(number, kept, received, end, heads):
        shape = (share, pl.cdiv(3 * wide, 128) * 128)
        finals = [like((share, 2 * wide), F32), like((wide, share), F32)]
        rows_of = [heads, share - heads] if heads else [share]
        outs = finals if end else [like((count, shape[1])) for count in rows_of]
        total = parts * slots
        scratch = [pltpu.VMEM((total, width), BF16) for width in (share, share, 2 * wide, wide)]
        scratch.append(pltpu.VMEM((max(1, len(received)), *shape), BF16))
        scratch += [pltpu.VMEM(out.shape, out.dtype) for out in (finals if end else [like(shape)])]
        sources = [array for arrays in kept + received for array in arrays]
        scratch.append(sems((len(sources) + parts + len(outs),)))
        pieces = [len(arrays) for arrays in received]
        return call(
            lambda *refs: weight_kernel(end, parts, pieces, *refs),
            "weight_part",
            outs,
            scratch,
            sources,
            scalars=[number[None]],
        )

    def combine(part, first, second, blocks):
        return call(
            lambda *refs: combine_kernel(part, cap, *refs),
            "combine",
            [like((rows, width))] * 2,
            [pltpu.VMEM((rows, 2 * width), BF16), pltpu.VMEM((slots, 2 * width), BF16), sems((4 + experts,))],
            [first, second, *blocks],
            [rel],
        )

    sent = [place(part) for part in range(parts)]
    results = []
    for part in range(parts):
        held = {0: (results[-1][0][0],)} if results else {}
        results.append(expert(exchange(sent[part], far, held)))
    kept = [result[1] for result in results]

    count = len(far.done)
    back = [exchange(results[0][0], far)]
    far_out = far.done[count:]
    near_out = back[0][experts // 2 - 1 : 0 : -1]

    received = {q: [] for q in range(groups)}
    sums = kept[0][0]
    for q in sorted(range(1, groups), key=lambda q: (q & -q, -q)):
        low = q & -q
        first_of_all = q == groups - 1
        if low == 2 and received[q ^ low]:
            sums = after(sums, *far_out[2:3], *near_out[:1])
        sent = weight_part(group ^ q, [[sums, *kept[0][1:]], *kept[1:]], received[q], False, 16 if first_of_all else 0)
        sums = after(sums, sent[0])
        lane = Lane(1)
        pairs = [(i, i ^ low) for i in range(groups)]
        received[q ^ low].append([lane.send(piece, "grp", pairs, *(far_out[:2] if index else ())) for index, piece in enumerate(sent)])

    mixed, grad = tokens, grad_out
    for part in range(1, parts):
        mixed, grad = combine(part - 1, mixed, grad, back[-1])
        back.append(exchange(results[part][0], far, {0: (mixed, *received[0][-1])}))
    grad_gate_up, grad_down = weight_part(group, [[sums, *kept[0][1:]], *kept[1:]], received[0], True, 0)
    back[-1][0] = after(back[-1][0], grad_gate_up)
    mixed, grad = combine(parts - 1, mixed, grad, back[-1])
    return (mixed, grad, grad_gate_up[None], grad_down[None])


def solution(mesh):
    in_specs = (
        P(("grp", "exp"), None),
        P(("grp", "exp"), None),
        P("exp", None, None),
        P("exp", None, None),
        P(("grp", "exp"), None),
    )
    out_specs = (
        P(("grp", "exp"), None),
        P(("grp", "exp"), None),
        P("exp", "grp", None),
        P("exp", None, "grp"),
    )
    return jax.shard_map(body, mesh=mesh, in_specs=in_specs, out_specs=out_specs, check_vma=False)
```

```python
import jax
import jax.numpy as jnp
import numpy as np
from jax import lax
from jax.experimental import pallas as pl
from jax.experimental.pallas import tpu as pltpu
from jax.sharding import PartitionSpec as P

VMEM_BYTES = 64 * 1024 * 1024
SMALL = pl.CostEstimate(flops=1024, bytes_accessed=1024, transcendentals=0)
BF16 = jnp.bfloat16
F32 = jnp.float32
ROWS = ((0,), (0,))
COLS = ((1,), (1,))
PLAIN = ((1,), (0,))


def dot(left, right, dims):
    return lax.dot_general(left, right, (dims, ((), ())), preferred_element_type=F32)


def like(shape, dtype=BF16):
    return jax.ShapeDtypeStruct(shape, dtype)


def call(kernel, name, outs, scratch, arrays, small=(), scalars=()):
    hbm = pl.BlockSpec(memory_space=pltpu.HBM)
    return pl.pallas_call(
        kernel,
        in_specs=[pl.BlockSpec(memory_space=pltpu.SMEM)] * len(scalars)
        + [pl.BlockSpec(memory_space=pltpu.VMEM)] * len(small)
        + [hbm] * len(arrays),
        out_specs=[hbm] * len(outs),
        out_shape=outs,
        scratch_shapes=scratch,
        compiler_params=pltpu.CompilerParams(vmem_limit_bytes=VMEM_BYTES),
        cost_estimate=SMALL,
        name=name,
    )(*scalars, *small, *arrays)


class Copies:
    def __init__(self, sems):
        self.sems = sems
        self.used = 0

    def start(self, source, target):
        copy = pltpu.make_async_copy(source, target, self.sems.at[self.used])
        self.used += 1
        copy.start()
        return copy


def wait(copies):
    for copy in copies:
        copy.wait()


def place_kernel(part, cap, me_ref, table_ref, ids_ref, tokens_ref, grad_ref, *refs):
    blocks, (data, moved, sems) = refs[:-3], refs[-3:]
    width = tokens_ref.shape[1]
    copies = Copies(sems)
    loads = [
        copies.start(ref, data.at[:, side * width : (side + 1) * width]) for side, ref in enumerate((tokens_ref, grad_ref))
    ]
    placing = placing_of(me_ref, table_ref, ids_ref, len(blocks), part, cap)
    stores = []
    for side in range(2):
        here = slice(side * width, (side + 1) * width)
        loads[side].wait()
        moved[:, here] = dot(placing, data[:, here], PLAIN).astype(BF16)
        for index, block in enumerate(blocks):
            stores.append(copies.start(moved.at[index * cap : (index + 1) * cap, here], block.at[:, here]))
    wait(stores)


def placing_of(me_ref, table_ref, ids_ref, experts, part, cap):
    ids = ids_ref[...]
    rows = ids.shape[1]
    me = me_ref[0]
    rel = jnp.zeros((1, rows), jnp.int32)
    for expert in range(experts):
        rel = jnp.where(ids == expert, table_ref[me, expert], rel)
    onehot = lax.broadcasted_iota(jnp.int32, (max(experts, 16), rows), 0) == rel
    before = lax.broadcasted_iota(jnp.int32, (rows, rows), 0) < lax.broadcasted_iota(jnp.int32, (rows, rows), 1)
    ranks = dot(onehot.astype(BF16), before.astype(BF16), PLAIN)
    rank = jnp.sum(jnp.where(onehot, ranks, 0.0), axis=0, keepdims=True).astype(jnp.int32) - part * cap
    target = jnp.where((rank >= 0) & (rank < cap), rel * cap + rank, -1)
    return (lax.broadcasted_iota(jnp.int32, (experts * cap, rows), 0) == target).astype(BF16)


def expert_kernel(*refs):
    count = (len(refs) - 12) // 2
    blocks, (one_ref, two_ref), outs = refs[:count], refs[count : count + 2], refs[count + 2 : 2 * count + 2]
    slot_out, proj_out, hidden_out, slot, one, two, back, proj, hidden, sems = refs[2 * count + 2 :]
    cap = blocks[0].shape[0]
    wide, width = two.shape
    copies = Copies(sems)
    loads = [copies.start(block, slot.at[index * cap : (index + 1) * cap]) for index, block in enumerate(blocks)]
    one_load = copies.start(one_ref, one)
    two_load = copies.start(two_ref, two)
    wait(loads)
    stores = [copies.start(slot, slot_out)]
    one_load.wait()
    both = dot(slot[:, :width], one[...], PLAIN)
    gate, upper = both[:, :wide], both[:, wide:]
    sigma = 1.0 / (1.0 + jnp.exp(-gate))
    silu = gate * sigma
    hidden[...] = (silu * upper).astype(BF16)
    stores.append(copies.start(hidden, hidden_out))
    two_load.wait()
    grad_hidden = dot(slot[:, width:], two[...], COLS)
    proj[...] = jnp.concatenate(
        [grad_hidden * upper * sigma * (1.0 + gate * (1.0 - sigma)), grad_hidden * silu], axis=1
    ).astype(BF16)
    stores.append(copies.start(proj, proj_out))
    back[:, :width] = dot(hidden[...], two[...], PLAIN).astype(BF16)
    back[:, width:] = dot(proj[...], one[...], COLS).astype(BF16)
    stores += [copies.start(back.at[index * cap : (index + 1) * cap], out) for index, out in enumerate(outs)]
    wait(stores)


def weight_kernel(end, parts, pieces, number_ref, *refs):
    sources, refs = refs[: 3 * parts], refs[3 * parts :]
    more, refs = refs[: sum(pieces)], refs[sum(pieces) :]
    results, sems = refs[-3 if end else -2 : -1], refs[-1]
    outs, (x, dy, proj, hidden, received) = refs[: -6 - len(results)], refs[-6 - len(results) : -1 - len(results)]
    cap = x.shape[0] // parts
    share, wide = x.shape[1], hidden.shape[1]
    width = sources[0].shape[1] // 2
    first = pl.multiple_of(number_ref[0] * share, share)
    copies = Copies(sems)
    loads = []
    for part in range(parts):
        slot_ref, proj_ref, hidden_ref = sources[3 * part : 3 * part + 3]
        here = slice(part * cap, (part + 1) * cap)
        loads.append(copies.start(slot_ref.at[:, pl.ds(first, share)], x.at[here]))
        loads.append(copies.start(slot_ref.at[:, pl.ds(pl.multiple_of(first + width, share), share)], dy.at[here]))
        loads.append(copies.start(proj_ref, proj.at[here]))
        loads.append(copies.start(hidden_ref, hidden.at[here]))
    more_loads = []
    for index, number in enumerate(pieces):
        row = 0
        for ref in more[:number]:
            more_loads.append(copies.start(ref, received.at[index, row : row + ref.shape[0]]))
            row += ref.shape[0]
        more = more[number:]
    wait(loads)
    up = dot(x[...], proj[...], ROWS)
    down = dot(hidden[...], dy[...], ROWS) if end else dot(dy[...], hidden[...], ROWS)
    wait(more_loads)
    for index in range(len(pieces)):
        up = up + received[index, :, : 2 * wide].astype(F32)
        extra = received[index, :, 2 * wide : 3 * wide]
        if end:
            row = lax.broadcasted_iota(jnp.int32, (share, share), 0)
            unit = (row == lax.broadcasted_iota(jnp.int32, (share, share), 1)).astype(BF16)
            down = down + dot(extra, unit, ROWS)
        else:
            down = down + extra.astype(F32)
    if end:
        results[0][...] = up
        results[1][...] = down
        wait([copies.start(result, out) for result, out in zip(results, outs)])
        return
    results[0][:, : 2 * wide] = up.astype(BF16)
    results[0][:, 2 * wide : 3 * wide] = down.astype(BF16)
    stores, row = [], 0
    for out in outs:
        stores.append(copies.start(results[0].at[row : row + out.shape[0]], out))
        row += out.shape[0]
    wait(stores)


def combine_kernel(part, cap, me_ref, table_ref, ids_ref, tokens_ref, grad_ref, *refs):
    blocks, (mixed_out, grad_out, data, back, sems) = refs[:-5], refs[-5:]
    width = tokens_ref.shape[1]
    copies = Copies(sems)
    loads = [copies.start(ref, data.at[:, side * width : (side + 1) * width]) for side, ref in enumerate((tokens_ref, grad_ref))]
    loads += [copies.start(block, back.at[index * cap : (index + 1) * cap]) for index, block in enumerate(blocks)]
    placing = placing_of(me_ref, table_ref, ids_ref, len(blocks), part, cap)
    wait(loads)
    stores = []
    for side, out in enumerate((mixed_out, grad_out)):
        here = slice(side * width, (side + 1) * width)
        data[:, here] = (data[:, here].astype(F32) + dot(placing, back[:, here], ROWS)).astype(BF16)
        stores.append(copies.start(data.at[:, here], out))
    wait(stores)


def after(value, *earlier):
    if not earlier:
        return value
    return lax.optimization_barrier((value, *earlier))[0]


class Lane:
    def __init__(self, window):
        self.window = window
        self.done = []

    def send(self, value, axis, pairs, *earlier):
        if len(self.done) >= self.window:
            earlier = (self.done[-self.window], *earlier)
        self.done.append(lax.ppermute(after(value, *earlier), axis, pairs))
        return self.done[-1]


def rounds_of(experts):
    half = experts // 2
    rounds = [list(range(experts))]
    for near in range(1, half):
        units = [unit for unit in range(1, half) if bin(unit & near).count("1") % 2 == 0]
        for turn in range(2):
            far_now = [bin(place & units[0]).count("1") % 2 == turn if units else not turn for place in range(experts)]
            rounds.append([place ^ (near + half if far else near) for place, far in zip(range(experts), far_now)])
    rounds.append([place ^ half for place in range(experts)])
    return rounds


def table_of(rounds):
    table = np.zeros((len(rounds), len(rounds)), np.int32)
    for number, partners in enumerate(rounds):
        for place, partner in enumerate(partners):
            table[place, partner] = number
    return table


def exchange(blocks, rounds, lane, held={}):
    moved = [blocks[0]]
    for number in range(1, len(rounds)):
        moved.append(lane.send(blocks[number], "exp", list(enumerate(rounds[number])), *held.get(number, ())))
    return moved


def body(tokens, expert_ids, gate_up_weight, down_weight, grad_out):
    rows, width = tokens.shape
    experts = lax.axis_size("exp")
    groups = lax.axis_size("grp")
    capacity = 2 * rows // experts
    parts = 2 if capacity % 32 == 0 else 1
    cap = capacity // parts
    slots = experts * cap
    weight_one = gate_up_weight[0]
    weight_two = down_weight[0]
    wide = weight_two.shape[0]
    share = width // groups
    pair = like((cap, 2 * width))
    sems = pltpu.SemaphoreType.DMA
    lane = Lane(4)
    last = experts - 1
    ids = expert_ids.reshape(1, rows)
    me = lax.axis_index("exp").astype(jnp.int32)[None]
    rounds = rounds_of(experts)
    table = jnp.asarray(table_of(rounds))
    group = lax.axis_index("grp").astype(jnp.int32)

    def place(part):
        return call(
            lambda *refs: place_kernel(part, cap, *refs),
            "place",
            [pair] * experts,
            [pltpu.VMEM((rows, 2 * width), BF16), pltpu.VMEM((slots, 2 * width), BF16), sems((2 + 2 * experts,))],
            [tokens, grad_out],
            [ids],
            [me, table],
        )

    def expert(blocks):
        shapes = [(slots, 2 * width), (slots, 2 * wide), (slots, wide)]
        back = [pltpu.VMEM(shape, BF16) for shape in shapes]
        scratch = [back[0], pltpu.VMEM(weight_one.shape, BF16), pltpu.VMEM(weight_two.shape, BF16)]
        outs = call(
            expert_kernel,
            "expert",
            [pair] * experts + [like(shape) for shape in shapes],
            scratch + back + [sems((5 + 2 * experts,))],
            [*blocks, weight_one, weight_two],
        )
        return outs[:experts], outs[experts:]

    def weight_part(number, kept, received, end, heads):
        shape = (share, pl.cdiv(3 * wide, 128) * 128)
        finals = [like((share, 2 * wide), F32), like((wide, share), F32)]
        rows_of = [heads, share - heads] if heads else [share]
        outs = finals if end else [like((count, shape[1])) for count in rows_of]
        total = parts * slots
        scratch = [pltpu.VMEM((total, width), BF16) for width in (share, share, 2 * wide, wide)]
        scratch.append(pltpu.VMEM((max(1, len(received)), *shape), BF16))
        scratch += [pltpu.VMEM(out.shape, out.dtype) for out in (finals if end else [like(shape)])]
        sources = [array for arrays in kept + received for array in arrays]
        scratch.append(sems((len(sources) + parts + len(outs),)))
        pieces = [len(arrays) for arrays in received]
        return call(
            lambda *refs: weight_kernel(end, parts, pieces, *refs),
            "weight_part",
            outs,
            scratch,
            sources,
            scalars=[number[None]],
        )

    def combine(part, first, second, blocks):
        return call(
            lambda *refs: combine_kernel(part, cap, *refs),
            "combine",
            [like((rows, width))] * 2,
            [pltpu.VMEM((rows, 2 * width), BF16), pltpu.VMEM((slots, 2 * width), BF16), sems((4 + experts,))],
            [first, second, *blocks],
            [ids],
            [me, table],
        )

    sent = [place(part) for part in range(parts)]
    results = []
    for part in range(parts):
        held = {last: (results[-1][0][0],)} if results else {}
        results.append(expert(exchange(sent[part], rounds, lane, held)))
    kept = [result[1] for result in results]

    count = len(lane.done)
    back = [exchange(results[0][0], rounds, lane)]
    done = lane.done[count:]

    received = {q: [] for q in range(groups)}
    sums = kept[0][0]
    for q in sorted(range(1, groups), key=lambda q: (q & -q, -q)):
        low = q & -q
        first_of_all = q == groups - 1
        if low == 2 and received[q ^ low]:
            sums = after(sums, *done[3:5])
        sent = weight_part(group ^ q, [[sums, *kept[0][1:]], *kept[1:]], received[q], False, 16 if first_of_all else 0)
        sums = after(sums, sent[0])
        pairs = [(i, i ^ low) for i in range(groups)]
        short = Lane(1)
        held = [(), done[:3]]
        received[q ^ low].append([short.send(piece, "grp", pairs, *more) for piece, more in zip(sent, held)])

    mixed, grad = tokens, grad_out
    for part in range(1, parts):
        mixed, grad = combine(part - 1, mixed, grad, back[-1])
        back.append(exchange(results[part][0], rounds, lane, {last: (mixed, *received[0][-1])}))
    grad_gate_up, grad_down = weight_part(group, [[sums, *kept[0][1:]], *kept[1:]], received[0], True, 0)
    back[-1][0] = after(back[-1][0], grad_gate_up)
    mixed, grad = combine(parts - 1, mixed, grad, back[-1])
    return (mixed, grad, grad_gate_up[None], grad_down[None])


def solution(mesh):
    in_specs = (
        P(("grp", "exp"), None),
        P(("grp", "exp"), None),
        P("exp", None, None),
        P("exp", None, None),
        P(("grp", "exp"), None),
    )
    out_specs = (
        P(("grp", "exp"), None),
        P(("grp", "exp"), None),
        P("exp", "grp", None),
        P("exp", None, "grp"),
    )
    return jax.shard_map(body, mesh=mesh, in_specs=in_specs, out_specs=out_specs, check_vma=False)
```

```python
import jax
import jax.numpy as jnp
import numpy as np
from jax import lax
from jax.experimental import pallas as pl
from jax.experimental.pallas import tpu as pltpu
from jax.sharding import PartitionSpec as P

VMEM_BYTES = 64 * 1024 * 1024
PIECES = 4
SMALL = pl.CostEstimate(flops=1024, bytes_accessed=1024, transcendentals=0)
BF16 = jnp.bfloat16
F32 = jnp.float32
ROWS = ((0,), (0,))
COLS = ((1,), (1,))
PLAIN = ((1,), (0,))


def dot(left, right, dims):
    return lax.dot_general(left, right, (dims, ((), ())), preferred_element_type=F32)


def like(shape, dtype=BF16):
    return jax.ShapeDtypeStruct(shape, dtype)


def call(kernel, name, outs, scratch, arrays, small=(), scalars=()):
    hbm = pl.BlockSpec(memory_space=pltpu.HBM)
    return pl.pallas_call(
        kernel,
        in_specs=[pl.BlockSpec(memory_space=pltpu.SMEM)] * len(scalars)
        + [pl.BlockSpec(memory_space=pltpu.VMEM)] * len(small)
        + [hbm] * len(arrays),
        out_specs=[hbm] * len(outs),
        out_shape=outs,
        scratch_shapes=scratch,
        compiler_params=pltpu.CompilerParams(vmem_limit_bytes=VMEM_BYTES),
        cost_estimate=SMALL,
        name=name,
    )(*scalars, *small, *arrays)


class Copies:
    def __init__(self, sems):
        self.sems = sems
        self.used = 0

    def start(self, source, target):
        copy = pltpu.make_async_copy(source, target, self.sems.at[self.used])
        self.used += 1
        copy.start()
        return copy


def wait(copies):
    for copy in copies:
        copy.wait()


def place_kernel(part, cap, me_ref, table_ref, ids_ref, tokens_ref, grad_ref, *refs):
    blocks, (data, moved, sems) = refs[:-3], refs[-3:]
    copies = Copies(sems)
    pieces = pieces_of(tokens_ref, grad_ref)
    loads = [copies.start(ref.at[:, there], data.at[:, here]) for ref, there, here in pieces]
    placing = placing_of(me_ref, table_ref, ids_ref, len(blocks), part, cap)
    stores = []
    for load, (_, _, here) in zip(loads, pieces):
        load.wait()
        moved[:, here] = dot(placing, data[:, here], PLAIN).astype(BF16)
        for index, block in enumerate(blocks):
            stores.append(copies.start(moved.at[index * cap : (index + 1) * cap, here], block.at[:, here]))
    wait(stores)


def pieces_of(first_ref, second_ref):
    width = first_ref.shape[1]
    step = width // (PIECES // 2)
    return [
        (ref, slice(start, start + step), slice(side * width + start, side * width + start + step))
        for side, ref in enumerate((first_ref, second_ref))
        for start in range(0, width, step)
    ]


def placing_of(me_ref, table_ref, ids_ref, experts, part, cap):
    ids = ids_ref[...]
    rows = ids.shape[1]
    me = me_ref[0]
    rel = jnp.zeros((1, rows), jnp.int32)
    for expert in range(experts):
        rel = jnp.where(ids == expert, table_ref[me, expert], rel)
    onehot = lax.broadcasted_iota(jnp.int32, (max(experts, 16), rows), 0) == rel
    before = lax.broadcasted_iota(jnp.int32, (rows, rows), 0) < lax.broadcasted_iota(jnp.int32, (rows, rows), 1)
    ranks = dot(onehot.astype(BF16), before.astype(BF16), PLAIN)
    rank = jnp.sum(jnp.where(onehot, ranks, 0.0), axis=0, keepdims=True).astype(jnp.int32) - part * cap
    target = jnp.where((rank >= 0) & (rank < cap), rel * cap + rank, -1)
    return (lax.broadcasted_iota(jnp.int32, (experts * cap, rows), 0) == target).astype(BF16)


def expert_kernel(*refs):
    count = (len(refs) - 12) // 2
    blocks, (one_ref, two_ref), outs = refs[:count], refs[count : count + 2], refs[count + 2 : 2 * count + 2]
    slot_out, proj_out, hidden_out, slot, one, two, back, proj, hidden, sems = refs[2 * count + 2 :]
    cap = blocks[0].shape[0]
    wide, width = two.shape
    copies = Copies(sems)
    loads = [copies.start(block, slot.at[index * cap : (index + 1) * cap]) for index, block in enumerate(blocks)]
    two_load = copies.start(two_ref, two)
    one_load = copies.start(one_ref, one)
    wait(loads)
    stores = [copies.start(slot, slot_out)]
    two_load.wait()
    grad_hidden = dot(slot[:, width:], two[...], COLS)
    one_load.wait()
    both = dot(slot[:, :width], one[...], PLAIN)
    gate, upper = both[:, :wide], both[:, wide:]
    sigma = 1.0 / (1.0 + jnp.exp(-gate))
    silu = gate * sigma
    hidden[...] = (silu * upper).astype(BF16)
    stores.append(copies.start(hidden, hidden_out))
    proj[...] = jnp.concatenate(
        [grad_hidden * upper * sigma * (1.0 + gate * (1.0 - sigma)), grad_hidden * silu], axis=1
    ).astype(BF16)
    stores.append(copies.start(proj, proj_out))
    back[:, :width] = dot(hidden[...], two[...], PLAIN).astype(BF16)
    back[:, width:] = dot(proj[...], one[...], COLS).astype(BF16)
    stores += [copies.start(back.at[index * cap : (index + 1) * cap], out) for index, out in enumerate(outs)]
    wait(stores)


def weight_kernel(end, parts, pieces, number_ref, *refs):
    sources, refs = refs[: 3 * parts], refs[3 * parts :]
    more, refs = refs[: sum(pieces)], refs[sum(pieces) :]
    results, sems = refs[-3 if end else -2 : -1], refs[-1]
    outs, (x, dy, proj, hidden, received) = refs[: -6 - len(results)], refs[-6 - len(results) : -1 - len(results)]
    cap = x.shape[0] // parts
    share, wide = x.shape[1], hidden.shape[1]
    width = sources[0].shape[1] // 2
    first = pl.multiple_of(number_ref[0] * share, share)
    copies = Copies(sems)
    loads = []
    for part in range(parts):
        slot_ref, proj_ref, hidden_ref = sources[3 * part : 3 * part + 3]
        here = slice(part * cap, (part + 1) * cap)
        loads.append(copies.start(slot_ref.at[:, pl.ds(first, share)], x.at[here]))
        loads.append(copies.start(slot_ref.at[:, pl.ds(pl.multiple_of(first + width, share), share)], dy.at[here]))
        loads.append(copies.start(proj_ref, proj.at[here]))
        loads.append(copies.start(hidden_ref, hidden.at[here]))
    more_loads = []
    for index, number in enumerate(pieces):
        row = 0
        for ref in more[:number]:
            more_loads.append(copies.start(ref, received.at[index, row : row + ref.shape[0]]))
            row += ref.shape[0]
        more = more[number:]
    wait(loads)
    up = dot(x[...], proj[...], ROWS)
    down = dot(hidden[...], dy[...], ROWS) if end else dot(dy[...], hidden[...], ROWS)
    wait(more_loads)
    for index in range(len(pieces)):
        up = up + received[index, :, : 2 * wide].astype(F32)
        extra = received[index, :, 2 * wide : 3 * wide]
        if end:
            row = lax.broadcasted_iota(jnp.int32, (share, share), 0)
            unit = (row == lax.broadcasted_iota(jnp.int32, (share, share), 1)).astype(BF16)
            down = down + dot(extra, unit, ROWS)
        else:
            down = down + extra.astype(F32)
    if end:
        results[0][...] = up
        results[1][...] = down
        wait([copies.start(result, out) for result, out in zip(results, outs)])
        return
    results[0][:, : 2 * wide] = up.astype(BF16)
    results[0][:, 2 * wide : 3 * wide] = down.astype(BF16)
    stores, row = [], 0
    for out in outs:
        stores.append(copies.start(results[0].at[row : row + out.shape[0]], out))
        row += out.shape[0]
    wait(stores)


def combine_kernel(part, cap, me_ref, table_ref, ids_ref, tokens_ref, grad_ref, *refs):
    blocks, (mixed_out, grad_out, data, back, sems) = refs[:-5], refs[-5:]
    copies = Copies(sems)
    pieces = pieces_of(tokens_ref, grad_ref)
    loads = []
    for ref, there, here in pieces:
        loads.append([copies.start(ref.at[:, there], data.at[:, here])])
        for index, block in enumerate(blocks):
            loads[-1].append(copies.start(block.at[:, here], back.at[index * cap : (index + 1) * cap, here]))
    placing = placing_of(me_ref, table_ref, ids_ref, len(blocks), part, cap)
    stores = []
    for load, (_, there, here), (out, _, _) in zip(loads, pieces, pieces_of(mixed_out, grad_out)):
        wait(load)
        data[:, here] = (data[:, here].astype(F32) + dot(placing, back[:, here], ROWS)).astype(BF16)
        stores.append(copies.start(data.at[:, here], out.at[:, there]))
    wait(stores)


def after(value, *earlier):
    if not earlier:
        return value
    return lax.optimization_barrier((value, *earlier))[0]


class Lane:
    def __init__(self, window):
        self.window = window
        self.done = []

    def send(self, value, axis, pairs, *earlier):
        if len(self.done) >= self.window:
            earlier = (self.done[-self.window], *earlier)
        self.done.append(lax.ppermute(after(value, *earlier), axis, pairs))
        return self.done[-1]


def rounds_of(experts):
    half = experts // 2
    rounds = [list(range(experts))]
    for near in range(1, half):
        units = [unit for unit in range(1, half) if bin(unit & near).count("1") % 2 == 0]
        for turn in range(2):
            far_now = [bin(place & units[0]).count("1") % 2 == turn if units else not turn for place in range(experts)]
            rounds.append([place ^ (near + half if far else near) for place, far in zip(range(experts), far_now)])
    rounds.append([place ^ half for place in range(experts)])
    return rounds


def table_of(rounds):
    table = np.zeros((len(rounds), len(rounds)), np.int32)
    for number, partners in enumerate(rounds):
        for place, partner in enumerate(partners):
            table[place, partner] = number
    return table


def exchange(blocks, rounds, lane, held={}):
    moved = [blocks[0]]
    for number in range(1, len(rounds)):
        moved.append(lane.send(blocks[number], "exp", list(enumerate(rounds[number])), *held.get(number, ())))
    return moved


def body(tokens, expert_ids, gate_up_weight, down_weight, grad_out):
    rows, width = tokens.shape
    experts = lax.axis_size("exp")
    groups = lax.axis_size("grp")
    capacity = 2 * rows // experts
    parts = 2 if capacity % 32 == 0 else 1
    cap = capacity // parts
    slots = experts * cap
    weight_one = gate_up_weight[0]
    weight_two = down_weight[0]
    wide = weight_two.shape[0]
    share = width // groups
    pair = like((cap, 2 * width))
    sems = pltpu.SemaphoreType.DMA
    lane = Lane(4)
    last = experts - 1
    ids = expert_ids.reshape(1, rows)
    me = lax.axis_index("exp").astype(jnp.int32)[None]
    rounds = rounds_of(experts)
    table = jnp.asarray(table_of(rounds))
    group = lax.axis_index("grp").astype(jnp.int32)

    def place(part):
        return call(
            lambda *refs: place_kernel(part, cap, *refs),
            "place",
            [pair] * experts,
            [pltpu.VMEM((rows, 2 * width), BF16), pltpu.VMEM((slots, 2 * width), BF16), sems((PIECES * (1 + experts),))],
            [tokens, grad_out],
            [ids],
            [me, table],
        )

    def expert(blocks):
        shapes = [(slots, 2 * width), (slots, 2 * wide), (slots, wide)]
        back = [pltpu.VMEM(shape, BF16) for shape in shapes]
        scratch = [back[0], pltpu.VMEM(weight_one.shape, BF16), pltpu.VMEM(weight_two.shape, BF16)]
        outs = call(
            expert_kernel,
            "expert",
            [pair] * experts + [like(shape) for shape in shapes],
            scratch + back + [sems((5 + 2 * experts,))],
            [*blocks, weight_one, weight_two],
        )
        return outs[:experts], outs[experts:]

    def weight_part(number, kept, received, end, heads):
        shape = (share, pl.cdiv(3 * wide, 128) * 128)
        finals = [like((share, 2 * wide), F32), like((wide, share), F32)]
        rows_of = [heads, share - heads] if heads else [share]
        outs = finals if end else [like((count, shape[1])) for count in rows_of]
        total = parts * slots
        scratch = [pltpu.VMEM((total, width), BF16) for width in (share, share, 2 * wide, wide)]
        scratch.append(pltpu.VMEM((max(1, len(received)), *shape), BF16))
        scratch += [pltpu.VMEM(out.shape, out.dtype) for out in (finals if end else [like(shape)])]
        sources = [array for arrays in kept + received for array in arrays]
        scratch.append(sems((len(sources) + parts + len(outs),)))
        pieces = [len(arrays) for arrays in received]
        return call(
            lambda *refs: weight_kernel(end, parts, pieces, *refs),
            "weight_part",
            outs,
            scratch,
            sources,
            scalars=[number[None]],
        )

    def combine(part, first, second, blocks):
        return call(
            lambda *refs: combine_kernel(part, cap, *refs),
            "combine",
            [like((rows, width))] * 2,
            [pltpu.VMEM((rows, 2 * width), BF16), pltpu.VMEM((slots, 2 * width), BF16), sems((PIECES * (2 + experts),))],
            [first, second, *blocks],
            [ids],
            [me, table],
        )

    sent = [place(part) for part in range(parts)]
    results = []
    for part in range(parts):
        held = {last: (results[-1][0][0],)} if results else {}
        results.append(expert(exchange(sent[part], rounds, lane, held)))
    kept = [result[1] for result in results]

    count = len(lane.done)
    back = [exchange(results[0][0], rounds, lane)]
    done = lane.done[count:]

    received = {q: [] for q in range(groups)}
    sums = kept[0][0]
    held = {groups - 1: done[:3], 2: done[3:6]}
    for q in sorted(range(1, groups), key=lambda q: (q & -q, -q)):
        low = q & -q
        sent = weight_part(group ^ q, [[sums, *kept[0][1:]], *kept[1:]], received[q], False, 16 if q in held else 0)
        sums = after(sums, sent[0])
        pairs = [(i, i ^ low) for i in range(groups)]
        short = Lane(1)
        received[q ^ low].append([short.send(sent[0], "grp", pairs)])
        received[q ^ low][-1] += [short.send(piece, "grp", pairs, *held[q]) for piece in sent[1:]]

    mixed, grad = tokens, grad_out
    for part in range(1, parts):
        mixed, grad = combine(part - 1, mixed, grad, back[-1])
        back.append(exchange(results[part][0], rounds, lane, {last: (mixed, *received[0][-1])}))
    grad_gate_up, grad_down = weight_part(group, [[sums, *kept[0][1:]], *kept[1:]], received[0], True, 0)
    back[-1][0] = after(back[-1][0], grad_gate_up)
    mixed, grad = combine(parts - 1, mixed, grad, back[-1])
    return (mixed, grad, grad_gate_up[None], grad_down[None])


def solution(mesh):
    in_specs = (
        P(("grp", "exp"), None),
        P(("grp", "exp"), None),
        P("exp", None, None),
        P("exp", None, None),
        P(("grp", "exp"), None),
    )
    out_specs = (
        P(("grp", "exp"), None),
        P(("grp", "exp"), None),
        P("exp", "grp", None),
        P("exp", None, "grp"),
    )
    return jax.shard_map(body, mesh=mesh, in_specs=in_specs, out_specs=out_specs, check_vma=False)
```

```python
import jax
import jax.numpy as jnp
from jax import lax
from jax.experimental import pallas as pl
from jax.experimental.pallas import tpu as pltpu
from jax.sharding import PartitionSpec as P

VMEM_BYTES = 64 * 1024 * 1024
PIECES = 4
SMALL = pl.CostEstimate(flops=1024, bytes_accessed=1024, transcendentals=0)
BF16 = jnp.bfloat16
F32 = jnp.float32
ROWS = ((0,), (0,))
COLS = ((1,), (1,))
PLAIN = ((1,), (0,))


def dot(left, right, dims):
    return lax.dot_general(left, right, (dims, ((), ())), preferred_element_type=F32)


def like(shape, dtype=BF16):
    return jax.ShapeDtypeStruct(shape, dtype)


def call(kernel, name, outs, scratch, arrays, scalars=()):
    hbm = pl.BlockSpec(memory_space=pltpu.HBM)
    return pl.pallas_call(
        kernel,
        in_specs=[pl.BlockSpec(memory_space=pltpu.SMEM)] * len(scalars) + [hbm] * len(arrays),
        out_specs=[hbm] * len(outs),
        out_shape=outs,
        scratch_shapes=scratch,
        compiler_params=pltpu.CompilerParams(vmem_limit_bytes=VMEM_BYTES),
        cost_estimate=SMALL,
        name=name,
    )(*scalars, *arrays)


class Copies:
    def __init__(self, sems):
        self.sems = sems
        self.used = 0

    def start(self, source, target):
        copy = pltpu.make_async_copy(source, target, self.sems.at[self.used])
        self.used += 1
        copy.start()
        return copy


def wait(copies):
    for copy in copies:
        copy.wait()


def place_kernel(part, cap, ids_ref, tokens_ref, grad_ref, *refs):
    blocks, (ids, data, moved, sems) = refs[:-4], refs[-4:]
    copies = Copies(sems)
    ids_load = copies.start(ids_ref, ids)
    pieces = pieces_of(tokens_ref, grad_ref)
    loads = [copies.start(ref.at[:, there], data.at[:, here]) for ref, there, here in pieces]
    ids_load.wait()
    placing = placing_of(ids[...], len(blocks), part, cap)
    stores = []
    for load, (_, _, here) in zip(loads, pieces):
        load.wait()
        moved[:, here] = dot(placing, data[:, here], PLAIN).astype(BF16)
        stores += store_rows(copies, moved, blocks, here)
    wait(stores)


def pieces_of(first_ref, second_ref):
    width = first_ref.shape[1]
    step = width // (PIECES // 2)
    return [
        (ref, slice(start, start + step), slice(side * width + start, side * width + start + step))
        for side, ref in enumerate((first_ref, second_ref))
        for start in range(0, width, step)
    ]


def placing_of(ids, experts, part, cap):
    rows = ids.shape[1]
    rel = jnp.zeros((1, rows), jnp.int32)
    me = lax.axis_index("exp").astype(jnp.int32)
    for mask in range(1, experts):
        rel = jnp.where(ids == (me ^ mask), round_of(me, mask, experts), rel)
    onehot = lax.broadcasted_iota(jnp.int32, (max(experts, 16), rows), 0) == rel
    before = lax.broadcasted_iota(jnp.int32, (rows, rows), 0) < lax.broadcasted_iota(jnp.int32, (rows, rows), 1)
    ranks = dot(onehot.astype(BF16), before.astype(BF16), PLAIN)
    rank = jnp.sum(jnp.where(onehot, ranks, 0.0), axis=0, keepdims=True).astype(jnp.int32) - part * cap
    target = jnp.where((rank >= 0) & (rank < cap), rel * cap + rank, -1)
    return (lax.broadcasted_iota(jnp.int32, (experts * cap, rows), 0) == target).astype(BF16)


def expert_kernel(*refs):
    count = (len(refs) - 12) // 2
    blocks, (one_ref, two_ref), outs = refs[:count], refs[count : count + 2], refs[count + 2 : 2 * count + 2]
    slot_out, proj_out, hidden_out, slot, one, two, back, proj, hidden, sems = refs[2 * count + 2 :]
    cap = blocks[0].shape[0]
    wide, width = two.shape
    copies = Copies(sems)
    loads = [copies.start(block, slot.at[index * cap : (index + 1) * cap]) for index, block in enumerate(blocks)]
    two_load = copies.start(two_ref, two)
    half = width // 2
    one_loads = [copies.start(one_ref.at[start : start + half], one.at[start : start + half]) for start in (0, half)]
    wait(loads)
    stores = [copies.start(slot, slot_out)]
    two_load.wait()
    grad_hidden = dot(slot[:, width:], two[...], COLS)
    one_loads[0].wait()
    both = dot(slot[:, :half], one[:half], PLAIN)
    one_loads[1].wait()
    both = both + dot(slot[:, half:width], one[half:], PLAIN)
    gate, upper = both[:, :wide], both[:, wide:]
    sigma = 1.0 / (1.0 + jnp.exp(-gate))
    silu = gate * sigma
    hidden[...] = (silu * upper).astype(BF16)
    stores.append(copies.start(hidden, hidden_out))
    proj[...] = jnp.concatenate(
        [grad_hidden * upper * sigma * (1.0 + gate * (1.0 - sigma)), grad_hidden * silu], axis=1
    ).astype(BF16)
    stores.append(copies.start(proj, proj_out))
    back[:, :width] = dot(hidden[...], two[...], PLAIN).astype(BF16)
    stores += store_rows(copies, back, outs, slice(0, width))
    back[:, width:] = dot(proj[...], one[...], COLS).astype(BF16)
    stores += store_rows(copies, back, outs, slice(width, 2 * width))
    wait(stores)


def store_rows(copies, source, outs, here):
    cap = outs[0].shape[0]
    return [copies.start(source.at[index * cap : (index + 1) * cap, here], out.at[:, here]) for index, out in enumerate(outs)]


def weight_kernel(end, parts, pieces, number_ref, *refs):
    sources, refs = refs[: 3 * parts], refs[3 * parts :]
    more, refs = refs[: sum(pieces)], refs[sum(pieces) :]
    results, sems = refs[-3 if end else -2 : -1], refs[-1]
    outs, (x, dy, proj, hidden, received) = refs[: -6 - len(results)], refs[-6 - len(results) : -1 - len(results)]
    cap = x.shape[0] // parts
    share, wide = x.shape[1], hidden.shape[1]
    width = sources[0].shape[1] // 2
    first = pl.multiple_of(number_ref[0] * share, share)
    copies = Copies(sems)
    loads = []
    for part in range(parts):
        slot_ref, proj_ref, hidden_ref = sources[3 * part : 3 * part + 3]
        here = slice(part * cap, (part + 1) * cap)
        loads.append(copies.start(slot_ref.at[:, pl.ds(first, share)], x.at[here]))
        loads.append(copies.start(slot_ref.at[:, pl.ds(pl.multiple_of(first + width, share), share)], dy.at[here]))
        loads.append(copies.start(proj_ref, proj.at[here]))
        loads.append(copies.start(hidden_ref, hidden.at[here]))
    more_loads = []
    for index, number in enumerate(pieces):
        row = 0
        for ref in more[:number]:
            more_loads.append(copies.start(ref, received.at[index, row : row + ref.shape[0]]))
            row += ref.shape[0]
        more = more[number:]
    wait(loads)
    up = dot(x[...], proj[...], ROWS)
    down = dot(hidden[...], dy[...], ROWS) if end else dot(dy[...], hidden[...], ROWS)
    wait(more_loads)
    for index in range(len(pieces)):
        up = up + received[index, :, : 2 * wide].astype(F32)
        extra = received[index, :, 2 * wide : 3 * wide]
        if end:
            row = lax.broadcasted_iota(jnp.int32, (share, share), 0)
            unit = (row == lax.broadcasted_iota(jnp.int32, (share, share), 1)).astype(BF16)
            down = down + dot(extra, unit, ROWS)
        else:
            down = down + extra.astype(F32)
    if end:
        results[0][...] = up
        results[1][...] = down
        wait([copies.start(result, out) for result, out in zip(results, outs)])
        return
    results[0][:, : 2 * wide] = up.astype(BF16)
    results[0][:, 2 * wide : 3 * wide] = down.astype(BF16)
    stores, row = [], 0
    for out in outs:
        stores.append(copies.start(results[0].at[row : row + out.shape[0]], out))
        row += out.shape[0]
    wait(stores)


def combine_kernel(part, cap, ids_ref, tokens_ref, grad_ref, *refs):
    blocks, (mixed_out, grad_out, ids, data, back, sems) = refs[:-6], refs[-6:]
    copies = Copies(sems)
    ids_load = copies.start(ids_ref, ids)
    pieces = pieces_of(tokens_ref, grad_ref)
    loads = []
    for ref, there, here in pieces:
        loads.append([copies.start(ref.at[:, there], data.at[:, here])])
        for index, block in enumerate(blocks):
            loads[-1].append(copies.start(block.at[:, here], back.at[index * cap : (index + 1) * cap, here]))
    ids_load.wait()
    placing = placing_of(ids[...], len(blocks), part, cap)
    stores = []
    for load, (_, there, here), (out, _, _) in zip(loads, pieces, pieces_of(mixed_out, grad_out)):
        wait(load)
        data[:, here] = (data[:, here].astype(F32) + dot(placing, back[:, here], ROWS)).astype(BF16)
        stores.append(copies.start(data.at[:, here], out.at[:, there]))
    wait(stores)


def after(value, *earlier):
    if not earlier:
        return value
    return lax.optimization_barrier((value, *earlier))[0]


class Lane:
    def __init__(self, window):
        self.window = window
        self.done = []

    def send(self, value, axis, pairs, *earlier):
        if len(self.done) >= self.window:
            earlier = (self.done[-self.window], *earlier)
        self.done.append(lax.ppermute(after(value, *earlier), axis, pairs))
        return self.done[-1]


def rounds_of(experts):
    rounds = [[0] * experts for _ in range(experts)]
    for place in range(experts):
        for mask in range(experts):
            rounds[round_of(place, mask, experts)][place] = place ^ mask
    return rounds


def round_of(place, mask, experts):
    half = experts // 2
    near = mask % half
    if near == 0:
        return experts - 1 if mask else 0
    units = [unit for unit in range(1, half) if bin(unit & near).count("1") % 2 == 0]
    turn = 0
    for bit in range(half.bit_length() if units else 0):
        if units[0] >> bit & 1:
            turn = turn ^ ((place >> bit) & 1)
    return 2 * near - 1 + (turn if mask >= half else 1 - turn)


def exchange(blocks, rounds, lane, numbers, *earlier):
    moved = []
    for number in numbers:
        more = earlier if number == numbers[-1] else ()
        moved.append(lane.send(blocks[number], "exp", list(enumerate(rounds[number])), *more))
    return moved


def body(tokens, expert_ids, gate_up_weight, down_weight, grad_out):
    rows, width = tokens.shape
    experts = lax.axis_size("exp")
    groups = lax.axis_size("grp")
    capacity = 2 * rows // experts
    parts = 2 if capacity % 32 == 0 else 1
    cap = capacity // parts
    slots = experts * cap
    weight_one = gate_up_weight[0]
    weight_two = down_weight[0]
    wide = weight_two.shape[0]
    share = width // groups
    pair = like((cap, 2 * width))
    sems = pltpu.SemaphoreType.DMA
    ids_here = pltpu.VMEM((1, rows), jnp.int32)
    halves = [pltpu.VMEM((count, 2 * width), BF16) for count in (rows, slots)]
    lane = Lane(4)
    numbers = range(1, experts)
    ids = expert_ids.reshape(1, rows)
    rounds = rounds_of(experts)
    group = lax.axis_index("grp").astype(jnp.int32)

    def place(part):
        return call(
            lambda *refs: place_kernel(part, cap, *refs),
            "place",
            [pair] * experts,
            [ids_here, *halves, sems((1 + PIECES * (1 + experts),))],
            [ids, tokens, grad_out],
        )

    def expert(blocks):
        shapes = [(slots, 2 * width), (slots, 2 * wide), (slots, wide)]
        back = [pltpu.VMEM(shape, BF16) for shape in shapes]
        scratch = [back[0], pltpu.VMEM(weight_one.shape, BF16), pltpu.VMEM(weight_two.shape, BF16)]
        outs = call(
            expert_kernel,
            "expert",
            [pair] * experts + [like(shape) for shape in shapes],
            scratch + back + [sems((6 + 3 * experts,))],
            [*blocks, weight_one, weight_two],
        )
        return outs[:experts], outs[experts:]

    def weight_part(number, kept, received, end, heads):
        shape = (share, pl.cdiv(3 * wide, 128) * 128)
        finals = [like((share, 2 * wide), F32), like((wide, share), F32)]
        rows_of = [heads, share - heads] if heads else [share]
        outs = finals if end else [like((count, shape[1])) for count in rows_of]
        total = parts * slots
        scratch = [pltpu.VMEM((total, width), BF16) for width in (share, share, 2 * wide, wide)]
        scratch.append(pltpu.VMEM((max(1, len(received)), *shape), BF16))
        scratch += [pltpu.VMEM(out.shape, out.dtype) for out in (finals if end else [like(shape)])]
        sources = [array for arrays in kept + received for array in arrays]
        scratch.append(sems((len(sources) + parts + len(outs),)))
        pieces = [len(arrays) for arrays in received]
        return call(
            lambda *refs: weight_kernel(end, parts, pieces, *refs),
            "weight_part",
            outs,
            scratch,
            sources,
            scalars=[number[None]],
        )

    def combine(part, first, second, blocks):
        return call(
            lambda *refs: combine_kernel(part, cap, *refs),
            "combine",
            [like((rows, width))] * 2,
            [ids_here, *halves, sems((1 + PIECES * (2 + experts),))],
            [ids, first, second, *blocks],
        )

    sent = [place(part) for part in range(parts)]
    results = []
    for part in range(parts):
        earlier = [results[-1][0][0]] if results else []
        results.append(expert([sent[part][0]] + exchange(sent[part], rounds, lane, numbers, *earlier)))
    kept = [result[1] for result in results]

    count = len(lane.done)
    mixed, grad = tokens, grad_out
    back = []
    for part in range(parts):
        if back:
            mixed, grad = combine(part - 1, mixed, grad, back)
        blocks = results[part][0]
        back = [blocks[0]] + exchange(blocks, rounds, lane, numbers if part < parts - 1 else numbers[:-1])
    done = lane.done[count:]

    received = {q: [] for q in range(groups)}
    sums = kept[0][0]
    held = {groups - 1: done[:3], 2: done[3:5]}
    for q in sorted(range(1, groups), key=lambda q: (q & -q, -q)):
        low = q & -q
        sent = weight_part(group ^ q, [[sums, *kept[0][1:]], *kept[1:]], received[q], False, 16 if q in held else 0)
        sums = after(sums, sent[0])
        pairs = [(i, i ^ low) for i in range(groups)]
        short = Lane(1)
        received[q ^ low].append([short.send(sent[0], "grp", pairs)])
        received[q ^ low][-1] += [short.send(piece, "grp", pairs, *held[q]) for piece in sent[1:]]

    grad_gate_up, grad_down = weight_part(group, [[sums, *kept[0][1:]], *kept[1:]], received[0], True, 0)
    back += exchange(blocks, rounds, lane, numbers[-1:], mixed, lane.done[-3])
    back[0] = after(back[0], grad_gate_up)
    mixed, grad = combine(parts - 1, mixed, grad, back)
    return (mixed, grad, grad_gate_up[None], grad_down[None])


def solution(mesh):
    in_specs = (
        P(("grp", "exp"), None),
        P(("grp", "exp"), None),
        P("exp", None, None),
        P("exp", None, None),
        P(("grp", "exp"), None),
    )
    out_specs = (
        P(("grp", "exp"), None),
        P(("grp", "exp"), None),
        P("exp", "grp", None),
        P("exp", None, "grp"),
    )
    return jax.shard_map(body, mesh=mesh, in_specs=in_specs, out_specs=out_specs, check_vma=False)
```

```python
import jax
import jax.numpy as jnp
from jax import lax
from jax.experimental import pallas as pl
from jax.experimental.pallas import tpu as pltpu
from jax.sharding import PartitionSpec as P

VMEM_BYTES = 64 * 1024 * 1024
PIECES = 4
SMALL = pl.CostEstimate(flops=1024, bytes_accessed=1024, transcendentals=0)
BF16 = jnp.bfloat16
F32 = jnp.float32
ROWS = ((0,), (0,))
COLS = ((1,), (1,))
PLAIN = ((1,), (0,))


def dot(left, right, dims):
    return lax.dot_general(left, right, (dims, ((), ())), preferred_element_type=F32)


def like(shape, dtype=BF16):
    return jax.ShapeDtypeStruct(shape, dtype)


def call(kernel, name, outs, scratch, arrays, scalars=()):
    hbm = pl.BlockSpec(memory_space=pltpu.HBM)
    return pl.pallas_call(
        kernel,
        in_specs=[pl.BlockSpec(memory_space=pltpu.SMEM)] * len(scalars) + [hbm] * len(arrays),
        out_specs=[hbm] * len(outs),
        out_shape=outs,
        scratch_shapes=scratch,
        compiler_params=pltpu.CompilerParams(vmem_limit_bytes=VMEM_BYTES),
        cost_estimate=SMALL,
        name=name,
    )(*scalars, *arrays)


class Copies:
    def __init__(self, sems):
        self.sems = sems
        self.used = 0

    def start(self, source, target):
        copy = pltpu.make_async_copy(source, target, self.sems.at[self.used])
        self.used += 1
        copy.start()
        return copy


def wait(copies):
    for copy in copies:
        copy.wait()


def place_kernel(part, cap, ids_ref, tokens_ref, grad_ref, *refs):
    blocks, (ids, data, moved, sems) = refs[:-4], refs[-4:]
    copies = Copies(sems)
    ids_load = copies.start(ids_ref, ids)
    pieces = pieces_of(tokens_ref, grad_ref)
    loads = [copies.start(ref.at[:, there], data.at[:, here]) for ref, there, here in pieces]
    ids_load.wait()
    placing = placing_of(ids[...], len(blocks), part, cap)
    stores = []
    for load, (_, _, here) in zip(loads, pieces):
        load.wait()
        moved[:, here] = dot(placing, data[:, here], PLAIN).astype(BF16)
        stores += store_rows(copies, moved, blocks, here)
    wait(stores)


def pieces_of(first_ref, second_ref):
    width = first_ref.shape[1]
    step = width // (PIECES // 2)
    return [
        (ref, slice(start, start + step), slice(side * width + start, side * width + start + step))
        for side, ref in enumerate((first_ref, second_ref))
        for start in range(0, width, step)
    ]


def placing_of(ids, experts, part, cap):
    rows = ids.shape[1]
    rel = jnp.zeros((1, rows), jnp.int32)
    me = lax.axis_index("exp").astype(jnp.int32)
    for mask in range(1, experts):
        rel = jnp.where(ids == (me ^ mask), round_of(me, mask, experts), rel)
    onehot = lax.broadcasted_iota(jnp.int32, (max(experts, 16), rows), 0) == rel
    before = lax.broadcasted_iota(jnp.int32, (rows, rows), 0) < lax.broadcasted_iota(jnp.int32, (rows, rows), 1)
    ranks = dot(onehot.astype(BF16), before.astype(BF16), PLAIN)
    rank = jnp.sum(jnp.where(onehot, ranks, 0.0), axis=0, keepdims=True).astype(jnp.int32) - part * cap
    target = jnp.where((rank >= 0) & (rank < cap), rel * cap + rank, -1)
    return (lax.broadcasted_iota(jnp.int32, (experts * cap, rows), 0) == target).astype(BF16)


def expert_kernel(*refs):
    count = (len(refs) - 12) // 2
    blocks, (one_ref, two_ref), outs = refs[:count], refs[count : count + 2], refs[count + 2 : 2 * count + 2]
    slot_out, proj_out, hidden_out, slot, one, two, back, proj, hidden, sems = refs[2 * count + 2 :]
    cap = blocks[0].shape[0]
    wide, width = two.shape
    copies = Copies(sems)
    loads = [copies.start(block, slot.at[index * cap : (index + 1) * cap]) for index, block in enumerate(blocks)]
    two_load = copies.start(two_ref, two)
    half = width // 2
    one_loads = [copies.start(one_ref.at[start : start + half], one.at[start : start + half]) for start in (0, half)]
    wait(loads)
    stores = [copies.start(slot, slot_out)]
    two_load.wait()
    grad_hidden = dot(slot[:, width:], two[...], COLS)
    one_loads[0].wait()
    both = dot(slot[:, :half], one[:half], PLAIN)
    one_loads[1].wait()
    both = both + dot(slot[:, half:width], one[half:], PLAIN)
    gate, upper = both[:, :wide], both[:, wide:]
    sigma = 1.0 / (1.0 + jnp.exp(-gate))
    silu = gate * sigma
    hidden[...] = (silu * upper).astype(BF16)
    stores.append(copies.start(hidden, hidden_out))
    proj[...] = jnp.concatenate(
        [grad_hidden * upper * sigma * (1.0 + gate * (1.0 - sigma)), grad_hidden * silu], axis=1
    ).astype(BF16)
    stores.append(copies.start(proj, proj_out))
    back[:, :width] = dot(hidden[...], two[...], PLAIN).astype(BF16)
    stores += store_rows(copies, back, outs, slice(0, width))
    back[:, width:] = dot(proj[...], one[...], COLS).astype(BF16)
    stores += store_rows(copies, back, outs, slice(width, 2 * width))
    wait(stores)


def store_rows(copies, source, outs, here):
    cap = outs[0].shape[0]
    return [copies.start(source.at[index * cap : (index + 1) * cap, here], out.at[:, here]) for index, out in enumerate(outs)]


def weight_kernel(end, parts, pieces, number_ref, *refs):
    sources, refs = refs[: 3 * parts], refs[3 * parts :]
    more, refs = refs[: sum(pieces)], refs[sum(pieces) :]
    results, sems = refs[-3 if end else -2 : -1], refs[-1]
    outs, (x, dy, proj, hidden, received) = refs[: -6 - len(results)], refs[-6 - len(results) : -1 - len(results)]
    cap = x.shape[0] // parts
    share, wide = x.shape[1], hidden.shape[1]
    width = sources[0].shape[1] // 2
    first = pl.multiple_of(number_ref[0] * share, share)
    copies = Copies(sems)
    loads = []
    for part in range(parts):
        slot_ref, proj_ref, hidden_ref = sources[3 * part : 3 * part + 3]
        here = slice(part * cap, (part + 1) * cap)
        loads.append(copies.start(slot_ref.at[:, pl.ds(first, share)], x.at[here]))
        loads.append(copies.start(slot_ref.at[:, pl.ds(pl.multiple_of(first + width, share), share)], dy.at[here]))
        loads.append(copies.start(proj_ref, proj.at[here]))
        loads.append(copies.start(hidden_ref, hidden.at[here]))
    more_loads = []
    for index, number in enumerate(pieces):
        row = 0
        for ref in more[:number]:
            more_loads.append(copies.start(ref, received.at[index, row : row + ref.shape[0]]))
            row += ref.shape[0]
        more = more[number:]
    wait(loads)
    up = dot(x[...], proj[...], ROWS)
    down = dot(hidden[...], dy[...], ROWS) if end else dot(dy[...], hidden[...], ROWS)
    wait(more_loads)
    for index in range(len(pieces)):
        up = up + received[index, :, : 2 * wide].astype(F32)
        extra = received[index, :, 2 * wide : 3 * wide]
        if end:
            row = lax.broadcasted_iota(jnp.int32, (share, share), 0)
            unit = (row == lax.broadcasted_iota(jnp.int32, (share, share), 1)).astype(BF16)
            down = down + dot(extra, unit, ROWS)
        else:
            down = down + extra.astype(F32)
    if end:
        results[0][...] = up
        results[1][...] = down
        wait([copies.start(result, out) for result, out in zip(results, outs)])
        return
    results[0][:, : 2 * wide] = up.astype(BF16)
    results[0][:, 2 * wide : 3 * wide] = down.astype(BF16)
    stores, row = [], 0
    for out in outs:
        stores.append(copies.start(results[0].at[row : row + out.shape[0]], out))
        row += out.shape[0]
    wait(stores)


def combine_kernel(part, cap, ids_ref, tokens_ref, grad_ref, *refs):
    blocks, (mixed_out, grad_out, ids, data, back, sems) = refs[:-6], refs[-6:]
    copies = Copies(sems)
    ids_load = copies.start(ids_ref, ids)
    pieces = pieces_of(tokens_ref, grad_ref)
    loads = []
    for ref, there, here in pieces:
        loads.append([copies.start(ref.at[:, there], data.at[:, here])])
        for index, block in enumerate(blocks):
            loads[-1].append(copies.start(block.at[:, here], back.at[index * cap : (index + 1) * cap, here]))
    ids_load.wait()
    placing = placing_of(ids[...], len(blocks), part, cap)
    stores = []
    for load, (_, there, here), (out, _, _) in zip(loads, pieces, pieces_of(mixed_out, grad_out)):
        wait(load)
        data[:, here] = (data[:, here].astype(F32) + dot(placing, back[:, here], ROWS)).astype(BF16)
        stores.append(copies.start(data.at[:, here], out.at[:, there]))
    wait(stores)


def after(value, *earlier):
    if not earlier:
        return value
    return lax.optimization_barrier((value, *earlier))[0]


class Lane:
    def __init__(self, window):
        self.window = window
        self.done = []

    def send(self, value, axis, pairs, *earlier):
        if len(self.done) >= self.window:
            earlier = (self.done[-self.window], *earlier)
        self.done.append(lax.ppermute(after(value, *earlier), axis, pairs))
        return self.done[-1]


def rounds_of(experts):
    rounds = [[0] * experts for _ in range(experts)]
    for place in range(experts):
        for mask in range(experts):
            rounds[round_of(place, mask, experts)][place] = place ^ mask
    return rounds


def round_of(place, mask, experts):
    half = experts // 2
    near = mask % half
    if near == 0:
        return experts - 1 if mask else 0
    units = [unit for unit in range(1, half) if bin(unit & near).count("1") % 2 == 0]
    turn = 0
    for bit in range(half.bit_length() if units else 0):
        if units[0] >> bit & 1:
            turn = turn ^ ((place >> bit) & 1)
    return 2 * near - 1 + (turn if mask >= half else 1 - turn)


def exchange(blocks, rounds, lane, numbers, *earlier):
    moved = []
    for number in numbers:
        more = earlier if number == numbers[-1] else ()
        moved.append(lane.send(blocks[number], "exp", list(enumerate(rounds[number])), *more))
    return moved


def body(tokens, expert_ids, gate_up_weight, down_weight, grad_out):
    rows, width = tokens.shape
    experts = lax.axis_size("exp")
    groups = lax.axis_size("grp")
    capacity = 2 * rows // experts
    parts = 2 if capacity % 32 == 0 else 1
    cap = capacity // parts
    slots = experts * cap
    weight_one = gate_up_weight[0]
    weight_two = down_weight[0]
    wide = weight_two.shape[0]
    share = width // groups
    pair = like((cap, 2 * width))
    sems = pltpu.SemaphoreType.DMA
    ids_here = pltpu.VMEM((1, rows), jnp.int32)
    halves = [pltpu.VMEM((count, 2 * width), BF16) for count in (rows, slots)]
    lane = Lane(4)
    numbers = range(1, experts)
    ids = expert_ids.reshape(1, rows)
    rounds = rounds_of(experts)
    group = lax.axis_index("grp").astype(jnp.int32)

    def place(part):
        return call(
            lambda *refs: place_kernel(part, cap, *refs),
            "place",
            [pair] * experts,
            [ids_here, *halves, sems((1 + PIECES * (1 + experts),))],
            [ids, tokens, grad_out],
        )

    def expert(blocks):
        shapes = [(slots, 2 * width), (slots, 2 * wide), (slots, wide)]
        back = [pltpu.VMEM(shape, BF16) for shape in shapes]
        scratch = [back[0], pltpu.VMEM(weight_one.shape, BF16), pltpu.VMEM(weight_two.shape, BF16)]
        outs = call(
            expert_kernel,
            "expert",
            [pair] * experts + [like(shape) for shape in shapes],
            scratch + back + [sems((6 + 3 * experts,))],
            [*blocks, weight_one, weight_two],
        )
        return outs[:experts], outs[experts:]

    def weight_part(number, kept, received, end, heads):
        shape = (share, pl.cdiv(3 * wide, 128) * 128)
        finals = [like((share, 2 * wide), F32), like((wide, share), F32)]
        rows_of = [heads, share - heads] if heads else [share]
        outs = finals if end else [like((count, shape[1])) for count in rows_of]
        total = parts * slots
        scratch = [pltpu.VMEM((total, width), BF16) for width in (share, share, 2 * wide, wide)]
        scratch.append(pltpu.VMEM((max(1, len(received)), *shape), BF16))
        scratch += [pltpu.VMEM(out.shape, out.dtype) for out in (finals if end else [like(shape)])]
        sources = [array for arrays in kept + received for array in arrays]
        scratch.append(sems((len(sources) + parts + len(outs),)))
        pieces = [len(arrays) for arrays in received]
        return call(
            lambda *refs: weight_kernel(end, parts, pieces, *refs),
            "weight_part",
            outs,
            scratch,
            sources,
            scalars=[number[None]],
        )

    def combine(part, first, second, blocks):
        return call(
            lambda *refs: combine_kernel(part, cap, *refs),
            "combine",
            [like((rows, width))] * 2,
            [ids_here, *halves, sems((1 + PIECES * (2 + experts),))],
            [ids, first, second, *blocks],
        )

    sent = [place(part) for part in range(parts)]
    results = []
    for part in range(parts):
        earlier = [results[-1][0][0]] if results else []
        results.append(expert([sent[part][0]] + exchange(sent[part], rounds, lane, numbers, *earlier)))
    kept = [result[1] for result in results]

    count = len(lane.done)
    mixed, grad = tokens, grad_out
    back = []
    for part in range(parts):
        if back:
            mixed, grad = combine(part - 1, mixed, grad, back)
        blocks = results[part][0]
        back = [blocks[0]] + exchange(blocks, rounds, lane, numbers if part < parts - 1 else numbers[:-1])
    done = lane.done[count:]

    received = {q: [] for q in range(groups)}
    sums = kept[0][0]
    held = {groups - 1: done[:4], 2: done[4:6]}
    for q in sorted(range(1, groups), key=lambda q: (q & -q, -q)):
        low = q & -q
        sent = weight_part(group ^ q, [[sums, *kept[0][1:]], *kept[1:]], received[q], False, 16 if q in held else 0)
        sums = after(sums, sent[0])
        pairs = [(i, i ^ low) for i in range(groups)]
        short = Lane(1)
        received[q ^ low].append([short.send(sent[0], "grp", pairs)])
        received[q ^ low][-1] += [short.send(piece, "grp", pairs, *held[q]) for piece in sent[1:]]

    grad_gate_up, grad_down = weight_part(group, [[sums, *kept[0][1:]], *kept[1:]], received[0], True, 0)
    back += exchange(blocks, rounds, lane, numbers[-1:], mixed, lane.done[-3])
    back[0] = after(back[0], grad_gate_up)
    mixed, grad = combine(parts - 1, mixed, grad, back)
    return (mixed, grad, grad_gate_up[None], grad_down[None])


def solution(mesh):
    in_specs = (
        P(("grp", "exp"), None),
        P(("grp", "exp"), None),
        P("exp", None, None),
        P("exp", None, None),
        P(("grp", "exp"), None),
    )
    out_specs = (
        P(("grp", "exp"), None),
        P(("grp", "exp"), None),
        P("exp", "grp", None),
        P("exp", None, "grp"),
    )
    return jax.shard_map(body, mesh=mesh, in_specs=in_specs, out_specs=out_specs, check_vma=False)
```

```python
import jax
import jax.numpy as jnp
from jax import lax
from jax.experimental import pallas as pl
from jax.experimental.pallas import tpu as pltpu
from jax.sharding import PartitionSpec as P

VMEM_BYTES = 64 * 1024 * 1024
PIECES = 4
SMALL = pl.CostEstimate(flops=1024, bytes_accessed=1024, transcendentals=0)
BF16 = jnp.bfloat16
F32 = jnp.float32
ROWS = ((0,), (0,))
COLS = ((1,), (1,))
PLAIN = ((1,), (0,))


def dot(left, right, dims):
    return lax.dot_general(left, right, (dims, ((), ())), preferred_element_type=F32)


def like(shape, dtype=BF16):
    return jax.ShapeDtypeStruct(shape, dtype)


def call(kernel, name, outs, scratch, arrays, scalars=()):
    hbm = pl.BlockSpec(memory_space=pltpu.HBM)
    return pl.pallas_call(
        kernel,
        in_specs=[pl.BlockSpec(memory_space=pltpu.SMEM)] * len(scalars) + [hbm] * len(arrays),
        out_specs=[hbm] * len(outs),
        out_shape=outs,
        scratch_shapes=scratch,
        compiler_params=pltpu.CompilerParams(vmem_limit_bytes=VMEM_BYTES),
        cost_estimate=SMALL,
        name=name,
    )(*scalars, *arrays)


class Copies:
    def __init__(self, sems):
        self.sems = sems
        self.used = 0

    def start(self, source, target):
        copy = pltpu.make_async_copy(source, target, self.sems.at[self.used])
        self.used += 1
        copy.start()
        return copy


def wait(copies):
    for copy in copies:
        copy.wait()


def place_kernel(start, cap, ids_ref, tokens_ref, grad_ref, *refs):
    blocks, (ids, data, moved, sems) = refs[:-4], refs[-4:]
    copies = Copies(sems)
    ids_load = copies.start(ids_ref, ids)
    pieces = pieces_of(tokens_ref, grad_ref)
    loads = [copies.start(ref.at[:, there], data.at[:, here]) for ref, there, here in pieces]
    ids_load.wait()
    placing = placing_of(ids[...], len(blocks), start, cap)
    stores = []
    for load, (_, _, here) in zip(loads, pieces):
        load.wait()
        moved[:, here] = dot(placing, data[:, here], PLAIN).astype(BF16)
        stores += store_rows(copies, moved, blocks, here)
    wait(stores)


def pieces_of(first_ref, second_ref):
    width = first_ref.shape[1]
    step = width // (PIECES // 2)
    return [
        (ref, slice(start, start + step), slice(side * width + start, side * width + start + step))
        for side, ref in enumerate((first_ref, second_ref))
        for start in range(0, width, step)
    ]


def placing_of(ids, experts, start, cap):
    rows = ids.shape[1]
    rel = jnp.zeros((1, rows), jnp.int32)
    me = lax.axis_index("exp").astype(jnp.int32)
    for mask in range(1, experts):
        rel = jnp.where(ids == (me ^ mask), round_of(me, mask, experts), rel)
    onehot = lax.broadcasted_iota(jnp.int32, (max(experts, 16), rows), 0) == rel
    before = lax.broadcasted_iota(jnp.int32, (rows, rows), 0) < lax.broadcasted_iota(jnp.int32, (rows, rows), 1)
    ranks = dot(onehot.astype(BF16), before.astype(BF16), PLAIN)
    rank = jnp.sum(jnp.where(onehot, ranks, 0.0), axis=0, keepdims=True).astype(jnp.int32) - start
    target = jnp.where((rank >= 0) & (rank < cap), rel * cap + rank, -1)
    return (lax.broadcasted_iota(jnp.int32, (experts * cap, rows), 0) == target).astype(BF16)


def expert_kernel(*refs):
    count = (len(refs) - 12) // 2
    blocks, (one_ref, two_ref), outs = refs[:count], refs[count : count + 2], refs[count + 2 : 2 * count + 2]
    slot_out, proj_out, hidden_out, slot, one, two, back, proj, hidden, sems = refs[2 * count + 2 :]
    cap = blocks[0].shape[0]
    wide, width = two.shape
    copies = Copies(sems)
    loads = [copies.start(block, slot.at[index * cap : (index + 1) * cap]) for index, block in enumerate(blocks)]
    two_load = copies.start(two_ref, two)
    half = width // 2
    one_loads = [copies.start(one_ref.at[start : start + half], one.at[start : start + half]) for start in (0, half)]
    wait(loads)
    stores = [copies.start(slot, slot_out)]
    two_load.wait()
    grad_hidden = dot(slot[:, width:], two[...], COLS)
    one_loads[0].wait()
    both = dot(slot[:, :half], one[:half], PLAIN)
    one_loads[1].wait()
    both = both + dot(slot[:, half:width], one[half:], PLAIN)
    gate, upper = both[:, :wide], both[:, wide:]
    sigma = 1.0 / (1.0 + jnp.exp(-gate))
    silu = gate * sigma
    hidden[...] = (silu * upper).astype(BF16)
    stores.append(copies.start(hidden, hidden_out))
    proj[...] = jnp.concatenate(
        [grad_hidden * upper * sigma * (1.0 + gate * (1.0 - sigma)), grad_hidden * silu], axis=1
    ).astype(BF16)
    stores.append(copies.start(proj, proj_out))
    back[:, :width] = dot(hidden[...], two[...], PLAIN).astype(BF16)
    stores += store_rows(copies, back, outs, slice(0, width))
    back[:, width:] = dot(proj[...], one[...], COLS).astype(BF16)
    stores += store_rows(copies, back, outs, slice(width, 2 * width))
    wait(stores)


def store_rows(copies, source, outs, here):
    cap = outs[0].shape[0]
    return [copies.start(source.at[index * cap : (index + 1) * cap, here], out.at[:, here]) for index, out in enumerate(outs)]


def weight_kernel(end, parts, pieces, number_ref, *refs):
    sources, refs = refs[: 3 * parts], refs[3 * parts :]
    more, refs = refs[: sum(pieces)], refs[sum(pieces) :]
    results, sems = refs[-3 if end else -2 : -1], refs[-1]
    outs, (x, dy, proj, hidden, received) = refs[: -6 - len(results)], refs[-6 - len(results) : -1 - len(results)]
    share, wide = x.shape[1], hidden.shape[1]
    width = sources[0].shape[1] // 2
    first = pl.multiple_of(number_ref[0] * share, share)
    copies = Copies(sems)
    loads = []
    total = 0
    for part in range(parts):
        slot_ref, proj_ref, hidden_ref = sources[3 * part : 3 * part + 3]
        here = slice(total, total + slot_ref.shape[0])
        total = here.stop
        loads.append(copies.start(slot_ref.at[:, pl.ds(first, share)], x.at[here]))
        loads.append(copies.start(slot_ref.at[:, pl.ds(pl.multiple_of(first + width, share), share)], dy.at[here]))
        loads.append(copies.start(proj_ref, proj.at[here]))
        loads.append(copies.start(hidden_ref, hidden.at[here]))
    more_loads = []
    for index, number in enumerate(pieces):
        row = 0
        for ref in more[:number]:
            more_loads.append(copies.start(ref, received.at[index, row : row + ref.shape[0]]))
            row += ref.shape[0]
        more = more[number:]
    wait(loads)
    wait(more_loads)
    step = min(share, 128)
    stores = []
    for start in range(0, share, step):
        here = slice(start, start + step)
        up = dot(x[:, here], proj[...], ROWS)
        for index in range(len(pieces)):
            up = up + received[index, here, : 2 * wide].astype(F32)
        if end:
            results[0][here] = up
            stores.append(copies.start(results[0].at[here], outs[0].at[here]))
            continue
        down = dot(dy[:, here], hidden[...], ROWS)
        for index in range(len(pieces)):
            down = down + received[index, here, 2 * wide : 3 * wide].astype(F32)
        results[0][here, : 2 * wide] = up.astype(BF16)
        results[0][here, 2 * wide : 3 * wide] = down.astype(BF16)
        row = 0
        for out in outs:
            first_row, last_row = max(row, start), min(row + out.shape[0], start + step)
            if first_row < last_row:
                there = out.at[first_row - row : last_row - row]
                stores.append(copies.start(results[0].at[first_row:last_row], there))
            row += out.shape[0]
    if end:
        down = dot(hidden[...], dy[...], ROWS)
        row = lax.broadcasted_iota(jnp.int32, (share, share), 0)
        unit = (row == lax.broadcasted_iota(jnp.int32, (share, share), 1)).astype(BF16)
        for index in range(len(pieces)):
            down = down + dot(received[index, :, 2 * wide : 3 * wide], unit, ROWS)
        results[1][...] = down
        stores.append(copies.start(results[1], outs[1]))
    wait(stores)


def combine_kernel(start, cap, ids_ref, tokens_ref, grad_ref, *refs):
    blocks, (mixed_out, grad_out, ids, data, back, sems) = refs[:-6], refs[-6:]
    copies = Copies(sems)
    ids_load = copies.start(ids_ref, ids)
    pieces = pieces_of(tokens_ref, grad_ref)
    loads = []
    for ref, there, here in pieces:
        loads.append([copies.start(ref.at[:, there], data.at[:, here])])
        for index, block in enumerate(blocks):
            loads[-1].append(copies.start(block.at[:, here], back.at[index * cap : (index + 1) * cap, here]))
    ids_load.wait()
    placing = placing_of(ids[...], len(blocks), start, cap)
    stores = []
    for load, (_, there, here), (out, _, _) in zip(loads, pieces, pieces_of(mixed_out, grad_out)):
        wait(load)
        data[:, here] = (data[:, here].astype(F32) + dot(placing, back[:, here], ROWS)).astype(BF16)
        stores.append(copies.start(data.at[:, here], out.at[:, there]))
    wait(stores)


def after(value, *earlier):
    if not earlier:
        return value
    return lax.optimization_barrier((value, *earlier))[0]


class Lane:
    def __init__(self, window):
        self.window = window
        self.done = []

    def send(self, value, axis, pairs, *earlier):
        if len(self.done) >= self.window:
            earlier = (self.done[-self.window], *earlier)
        self.done.append(lax.ppermute(after(value, *earlier), axis, pairs))
        return self.done[-1]


def rounds_of(experts):
    rounds = [[0] * experts for _ in range(experts)]
    for place in range(experts):
        for mask in range(experts):
            rounds[round_of(place, mask, experts)][place] = place ^ mask
    return rounds


def round_of(place, mask, experts):
    half = experts // 2
    near = mask % half
    if near == 0:
        return experts - 1 if mask else 0
    units = [unit for unit in range(1, half) if bin(unit & near).count("1") % 2 == 0]
    turn = 0
    for bit in range(half.bit_length() if units else 0):
        if units[0] >> bit & 1:
            turn = turn ^ ((place >> bit) & 1)
    return 2 * near - 1 + (turn if mask >= half else 1 - turn)


def exchange(blocks, rounds, lane, numbers, *earlier):
    moved = []
    for number in numbers:
        more = earlier if number == numbers[-1] else ()
        moved.append(lane.send(blocks[number], "exp", list(enumerate(rounds[number])), *more))
    return moved


def body(tokens, expert_ids, gate_up_weight, down_weight, grad_out):
    rows, width = tokens.shape
    experts = lax.axis_size("exp")
    groups = lax.axis_size("grp")
    capacity = 2 * rows // experts
    first = capacity * 3 // 4
    cuts = [(0, first), (first, capacity - first)] if capacity % 64 == 0 else [(0, capacity)]
    parts = len(cuts)
    weight_one = gate_up_weight[0]
    weight_two = down_weight[0]
    wide = weight_two.shape[0]
    share = width // groups
    sems = pltpu.SemaphoreType.DMA
    ids_here = pltpu.VMEM((1, rows), jnp.int32)

    def halves(cap):
        return [pltpu.VMEM((count, 2 * width), BF16) for count in (rows, experts * cap)]

    lane = Lane(4)
    numbers = range(1, experts)
    ids = expert_ids.reshape(1, rows)
    rounds = rounds_of(experts)
    group = lax.axis_index("grp").astype(jnp.int32)

    def place(start, cap):
        return call(
            lambda *refs: place_kernel(start, cap, *refs),
            "place",
            [like((cap, 2 * width))] * experts,
            [ids_here, *halves(cap), sems((1 + PIECES * (1 + experts),))],
            [ids, tokens, grad_out],
        )

    def expert(blocks):
        slots = experts * blocks[0].shape[0]
        shapes = [(slots, 2 * width), (slots, 2 * wide), (slots, wide)]
        back = [pltpu.VMEM(shape, BF16) for shape in shapes]
        scratch = [back[0], pltpu.VMEM(weight_one.shape, BF16), pltpu.VMEM(weight_two.shape, BF16)]
        outs = call(
            expert_kernel,
            "expert",
            [like(blocks[0].shape)] * experts + [like(shape) for shape in shapes],
            scratch + back + [sems((6 + 3 * experts,))],
            [*blocks, weight_one, weight_two],
        )
        return outs[:experts], outs[experts:]

    def weight_part(number, kept, received, end, heads):
        shape = (share, pl.cdiv(3 * wide, 128) * 128)
        finals = [like((share, 2 * wide), F32), like((wide, share), F32)]
        rows_of = [heads, share - heads] if heads else [share]
        outs = finals if end else [like((count, shape[1])) for count in rows_of]
        total = experts * capacity
        scratch = [pltpu.VMEM((total, width), BF16) for width in (share, share, 2 * wide, wide)]
        scratch.append(pltpu.VMEM((max(1, len(received)), *shape), BF16))
        scratch += [pltpu.VMEM(out.shape, out.dtype) for out in (finals if end else [like(shape)])]
        sources = [array for arrays in kept + received for array in arrays]
        scratch.append(sems((len(sources) + parts + len(outs) + 4 * groups,)))
        pieces = [len(arrays) for arrays in received]
        return call(
            lambda *refs: weight_kernel(end, parts, pieces, *refs),
            "weight_part",
            outs,
            scratch,
            sources,
            scalars=[number[None]],
        )

    def combine(start, cap, first, second, blocks):
        return call(
            lambda *refs: combine_kernel(start, cap, *refs),
            "combine",
            [like((rows, width))] * 2,
            [ids_here, *halves(cap), sems((1 + PIECES * (2 + experts),))],
            [ids, first, second, *blocks],
        )

    sent = [place(*cut) for cut in cuts]
    results = []
    for part in range(parts):
        earlier = [results[-1][0][0]] if results else []
        results.append(expert([sent[part][0]] + exchange(sent[part], rounds, lane, numbers, *earlier)))
    kept = [result[1] for result in results]

    count = len(lane.done)
    mixed, grad = tokens, grad_out
    back = []
    for part in range(parts):
        if back:
            mixed, grad = combine(*cuts[part - 1], mixed, grad, back)
        blocks = results[part][0]
        back = [blocks[0]] + exchange(blocks, rounds, lane, numbers if part < parts - 1 else numbers[:-1])
    done = lane.done[count:]

    received = {q: [] for q in range(groups)}
    sums = kept[0][0]
    held = {groups - 1: done[:2], 2: done[2:4]}
    for q in sorted(range(1, groups), key=lambda q: (q & -q, -q)):
        low = q & -q
        sent = weight_part(group ^ q, [[sums, *kept[0][1:]], *kept[1:]], received[q], False, 16 if q in held else 0)
        sums = after(sums, sent[0])
        pairs = [(i, i ^ low) for i in range(groups)]
        short = Lane(1)
        received[q ^ low].append([short.send(sent[0], "grp", pairs)])
        received[q ^ low][-1] += [short.send(piece, "grp", pairs, *held[q]) for piece in sent[1:]]

    grad_gate_up, grad_down = weight_part(group, [[sums, *kept[0][1:]], *kept[1:]], received[0], True, 0)
    back += exchange(blocks, rounds, lane, numbers[-1:], mixed, lane.done[-3])
    back[0] = after(back[0], grad_gate_up)
    mixed, grad = combine(*cuts[-1], mixed, grad, back)
    return (mixed, grad, grad_gate_up[None], grad_down[None])


def solution(mesh):
    in_specs = (
        P(("grp", "exp"), None),
        P(("grp", "exp"), None),
        P("exp", None, None),
        P("exp", None, None),
        P(("grp", "exp"), None),
    )
    out_specs = (
        P(("grp", "exp"), None),
        P(("grp", "exp"), None),
        P("exp", "grp", None),
        P("exp", None, "grp"),
    )
    return jax.shard_map(body, mesh=mesh, in_specs=in_specs, out_specs=out_specs, check_vma=False)
```

```python
import jax
import jax.numpy as jnp
from jax import lax
from jax.experimental import pallas as pl
from jax.experimental.pallas import tpu as pltpu
from jax.sharding import PartitionSpec as P

VMEM_BYTES = 64 * 1024 * 1024
PIECES = 4
SMALL = pl.CostEstimate(flops=1024, bytes_accessed=1024, transcendentals=0)
BF16 = jnp.bfloat16
F32 = jnp.float32
ROWS = ((0,), (0,))
COLS = ((1,), (1,))
PLAIN = ((1,), (0,))


def dot(left, right, dims):
    return lax.dot_general(left, right, (dims, ((), ())), preferred_element_type=F32)


def like(shape, dtype=BF16):
    return jax.ShapeDtypeStruct(shape, dtype)


def call(kernel, name, outs, scratch, arrays, scalars=()):
    hbm = pl.BlockSpec(memory_space=pltpu.HBM)
    return pl.pallas_call(
        kernel,
        in_specs=[pl.BlockSpec(memory_space=pltpu.SMEM)] * len(scalars) + [hbm] * len(arrays),
        out_specs=[hbm] * len(outs),
        out_shape=outs,
        scratch_shapes=scratch,
        compiler_params=pltpu.CompilerParams(vmem_limit_bytes=VMEM_BYTES),
        cost_estimate=SMALL,
        name=name,
    )(*scalars, *arrays)


class Copies:
    def __init__(self, sems):
        self.sems = sems
        self.used = 0

    def start(self, source, target):
        copy = pltpu.make_async_copy(source, target, self.sems.at[self.used])
        self.used += 1
        copy.start()
        return copy


def wait(copies):
    for copy in copies:
        copy.wait()


def place_kernel(start, cap, ids_ref, tokens_ref, grad_ref, *refs):
    blocks, (ids, data, moved, sems) = refs[:-4], refs[-4:]
    copies = Copies(sems)
    ids_load = copies.start(ids_ref, ids)
    pieces = pieces_of(tokens_ref, grad_ref)
    loads = [copies.start(ref.at[:, there], data.at[:, here]) for ref, there, here in pieces]
    ids_load.wait()
    placing = placing_of(ids[...], len(blocks), start, cap)
    stores = []
    for load, (_, _, here) in zip(loads, pieces):
        load.wait()
        moved[:, here] = dot(placing, data[:, here], PLAIN).astype(BF16)
        stores += store_rows(copies, moved, blocks, here)
    wait(stores)


def pieces_of(first_ref, second_ref):
    width = first_ref.shape[1]
    step = width // (PIECES // 2)
    return [
        (ref, slice(start, start + step), slice(side * width + start, side * width + start + step))
        for side, ref in enumerate((first_ref, second_ref))
        for start in range(0, width, step)
    ]


def placing_of(ids, experts, start, cap):
    rows = ids.shape[1]
    rel = jnp.zeros((1, rows), jnp.int32)
    me = lax.axis_index("exp").astype(jnp.int32)
    for mask in range(1, experts):
        rel = jnp.where(ids == (me ^ mask), round_of(me, mask, experts), rel)
    onehot = lax.broadcasted_iota(jnp.int32, (max(experts, 16), rows), 0) == rel
    before = lax.broadcasted_iota(jnp.int32, (rows, rows), 0) < lax.broadcasted_iota(jnp.int32, (rows, rows), 1)
    ranks = dot(onehot.astype(BF16), before.astype(BF16), PLAIN)
    rank = jnp.sum(jnp.where(onehot, ranks, 0.0), axis=0, keepdims=True).astype(jnp.int32) - start
    target = jnp.where((rank >= 0) & (rank < cap), rel * cap + rank, -1)
    return (lax.broadcasted_iota(jnp.int32, (experts * cap, rows), 0) == target).astype(BF16)


def expert_kernel(*refs):
    count = (len(refs) - 12) // 2
    blocks, (one_ref, two_ref), outs = refs[:count], refs[count : count + 2], refs[count + 2 : 2 * count + 2]
    slot_out, proj_out, hidden_out, slot, one, two, back, proj, hidden, sems = refs[2 * count + 2 :]
    cap = blocks[0].shape[0]
    wide, width = two.shape
    copies = Copies(sems)
    loads = [copies.start(block, slot.at[index * cap : (index + 1) * cap]) for index, block in enumerate(blocks)]
    two_load = copies.start(two_ref, two)
    half = width // 2
    one_loads = [copies.start(one_ref.at[start : start + half], one.at[start : start + half]) for start in (0, half)]
    wait(loads)
    stores = [copies.start(slot, slot_out)]
    two_load.wait()
    grad_hidden = dot(slot[:, width:], two[...], COLS)
    one_loads[0].wait()
    both = dot(slot[:, :half], one[:half], PLAIN)
    one_loads[1].wait()
    both = both + dot(slot[:, half:width], one[half:], PLAIN)
    gate, upper = both[:, :wide], both[:, wide:]
    sigma = 1.0 / (1.0 + jnp.exp(-gate))
    silu = gate * sigma
    hidden[...] = (silu * upper).astype(BF16)
    stores.append(copies.start(hidden, hidden_out))
    proj[...] = jnp.concatenate(
        [grad_hidden * upper * sigma * (1.0 + gate * (1.0 - sigma)), grad_hidden * silu], axis=1
    ).astype(BF16)
    stores.append(copies.start(proj, proj_out))
    back[:, :width] = dot(hidden[...], two[...], PLAIN).astype(BF16)
    stores += store_rows(copies, back, outs, slice(0, width))
    back[:, width:] = dot(proj[...], one[...], COLS).astype(BF16)
    stores += store_rows(copies, back, outs, slice(width, 2 * width))
    wait(stores)


def store_rows(copies, source, outs, here):
    cap = outs[0].shape[0]
    return [copies.start(source.at[index * cap : (index + 1) * cap, here], out.at[:, here]) for index, out in enumerate(outs)]


def weight_kernel(end, parts, pieces, number_ref, *refs):
    sources, refs = refs[: 3 * parts], refs[3 * parts :]
    more, refs = refs[: sum(pieces)], refs[sum(pieces) :]
    results, sems = refs[-3 if end else -2 : -1], refs[-1]
    outs, (x, dy, proj, hidden, received) = refs[: -6 - len(results)], refs[-6 - len(results) : -1 - len(results)]
    share, wide = x.shape[1], hidden.shape[1]
    width = sources[0].shape[1] // 2
    first = pl.multiple_of(number_ref[0] * share, share)
    copies = Copies(sems)
    loads = []
    total = 0
    for part in range(parts):
        slot_ref, proj_ref, hidden_ref = sources[3 * part : 3 * part + 3]
        here = slice(total, total + slot_ref.shape[0])
        total = here.stop
        loads.append(copies.start(slot_ref.at[:, pl.ds(first, share)], x.at[here]))
        loads.append(copies.start(slot_ref.at[:, pl.ds(pl.multiple_of(first + width, share), share)], dy.at[here]))
        loads.append(copies.start(proj_ref, proj.at[here]))
        loads.append(copies.start(hidden_ref, hidden.at[here]))
    more_loads = []
    for index, number in enumerate(pieces):
        row = 0
        for ref in more[:number]:
            more_loads.append(copies.start(ref, received.at[index, row : row + ref.shape[0]]))
            row += ref.shape[0]
        more = more[number:]
    wait(loads)
    wait(more_loads)
    step = min(share, 128)
    stores = []
    for start in range(0, share, step):
        here = slice(start, start + step)
        up = dot(x[:, here], proj[...], ROWS)
        for index in range(len(pieces)):
            up = up + received[index, here, : 2 * wide].astype(F32)
        if end:
            results[0][here] = up
            stores.append(copies.start(results[0].at[here], outs[0].at[here]))
            continue
        down = dot(dy[:, here], hidden[...], ROWS)
        for index in range(len(pieces)):
            down = down + received[index, here, 2 * wide : 3 * wide].astype(F32)
        results[0][here, : 2 * wide] = up.astype(BF16)
        results[0][here, 2 * wide : 3 * wide] = down.astype(BF16)
        row = 0
        for out in outs:
            first_row, last_row = max(row, start), min(row + out.shape[0], start + step)
            if first_row < last_row:
                there = out.at[first_row - row : last_row - row]
                stores.append(copies.start(results[0].at[first_row:last_row], there))
            row += out.shape[0]
    if end:
        down = dot(hidden[...], dy[...], ROWS)
        row = lax.broadcasted_iota(jnp.int32, (share, share), 0)
        unit = (row == lax.broadcasted_iota(jnp.int32, (share, share), 1)).astype(BF16)
        for index in range(len(pieces)):
            down = down + dot(received[index, :, 2 * wide : 3 * wide], unit, ROWS)
        results[1][...] = down
        stores.append(copies.start(results[1], outs[1]))
    wait(stores)


def combine_kernel(start, cap, ids_ref, tokens_ref, grad_ref, *refs):
    blocks, (mixed_out, grad_out, ids, data, back, sems) = refs[:-6], refs[-6:]
    copies = Copies(sems)
    ids_load = copies.start(ids_ref, ids)
    pieces = pieces_of(tokens_ref, grad_ref)
    loads = []
    for ref, there, here in pieces:
        loads.append([copies.start(ref.at[:, there], data.at[:, here])])
        for index, block in enumerate(blocks):
            loads[-1].append(copies.start(block.at[:, here], back.at[index * cap : (index + 1) * cap, here]))
    ids_load.wait()
    placing = placing_of(ids[...], len(blocks), start, cap)
    stores = []
    for load, (_, there, here), (out, _, _) in zip(loads, pieces, pieces_of(mixed_out, grad_out)):
        wait(load)
        data[:, here] = (data[:, here].astype(F32) + dot(placing, back[:, here], ROWS)).astype(BF16)
        stores.append(copies.start(data.at[:, here], out.at[:, there]))
    wait(stores)


def after(value, *earlier):
    if not earlier:
        return value
    return lax.optimization_barrier((value, *earlier))[0]


class Lane:
    def __init__(self, window):
        self.window = window
        self.done = []

    def send(self, value, axis, pairs, *earlier):
        if len(self.done) >= self.window:
            earlier = (self.done[-self.window], *earlier)
        self.done.append(lax.ppermute(after(value, *earlier), axis, pairs))
        return self.done[-1]


def rounds_of(experts):
    rounds = [[0] * experts for _ in range(experts)]
    for place in range(experts):
        for mask in range(experts):
            rounds[round_of(place, mask, experts)][place] = place ^ mask
    return rounds


def round_of(place, mask, experts):
    half = experts // 2
    near = mask % half
    if near == 0:
        return experts - 1 if mask else 0
    units = [unit for unit in range(1, half) if bin(unit & near).count("1") % 2 == 0]
    turn = 0
    for bit in range(half.bit_length() if units else 0):
        if units[0] >> bit & 1:
            turn = turn ^ ((place >> bit) & 1)
    return 2 * near - 1 + (turn if mask >= half else 1 - turn)


def exchange(blocks, rounds, lane, numbers, *earlier):
    moved = []
    for number in numbers:
        more = earlier if number == numbers[-1] else ()
        moved.append(lane.send(blocks[number], "exp", list(enumerate(rounds[number])), *more))
    return moved


def body(tokens, expert_ids, gate_up_weight, down_weight, grad_out):
    rows, width = tokens.shape
    experts = lax.axis_size("exp")
    groups = lax.axis_size("grp")
    capacity = 2 * rows // experts
    parts = 2 if capacity % 32 == 0 else 1
    cuts = [(part * capacity // parts, capacity // parts) for part in range(parts)]
    weight_one = gate_up_weight[0]
    weight_two = down_weight[0]
    wide = weight_two.shape[0]
    share = width // groups
    sems = pltpu.SemaphoreType.DMA
    ids_here = pltpu.VMEM((1, rows), jnp.int32)

    def halves(cap):
        return [pltpu.VMEM((count, 2 * width), BF16) for count in (rows, experts * cap)]

    lane = Lane(4)
    numbers = range(1, experts)
    ids = expert_ids.reshape(1, rows)
    rounds = rounds_of(experts)
    group = lax.axis_index("grp").astype(jnp.int32)

    def place(start, cap):
        return call(
            lambda *refs: place_kernel(start, cap, *refs),
            "place",
            [like((cap, 2 * width))] * experts,
            [ids_here, *halves(cap), sems((1 + PIECES * (1 + experts),))],
            [ids, tokens, grad_out],
        )

    def expert(blocks):
        slots = experts * blocks[0].shape[0]
        shapes = [(slots, 2 * width), (slots, 2 * wide), (slots, wide)]
        back = [pltpu.VMEM(shape, BF16) for shape in shapes]
        scratch = [back[0], pltpu.VMEM(weight_one.shape, BF16), pltpu.VMEM(weight_two.shape, BF16)]
        outs = call(
            expert_kernel,
            "expert",
            [like(blocks[0].shape)] * experts + [like(shape) for shape in shapes],
            scratch + back + [sems((6 + 3 * experts,))],
            [*blocks, weight_one, weight_two],
        )
        return outs[:experts], outs[experts:]

    def weight_part(number, kept, received, end, heads):
        shape = (share, pl.cdiv(3 * wide, 128) * 128)
        finals = [like((share, 2 * wide), F32), like((wide, share), F32)]
        rows_of = [heads, share - heads] if heads else [share]
        outs = finals if end else [like((count, shape[1])) for count in rows_of]
        total = experts * capacity
        scratch = [pltpu.VMEM((total, width), BF16) for width in (share, share, 2 * wide, wide)]
        scratch.append(pltpu.VMEM((max(1, len(received)), *shape), BF16))
        scratch += [pltpu.VMEM(out.shape, out.dtype) for out in (finals if end else [like(shape)])]
        sources = [array for arrays in kept + received for array in arrays]
        scratch.append(sems((len(sources) + parts + len(outs) + 4 * groups,)))
        pieces = [len(arrays) for arrays in received]
        return call(
            lambda *refs: weight_kernel(end, parts, pieces, *refs),
            "weight_part",
            outs,
            scratch,
            sources,
            scalars=[number[None]],
        )

    def combine(start, cap, first, second, blocks):
        return call(
            lambda *refs: combine_kernel(start, cap, *refs),
            "combine",
            [like((rows, width))] * 2,
            [ids_here, *halves(cap), sems((1 + PIECES * (2 + experts),))],
            [ids, first, second, *blocks],
        )

    sent = [place(*cut) for cut in cuts]
    results = []
    for part in range(parts):
        earlier = [results[-1][0][0]] if results else []
        results.append(expert([sent[part][0]] + exchange(sent[part], rounds, lane, numbers, *earlier)))
    kept = [result[1] for result in results]

    count = len(lane.done)
    mixed, grad = tokens, grad_out
    back = []
    for part in range(parts):
        if back:
            mixed, grad = combine(*cuts[part - 1], mixed, grad, back)
        blocks = results[part][0]
        back = [blocks[0]] + exchange(blocks, rounds, lane, numbers if part < parts - 1 else numbers[:-1])
    done = lane.done[count:]

    received = {q: [] for q in range(groups)}
    sums = kept[0][0]
    held = {groups - 1: done[:5], 2: done[5:7]}
    for q in sorted(range(1, groups), key=lambda q: (q & -q, -q)):
        low = q & -q
        sent = weight_part(group ^ q, [[sums, *kept[0][1:]], *kept[1:]], received[q], False, 16 if q in held else 0)
        sums = after(sums, sent[0])
        pairs = [(i, i ^ low) for i in range(groups)]
        short = Lane(1)
        received[q ^ low].append([short.send(sent[0], "grp", pairs)])
        received[q ^ low][-1] += [short.send(piece, "grp", pairs, *held[q]) for piece in sent[1:]]

    grad_gate_up, grad_down = weight_part(group, [[sums, *kept[0][1:]], *kept[1:]], received[0], True, 0)
    back += exchange(blocks, rounds, lane, numbers[-1:], mixed, lane.done[-3])
    back[0] = after(back[0], grad_gate_up)
    mixed, grad = combine(*cuts[-1], mixed, grad, back)
    return (mixed, grad, grad_gate_up[None], grad_down[None])


def solution(mesh):
    in_specs = (
        P(("grp", "exp"), None),
        P(("grp", "exp"), None),
        P("exp", None, None),
        P("exp", None, None),
        P(("grp", "exp"), None),
    )
    out_specs = (
        P(("grp", "exp"), None),
        P(("grp", "exp"), None),
        P("exp", "grp", None),
        P("exp", None, "grp"),
    )
    return jax.shard_map(body, mesh=mesh, in_specs=in_specs, out_specs=out_specs, check_vma=False)
```

```python
import jax
import jax.numpy as jnp
from jax import lax
from jax.experimental import pallas as pl
from jax.experimental.pallas import tpu as pltpu
from jax.sharding import PartitionSpec as P

VMEM_BYTES = 64 * 1024 * 1024
PIECES = 4
SMALL = pl.CostEstimate(flops=1024, bytes_accessed=1024, transcendentals=0)
BF16 = jnp.bfloat16
F32 = jnp.float32
ROWS = ((0,), (0,))
COLS = ((1,), (1,))
PLAIN = ((1,), (0,))


def dot(left, right, dims):
    return lax.dot_general(left, right, (dims, ((), ())), preferred_element_type=F32)


def like(shape, dtype=BF16):
    return jax.ShapeDtypeStruct(shape, dtype)


def call(kernel, name, outs, scratch, arrays, scalars=()):
    hbm = pl.BlockSpec(memory_space=pltpu.HBM)
    return pl.pallas_call(
        kernel,
        in_specs=[pl.BlockSpec(memory_space=pltpu.SMEM)] * len(scalars) + [hbm] * len(arrays),
        out_specs=[hbm] * len(outs),
        out_shape=outs,
        scratch_shapes=scratch,
        compiler_params=pltpu.CompilerParams(vmem_limit_bytes=VMEM_BYTES),
        cost_estimate=SMALL,
        name=name,
    )(*scalars, *arrays)


class Copies:
    def __init__(self, sems):
        self.sems = sems
        self.used = 0

    def start(self, source, target):
        copy = pltpu.make_async_copy(source, target, self.sems.at[self.used])
        self.used += 1
        copy.start()
        return copy


def wait(copies):
    for copy in copies:
        copy.wait()


def place_kernel(start, cap, ids_ref, tokens_ref, grad_ref, *refs):
    blocks, (ids, data, moved, sems) = refs[:-4], refs[-4:]
    copies = Copies(sems)
    ids_load = copies.start(ids_ref, ids)
    pieces = pieces_of(tokens_ref, grad_ref)
    loads = [copies.start(ref.at[:, there], data.at[:, here]) for ref, there, here in pieces]
    ids_load.wait()
    placing = placing_of(ids[...], len(blocks), start, cap)
    stores = []
    for load, (_, _, here) in zip(loads, pieces):
        load.wait()
        moved[:, here] = dot(placing, data[:, here], PLAIN).astype(BF16)
        stores += store_rows(copies, moved, blocks, here)
    wait(stores)


def pieces_of(first_ref, second_ref):
    width = first_ref.shape[1]
    step = width // (PIECES // 2)
    return [
        (ref, slice(start, start + step), slice(side * width + start, side * width + start + step))
        for side, ref in enumerate((first_ref, second_ref))
        for start in range(0, width, step)
    ]


def placing_of(ids, experts, start, cap):
    rows = ids.shape[1]
    rel = jnp.zeros((1, rows), jnp.int32)
    me = lax.axis_index("exp").astype(jnp.int32)
    for mask in range(1, experts):
        rel = jnp.where(ids == (me ^ mask), round_of(me, mask, experts), rel)
    onehot = lax.broadcasted_iota(jnp.int32, (max(experts, 16), rows), 0) == rel
    before = lax.broadcasted_iota(jnp.int32, (rows, rows), 0) < lax.broadcasted_iota(jnp.int32, (rows, rows), 1)
    ranks = dot(onehot.astype(BF16), before.astype(BF16), PLAIN)
    rank = jnp.sum(jnp.where(onehot, ranks, 0.0), axis=0, keepdims=True).astype(jnp.int32) - start
    target = jnp.where((rank >= 0) & (rank < cap), rel * cap + rank, -1)
    return (lax.broadcasted_iota(jnp.int32, (experts * cap, rows), 0) == target).astype(BF16)


def expert_kernel(*refs):
    count = (len(refs) - 12) // 2
    blocks, (one_ref, two_ref), outs = refs[:count], refs[count : count + 2], refs[count + 2 : 2 * count + 2]
    slot_out, proj_out, hidden_out, slot, one, two, back, proj, hidden, sems = refs[2 * count + 2 :]
    cap = blocks[0].shape[0]
    wide, width = two.shape
    copies = Copies(sems)
    loads = [copies.start(block, slot.at[index * cap : (index + 1) * cap]) for index, block in enumerate(blocks)]
    two_load = copies.start(two_ref, two)
    half = width // 2
    one_loads = [copies.start(one_ref.at[start : start + half], one.at[start : start + half]) for start in (0, half)]
    wait(loads)
    stores = [copies.start(slot, slot_out)]
    two_load.wait()
    grad_hidden = dot(slot[:, width:], two[...], COLS)
    one_loads[0].wait()
    both = dot(slot[:, :half], one[:half], PLAIN)
    one_loads[1].wait()
    both = both + dot(slot[:, half:width], one[half:], PLAIN)
    gate, upper = both[:, :wide], both[:, wide:]
    sigma = 1.0 / (1.0 + jnp.exp(-gate))
    silu = gate * sigma
    hidden[...] = (silu * upper).astype(BF16)
    stores.append(copies.start(hidden, hidden_out))
    proj[...] = jnp.concatenate(
        [grad_hidden * upper * sigma * (1.0 + gate * (1.0 - sigma)), grad_hidden * silu], axis=1
    ).astype(BF16)
    stores.append(copies.start(proj, proj_out))
    back[:, :width] = dot(hidden[...], two[...], PLAIN).astype(BF16)
    stores += store_rows(copies, back, outs, slice(0, width))
    back[:, width:] = dot(proj[...], one[...], COLS).astype(BF16)
    stores += store_rows(copies, back, outs, slice(width, 2 * width))
    wait(stores)


def store_rows(copies, source, outs, here):
    cap = outs[0].shape[0]
    return [copies.start(source.at[index * cap : (index + 1) * cap, here], out.at[:, here]) for index, out in enumerate(outs)]


def weight_kernel(end, parts, pieces, number_ref, *refs):
    sources, refs = refs[: 3 * parts], refs[3 * parts :]
    more, refs = refs[: sum(pieces)], refs[sum(pieces) :]
    results, sems = refs[-3 if end else -2 : -1], refs[-1]
    outs, (x, dy, proj, hidden, received) = refs[: -6 - len(results)], refs[-6 - len(results) : -1 - len(results)]
    share, wide = x.shape[1], hidden.shape[1]
    width = sources[0].shape[1] // 2
    first = pl.multiple_of(number_ref[0] * share, share)
    copies = Copies(sems)
    loads = []
    total = 0
    for part in range(parts):
        slot_ref, proj_ref, hidden_ref = sources[3 * part : 3 * part + 3]
        here = slice(total, total + slot_ref.shape[0])
        total = here.stop
        loads.append(copies.start(slot_ref.at[:, pl.ds(first, share)], x.at[here]))
        loads.append(copies.start(slot_ref.at[:, pl.ds(pl.multiple_of(first + width, share), share)], dy.at[here]))
        loads.append(copies.start(proj_ref, proj.at[here]))
        loads.append(copies.start(hidden_ref, hidden.at[here]))
    more_loads = []
    for index, number in enumerate(pieces):
        row = 0
        for ref in more[:number]:
            more_loads.append(copies.start(ref, received.at[index, row : row + ref.shape[0]]))
            row += ref.shape[0]
        more = more[number:]
    wait(loads)
    wait(more_loads)
    step = min(share, 128)
    stores = []
    for start in range(0, share, step):
        here = slice(start, start + step)
        up = dot(x[:, here], proj[...], ROWS)
        for index in range(len(pieces)):
            up = up + received[index, here, : 2 * wide].astype(F32)
        if end:
            results[0][here] = up
            stores.append(copies.start(results[0].at[here], outs[0].at[here]))
            continue
        down = dot(dy[:, here], hidden[...], ROWS)
        for index in range(len(pieces)):
            down = down + received[index, here, 2 * wide : 3 * wide].astype(F32)
        results[0][here, : 2 * wide] = up.astype(BF16)
        results[0][here, 2 * wide : 3 * wide] = down.astype(BF16)
        row = 0
        for out in outs:
            first_row, last_row = max(row, start), min(row + out.shape[0], start + step)
            if first_row < last_row:
                there = out.at[first_row - row : last_row - row]
                stores.append(copies.start(results[0].at[first_row:last_row], there))
            row += out.shape[0]
    if end:
        down = dot(hidden[...], dy[...], ROWS)
        row = lax.broadcasted_iota(jnp.int32, (share, share), 0)
        unit = (row == lax.broadcasted_iota(jnp.int32, (share, share), 1)).astype(BF16)
        for index in range(len(pieces)):
            down = down + dot(received[index, :, 2 * wide : 3 * wide], unit, ROWS)
        results[1][...] = down
        stores.append(copies.start(results[1], outs[1]))
    wait(stores)


def combine_kernel(start, cap, ids_ref, tokens_ref, grad_ref, *refs):
    blocks, (mixed_out, grad_out, ids, data, back, sems) = refs[:-6], refs[-6:]
    copies = Copies(sems)
    ids_load = copies.start(ids_ref, ids)
    pieces = pieces_of(tokens_ref, grad_ref)
    loads = []
    for ref, there, here in pieces:
        loads.append([copies.start(ref.at[:, there], data.at[:, here])])
        for index, block in enumerate(blocks):
            loads[-1].append(copies.start(block.at[:, here], back.at[index * cap : (index + 1) * cap, here]))
    ids_load.wait()
    placing = placing_of(ids[...], len(blocks), start, cap)
    stores = []
    for load, (_, there, here), (out, _, _) in zip(loads, pieces, pieces_of(mixed_out, grad_out)):
        wait(load)
        data[:, here] = (data[:, here].astype(F32) + dot(placing, back[:, here], ROWS)).astype(BF16)
        stores.append(copies.start(data.at[:, here], out.at[:, there]))
    wait(stores)


def after(value, *earlier):
    if not earlier:
        return value
    return lax.optimization_barrier((value, *earlier))[0]


class Lane:
    def __init__(self, window):
        self.window = window
        self.done = []

    def send(self, value, axis, pairs, *earlier):
        if len(self.done) >= self.window:
            earlier = (self.done[-self.window], *earlier)
        self.done.append(lax.ppermute(after(value, *earlier), axis, pairs))
        return self.done[-1]


def rounds_of(experts):
    rounds = [[0] * experts for _ in range(experts)]
    for place in range(experts):
        for mask in range(experts):
            rounds[round_of(place, mask, experts)][place] = place ^ mask
    return rounds


def round_of(place, mask, experts):
    half = experts // 2
    near = mask % half
    if near == 0:
        return experts - 1 if mask else 0
    units = [unit for unit in range(1, half) if bin(unit & near).count("1") % 2 == 0]
    turn = 0
    for bit in range(half.bit_length() if units else 0):
        if units[0] >> bit & 1:
            turn = turn ^ ((place >> bit) & 1)
    return 2 * near - 1 + (turn if mask >= half else 1 - turn)


def exchange(blocks, rounds, lane, numbers, *earlier):
    moved = []
    for number in numbers:
        more = earlier if number == numbers[-1] else ()
        moved.append(lane.send(blocks[number], "exp", list(enumerate(rounds[number])), *more))
    return moved


def body(tokens, expert_ids, gate_up_weight, down_weight, grad_out):
    rows, width = tokens.shape
    experts = lax.axis_size("exp")
    groups = lax.axis_size("grp")
    capacity = 2 * rows // experts
    parts = 2 if capacity % 32 == 0 else 1
    cuts = [(part * capacity // parts, capacity // parts) for part in range(parts)]
    weight_one = gate_up_weight[0]
    weight_two = down_weight[0]
    wide = weight_two.shape[0]
    share = width // groups
    sems = pltpu.SemaphoreType.DMA
    ids_here = pltpu.VMEM((1, rows), jnp.int32)

    def halves(cap):
        return [pltpu.VMEM((count, 2 * width), BF16) for count in (rows, experts * cap)]

    lane = Lane(4)
    numbers = range(1, experts)
    ids = expert_ids.reshape(1, rows)
    rounds = rounds_of(experts)
    group = lax.axis_index("grp").astype(jnp.int32)

    def place(start, cap):
        return call(
            lambda *refs: place_kernel(start, cap, *refs),
            "place",
            [like((cap, 2 * width))] * experts,
            [ids_here, *halves(cap), sems((1 + PIECES * (1 + experts),))],
            [ids, tokens, grad_out],
        )

    def expert(blocks):
        slots = experts * blocks[0].shape[0]
        shapes = [(slots, 2 * width), (slots, 2 * wide), (slots, wide)]
        back = [pltpu.VMEM(shape, BF16) for shape in shapes]
        scratch = [back[0], pltpu.VMEM(weight_one.shape, BF16), pltpu.VMEM(weight_two.shape, BF16)]
        outs = call(
            expert_kernel,
            "expert",
            [like(blocks[0].shape)] * experts + [like(shape) for shape in shapes],
            scratch + back + [sems((6 + 3 * experts,))],
            [*blocks, weight_one, weight_two],
        )
        return outs[:experts], outs[experts:]

    def weight_part(number, kept, received, end, heads):
        shape = (share, pl.cdiv(3 * wide, 128) * 128)
        finals = [like((share, 2 * wide), F32), like((wide, share), F32)]
        rows_of = [heads, share - heads] if heads else [share]
        outs = finals if end else [like((count, shape[1])) for count in rows_of]
        total = experts * capacity
        scratch = [pltpu.VMEM((total, width), BF16) for width in (share, share, 2 * wide, wide)]
        scratch.append(pltpu.VMEM((max(1, len(received)), *shape), BF16))
        scratch += [pltpu.VMEM(out.shape, out.dtype) for out in (finals if end else [like(shape)])]
        sources = [array for arrays in kept + received for array in arrays]
        scratch.append(sems((len(sources) + parts + len(outs) + 4 * groups,)))
        pieces = [len(arrays) for arrays in received]
        return call(
            lambda *refs: weight_kernel(end, parts, pieces, *refs),
            "weight_part",
            outs,
            scratch,
            sources,
            scalars=[number[None]],
        )

    def combine(start, cap, first, second, blocks):
        return call(
            lambda *refs: combine_kernel(start, cap, *refs),
            "combine",
            [like((rows, width))] * 2,
            [ids_here, *halves(cap), sems((1 + PIECES * (2 + experts),))],
            [ids, first, second, *blocks],
        )

    sent = [place(*cut) for cut in cuts]
    results = []
    for part in range(parts):
        earlier = [results[-1][0][0]] if results else []
        results.append(expert([sent[part][0]] + exchange(sent[part], rounds, lane, numbers, *earlier)))
    kept = [result[1] for result in results]

    count = len(lane.done)
    mixed, grad = tokens, grad_out
    back = []
    for part in range(parts):
        if back:
            mixed, grad = combine(*cuts[part - 1], mixed, grad, back)
        blocks = results[part][0]
        lane.window = 4 if part else 5
        back = [blocks[0]] + exchange(blocks, rounds, lane, numbers if part < parts - 1 else numbers[:-1])
    done = lane.done[count:]

    received = {q: [] for q in range(groups)}
    sums = kept[0][0]
    held = {groups - 1: done[:4], 2: done[4:6]}
    for q in sorted(range(1, groups), key=lambda q: (q & -q, -q)):
        low = q & -q
        sent = weight_part(group ^ q, [[sums, *kept[0][1:]], *kept[1:]], received[q], False, 16 if q in held else 0)
        sums = after(sums, sent[0])
        pairs = [(i, i ^ low) for i in range(groups)]
        short = Lane(1)
        received[q ^ low].append([short.send(sent[0], "grp", pairs)])
        received[q ^ low][-1] += [short.send(piece, "grp", pairs, *held[q]) for piece in sent[1:]]

    grad_gate_up, grad_down = weight_part(group, [[sums, *kept[0][1:]], *kept[1:]], received[0], True, 0)
    back += exchange(blocks, rounds, lane, numbers[-1:], mixed, lane.done[-3])
    back[0] = after(back[0], grad_gate_up)
    mixed, grad = combine(*cuts[-1], mixed, grad, back)
    return (mixed, grad, grad_gate_up[None], grad_down[None])


def solution(mesh):
    in_specs = (
        P(("grp", "exp"), None),
        P(("grp", "exp"), None),
        P("exp", None, None),
        P("exp", None, None),
        P(("grp", "exp"), None),
    )
    out_specs = (
        P(("grp", "exp"), None),
        P(("grp", "exp"), None),
        P("exp", "grp", None),
        P("exp", None, "grp"),
    )
    return jax.shard_map(body, mesh=mesh, in_specs=in_specs, out_specs=out_specs, check_vma=False)
```

```python
import jax
import jax.numpy as jnp
from jax import lax
from jax.experimental import pallas as pl
from jax.experimental.pallas import tpu as pltpu
from jax.sharding import PartitionSpec as P

VMEM_BYTES = 64 * 1024 * 1024
PIECES = 4
SMALL = pl.CostEstimate(flops=1024, bytes_accessed=1024, transcendentals=0)
BF16 = jnp.bfloat16
F32 = jnp.float32
ROWS = ((0,), (0,))
COLS = ((1,), (1,))
PLAIN = ((1,), (0,))


def dot(left, right, dims):
    return lax.dot_general(left, right, (dims, ((), ())), preferred_element_type=F32)


def like(shape, dtype=BF16):
    return jax.ShapeDtypeStruct(shape, dtype)


def call(kernel, name, outs, scratch, arrays, scalars=()):
    hbm = pl.BlockSpec(memory_space=pltpu.HBM)
    return pl.pallas_call(
        kernel,
        in_specs=[pl.BlockSpec(memory_space=pltpu.SMEM)] * len(scalars) + [hbm] * len(arrays),
        out_specs=[hbm] * len(outs),
        out_shape=outs,
        scratch_shapes=scratch,
        compiler_params=pltpu.CompilerParams(vmem_limit_bytes=VMEM_BYTES),
        cost_estimate=SMALL,
        name=name,
    )(*scalars, *arrays)


class Copies:
    def __init__(self, sems):
        self.sems = sems
        self.used = 0

    def start(self, source, target):
        copy = pltpu.make_async_copy(source, target, self.sems.at[self.used])
        self.used += 1
        copy.start()
        return copy


def wait(copies):
    for copy in copies:
        copy.wait()


def place_kernel(start, cap, ids_ref, tokens_ref, grad_ref, *refs):
    blocks, (ids, data, moved, sems) = refs[:-4], refs[-4:]
    copies = Copies(sems)
    ids_load = copies.start(ids_ref, ids)
    pieces = pieces_of(tokens_ref, grad_ref)
    loads = [copies.start(ref.at[:, there], data.at[:, here]) for ref, there, here in pieces]
    ids_load.wait()
    placing = placing_of(ids[...], len(blocks), start, cap)
    stores = []
    for load, (_, _, here) in zip(loads, pieces):
        load.wait()
        moved[:, here] = dot(placing, data[:, here], PLAIN).astype(BF16)
        stores += store_rows(copies, moved, blocks, here)
    wait(stores)


def pieces_of(first_ref, second_ref):
    width = first_ref.shape[1]
    step = width // (PIECES // 2)
    return [
        (ref, slice(start, start + step), slice(side * width + start, side * width + start + step))
        for side, ref in enumerate((first_ref, second_ref))
        for start in range(0, width, step)
    ]


def placing_of(ids, experts, start, cap):
    rows = ids.shape[1]
    rel = jnp.zeros((1, rows), jnp.int32)
    me = lax.axis_index("exp").astype(jnp.int32)
    for mask in range(1, experts):
        rel = jnp.where(ids == (me ^ mask), round_of(me, mask, experts), rel)
    onehot = lax.broadcasted_iota(jnp.int32, (max(experts, 16), rows), 0) == rel
    before = lax.broadcasted_iota(jnp.int32, (rows, rows), 0) < lax.broadcasted_iota(jnp.int32, (rows, rows), 1)
    ranks = dot(onehot.astype(BF16), before.astype(BF16), PLAIN)
    rank = jnp.sum(jnp.where(onehot, ranks, 0.0), axis=0, keepdims=True).astype(jnp.int32) - start
    target = jnp.where((rank >= 0) & (rank < cap), rel * cap + rank, -1)
    return (lax.broadcasted_iota(jnp.int32, (experts * cap, rows), 0) == target).astype(BF16)


def expert_kernel(*refs):
    count = (len(refs) - 12) // 2
    blocks, (one_ref, two_ref), outs = refs[:count], refs[count : count + 2], refs[count + 2 : 2 * count + 2]
    slot_out, proj_out, hidden_out, slot, one, two, back, proj, hidden, sems = refs[2 * count + 2 :]
    cap = blocks[0].shape[0]
    wide, width = two.shape
    copies = Copies(sems)
    loads = [copies.start(block, slot.at[index * cap : (index + 1) * cap]) for index, block in enumerate(blocks)]
    two_load = copies.start(two_ref, two)
    half = width // 2
    one_loads = [copies.start(one_ref.at[start : start + half], one.at[start : start + half]) for start in (0, half)]
    wait(loads)
    stores = [copies.start(slot, slot_out)]
    two_load.wait()
    grad_hidden = dot(slot[:, width:], two[...], COLS)
    one_loads[0].wait()
    both = dot(slot[:, :half], one[:half], PLAIN)
    one_loads[1].wait()
    both = both + dot(slot[:, half:width], one[half:], PLAIN)
    gate, upper = both[:, :wide], both[:, wide:]
    sigma = 1.0 / (1.0 + jnp.exp(-gate))
    silu = gate * sigma
    hidden[...] = (silu * upper).astype(BF16)
    stores.append(copies.start(hidden, hidden_out))
    proj[...] = jnp.concatenate(
        [grad_hidden * upper * sigma * (1.0 + gate * (1.0 - sigma)), grad_hidden * silu], axis=1
    ).astype(BF16)
    stores.append(copies.start(proj, proj_out))
    back[:, :width] = dot(hidden[...], two[...], PLAIN).astype(BF16)
    stores += store_rows(copies, back, outs, slice(0, width))
    back[:, width:] = dot(proj[...], one[...], COLS).astype(BF16)
    stores += store_rows(copies, back, outs, slice(width, 2 * width))
    wait(stores)


def store_rows(copies, source, outs, here):
    cap = outs[0].shape[0]
    return [copies.start(source.at[index * cap : (index + 1) * cap, here], out.at[:, here]) for index, out in enumerate(outs)]


def weight_kernel(end, parts, pieces, number_ref, *refs):
    sources, refs = refs[: 3 * parts], refs[3 * parts :]
    more, refs = refs[: sum(pieces)], refs[sum(pieces) :]
    results, sems = refs[-3 if end else -2 : -1], refs[-1]
    outs, (x, dy, proj, hidden, received) = refs[: -6 - len(results)], refs[-6 - len(results) : -1 - len(results)]
    share, wide = x.shape[1], hidden.shape[1]
    width = sources[0].shape[1] // 2
    first = pl.multiple_of(number_ref[0] * share, share)
    copies = Copies(sems)
    loads = []
    total = 0
    for part in range(parts):
        slot_ref, proj_ref, hidden_ref = sources[3 * part : 3 * part + 3]
        here = slice(total, total + slot_ref.shape[0])
        total = here.stop
        loads.append(copies.start(slot_ref.at[:, pl.ds(first, share)], x.at[here]))
        loads.append(copies.start(slot_ref.at[:, pl.ds(pl.multiple_of(first + width, share), share)], dy.at[here]))
        loads.append(copies.start(proj_ref, proj.at[here]))
        loads.append(copies.start(hidden_ref, hidden.at[here]))
    more_loads = []
    for index, number in enumerate(pieces):
        row = 0
        for ref in more[:number]:
            more_loads.append(copies.start(ref, received.at[index, row : row + ref.shape[0]]))
            row += ref.shape[0]
        more = more[number:]
    wait(loads)
    wait(more_loads)
    step = min(share, 128)
    stores = []
    for start in range(0, share, step):
        here = slice(start, start + step)
        up = dot(x[:, here], proj[...], ROWS)
        for index in range(len(pieces)):
            up = up + received[index, here, : 2 * wide].astype(F32)
        if end:
            results[0][here] = up
            stores.append(copies.start(results[0].at[here], outs[0].at[here]))
            continue
        down = dot(dy[:, here], hidden[...], ROWS)
        for index in range(len(pieces)):
            down = down + received[index, here, 2 * wide : 3 * wide].astype(F32)
        results[0][here, : 2 * wide] = up.astype(BF16)
        results[0][here, 2 * wide : 3 * wide] = down.astype(BF16)
        row = 0
        for out in outs:
            first_row, last_row = max(row, start), min(row + out.shape[0], start + step)
            if first_row < last_row:
                there = out.at[first_row - row : last_row - row]
                stores.append(copies.start(results[0].at[first_row:last_row], there))
            row += out.shape[0]
    if end:
        down = dot(hidden[...], dy[...], ROWS)
        row = lax.broadcasted_iota(jnp.int32, (share, share), 0)
        unit = (row == lax.broadcasted_iota(jnp.int32, (share, share), 1)).astype(BF16)
        for index in range(len(pieces)):
            down = down + dot(received[index, :, 2 * wide : 3 * wide], unit, ROWS)
        results[1][...] = down
        stores.append(copies.start(results[1], outs[1]))
    wait(stores)


def combine_kernel(start, cap, ids_ref, tokens_ref, grad_ref, *refs):
    blocks, (mixed_out, grad_out, ids, data, back, sems) = refs[:-6], refs[-6:]
    copies = Copies(sems)
    ids_load = copies.start(ids_ref, ids)
    pieces = pieces_of(tokens_ref, grad_ref)
    loads = []
    for ref, there, here in pieces:
        loads.append([copies.start(ref.at[:, there], data.at[:, here])])
        for index, block in enumerate(blocks):
            loads[-1].append(copies.start(block.at[:, here], back.at[index * cap : (index + 1) * cap, here]))
    ids_load.wait()
    placing = placing_of(ids[...], len(blocks), start, cap)
    stores = []
    for load, (_, there, here), (out, _, _) in zip(loads, pieces, pieces_of(mixed_out, grad_out)):
        wait(load)
        data[:, here] = (data[:, here].astype(F32) + dot(placing, back[:, here], ROWS)).astype(BF16)
        stores.append(copies.start(data.at[:, here], out.at[:, there]))
    wait(stores)


def after(value, *earlier):
    if not earlier:
        return value
    return lax.optimization_barrier((value, *earlier))[0]


class Lane:
    def __init__(self, window):
        self.window = window
        self.done = []

    def send(self, value, axis, pairs, *earlier):
        if len(self.done) >= self.window:
            earlier = (self.done[-self.window], *earlier)
        self.done.append(lax.ppermute(after(value, *earlier), axis, pairs))
        return self.done[-1]


def rounds_of(experts):
    rounds = [[0] * experts for _ in range(experts)]
    for place in range(experts):
        for mask in range(experts):
            rounds[round_of(place, mask, experts)][place] = place ^ mask
    return rounds


def round_of(place, mask, experts):
    half = experts // 2
    near = mask % half
    if near == 0:
        return 1 if mask else 0
    units = [unit for unit in range(1, half) if bin(unit & near).count("1") % 2 == 0]
    turn = 0
    for bit in range(half.bit_length() if units else 0):
        if units[0] >> bit & 1:
            turn = turn ^ ((place >> bit) & 1)
    return 2 * near + (turn if mask >= half else 1 - turn)


def exchange(blocks, rounds, lane, numbers, *earlier):
    moved = []
    for number in numbers:
        more = earlier if number == numbers[-1] else ()
        moved.append(lane.send(blocks[number], "exp", list(enumerate(rounds[number])), *more))
    return moved


def body(tokens, expert_ids, gate_up_weight, down_weight, grad_out):
    rows, width = tokens.shape
    experts = lax.axis_size("exp")
    groups = lax.axis_size("grp")
    capacity = 2 * rows // experts
    parts = 2 if capacity % 32 == 0 else 1
    cuts = [(part * capacity // parts, capacity // parts) for part in range(parts)]
    weight_one = gate_up_weight[0]
    weight_two = down_weight[0]
    wide = weight_two.shape[0]
    share = width // groups
    sems = pltpu.SemaphoreType.DMA
    ids_here = pltpu.VMEM((1, rows), jnp.int32)

    def halves(cap):
        return [pltpu.VMEM((count, 2 * width), BF16) for count in (rows, experts * cap)]

    lane = Lane(4)
    numbers = range(1, experts)
    ids = expert_ids.reshape(1, rows)
    rounds = rounds_of(experts)
    group = lax.axis_index("grp").astype(jnp.int32)

    def place(start, cap):
        return call(
            lambda *refs: place_kernel(start, cap, *refs),
            "place",
            [like((cap, 2 * width))] * experts,
            [ids_here, *halves(cap), sems((1 + PIECES * (1 + experts),))],
            [ids, tokens, grad_out],
        )

    def expert(blocks):
        slots = experts * blocks[0].shape[0]
        shapes = [(slots, 2 * width), (slots, 2 * wide), (slots, wide)]
        back = [pltpu.VMEM(shape, BF16) for shape in shapes]
        scratch = [back[0], pltpu.VMEM(weight_one.shape, BF16), pltpu.VMEM(weight_two.shape, BF16)]
        outs = call(
            expert_kernel,
            "expert",
            [like(blocks[0].shape)] * experts + [like(shape) for shape in shapes],
            scratch + back + [sems((6 + 3 * experts,))],
            [*blocks, weight_one, weight_two],
        )
        return outs[:experts], outs[experts:]

    def weight_part(number, kept, received, end, heads):
        shape = (share, pl.cdiv(3 * wide, 128) * 128)
        finals = [like((share, 2 * wide), F32), like((wide, share), F32)]
        rows_of = [heads, share - heads] if heads else [share]
        outs = finals if end else [like((count, shape[1])) for count in rows_of]
        total = experts * capacity
        scratch = [pltpu.VMEM((total, width), BF16) for width in (share, share, 2 * wide, wide)]
        scratch.append(pltpu.VMEM((max(1, len(received)), *shape), BF16))
        scratch += [pltpu.VMEM(out.shape, out.dtype) for out in (finals if end else [like(shape)])]
        sources = [array for arrays in kept + received for array in arrays]
        scratch.append(sems((len(sources) + parts + len(outs) + 4 * groups,)))
        pieces = [len(arrays) for arrays in received]
        return call(
            lambda *refs: weight_kernel(end, parts, pieces, *refs),
            "weight_part",
            outs,
            scratch,
            sources,
            scalars=[number[None]],
        )

    def combine(start, cap, first, second, blocks):
        return call(
            lambda *refs: combine_kernel(start, cap, *refs),
            "combine",
            [like((rows, width))] * 2,
            [ids_here, *halves(cap), sems((1 + PIECES * (2 + experts),))],
            [ids, first, second, *blocks],
        )

    sent = [place(*cut) for cut in cuts]
    results = []
    for part in range(parts):
        earlier = [results[-1][0][0]] if results else []
        results.append(expert([sent[part][0]] + exchange(sent[part], rounds, lane, numbers, *earlier)))
    kept = [result[1] for result in results]

    count = len(lane.done)
    mixed, grad = tokens, grad_out
    back = []
    for part in range(parts):
        if back:
            mixed, grad = combine(*cuts[part - 1], mixed, grad, back)
        blocks = results[part][0]
        lane.window = 4 if part else 5
        back = [blocks[0]] + exchange(blocks, rounds, lane, numbers if part < parts - 1 else numbers[:-1])
    done = lane.done[count:]

    received = {q: [] for q in range(groups)}
    sums = kept[0][0]
    held = {groups - 1: done[:4], 2: done[4:6]}
    for q in sorted(range(1, groups), key=lambda q: (q & -q, -q)):
        low = q & -q
        sent = weight_part(group ^ q, [[sums, *kept[0][1:]], *kept[1:]], received[q], False, 16 if q in held else 0)
        sums = after(sums, sent[0])
        pairs = [(i, i ^ low) for i in range(groups)]
        short = Lane(1)
        received[q ^ low].append([short.send(sent[0], "grp", pairs)])
        received[q ^ low][-1] += [short.send(piece, "grp", pairs, *held[q]) for piece in sent[1:]]

    grad_gate_up, grad_down = weight_part(group, [[sums, *kept[0][1:]], *kept[1:]], received[0], True, 0)
    back += exchange(blocks, rounds, lane, numbers[-1:], mixed, lane.done[-3])
    back[0] = after(back[0], grad_gate_up)
    mixed, grad = combine(*cuts[-1], mixed, grad, back)
    return (mixed, grad, grad_gate_up[None], grad_down[None])


def solution(mesh):
    in_specs = (
        P(("grp", "exp"), None),
        P(("grp", "exp"), None),
        P("exp", None, None),
        P("exp", None, None),
        P(("grp", "exp"), None),
    )
    out_specs = (
        P(("grp", "exp"), None),
        P(("grp", "exp"), None),
        P("exp", "grp", None),
        P("exp", None, "grp"),
    )
    return jax.shard_map(body, mesh=mesh, in_specs=in_specs, out_specs=out_specs, check_vma=False)
```

```python
import jax
import jax.numpy as jnp
from jax import lax
from jax.experimental import pallas as pl
from jax.experimental.pallas import tpu as pltpu
from jax.sharding import PartitionSpec as P

VMEM_BYTES = 64 * 1024 * 1024
PIECES = 4
SMALL = pl.CostEstimate(flops=1024, bytes_accessed=1024, transcendentals=0)
BF16 = jnp.bfloat16
F32 = jnp.float32
ROWS = ((0,), (0,))
COLS = ((1,), (1,))
PLAIN = ((1,), (0,))


def dot(left, right, dims):
    return lax.dot_general(left, right, (dims, ((), ())), preferred_element_type=F32)


def like(shape, dtype=BF16):
    return jax.ShapeDtypeStruct(shape, dtype)


def call(kernel, name, outs, scratch, arrays, scalars=()):
    hbm = pl.BlockSpec(memory_space=pltpu.HBM)
    return pl.pallas_call(
        kernel,
        in_specs=[pl.BlockSpec(memory_space=pltpu.SMEM)] * len(scalars) + [hbm] * len(arrays),
        out_specs=[hbm] * len(outs),
        out_shape=outs,
        scratch_shapes=scratch,
        compiler_params=pltpu.CompilerParams(vmem_limit_bytes=VMEM_BYTES),
        cost_estimate=SMALL,
        name=name,
    )(*scalars, *arrays)


class Copies:
    def __init__(self, sems):
        self.sems = sems
        self.used = 0

    def start(self, source, target):
        copy = pltpu.make_async_copy(source, target, self.sems.at[self.used])
        self.used += 1
        copy.start()
        return copy


def wait(copies):
    for copy in copies:
        copy.wait()


def place_kernel(start, cap, ids_ref, tokens_ref, grad_ref, *refs):
    blocks, (ids, data, moved, sems) = refs[:-4], refs[-4:]
    copies = Copies(sems)
    ids_load = copies.start(ids_ref, ids)
    pieces = pieces_of(tokens_ref, grad_ref)
    loads = [copies.start(ref.at[:, there], data.at[:, here]) for ref, there, here in pieces]
    ids_load.wait()
    placing = placing_of(ids[...], len(blocks), start, cap)
    stores = []
    for load, (_, _, here) in zip(loads, pieces):
        load.wait()
        moved[:, here] = dot(placing, data[:, here], PLAIN).astype(BF16)
        stores += store_rows(copies, moved, blocks, here)
    wait(stores)


def pieces_of(first_ref, second_ref):
    width = first_ref.shape[1]
    step = width // (PIECES // 2)
    return [
        (ref, slice(start, start + step), slice(side * width + start, side * width + start + step))
        for side, ref in enumerate((first_ref, second_ref))
        for start in range(0, width, step)
    ]


def placing_of(ids, experts, start, cap):
    rows = ids.shape[1]
    rel = jnp.zeros((1, rows), jnp.int32)
    me = lax.axis_index("exp").astype(jnp.int32)
    for mask in range(1, experts):
        rel = jnp.where(ids == (me ^ mask), round_of(me, mask, experts), rel)
    onehot = lax.broadcasted_iota(jnp.int32, (max(experts, 16), rows), 0) == rel
    before = lax.broadcasted_iota(jnp.int32, (rows, rows), 0) < lax.broadcasted_iota(jnp.int32, (rows, rows), 1)
    ranks = dot(onehot.astype(BF16), before.astype(BF16), PLAIN)
    rank = jnp.sum(jnp.where(onehot, ranks, 0.0), axis=0, keepdims=True).astype(jnp.int32) - start
    target = jnp.where((rank >= 0) & (rank < cap), rel * cap + rank, -1)
    return (lax.broadcasted_iota(jnp.int32, (experts * cap, rows), 0) == target).astype(BF16)


def expert_kernel(*refs):
    count = (len(refs) - 12) // 2
    blocks, (one_ref, two_ref), outs = refs[:count], refs[count : count + 2], refs[count + 2 : 2 * count + 2]
    slot_out, proj_out, hidden_out, slot, one, two, back, proj, hidden, sems = refs[2 * count + 2 :]
    cap = blocks[0].shape[0]
    wide, width = two.shape
    copies = Copies(sems)
    loads = [copies.start(block, slot.at[index * cap : (index + 1) * cap]) for index, block in enumerate(blocks)]
    two_load = copies.start(two_ref, two)
    half = width // 2
    one_loads = [copies.start(one_ref.at[start : start + half], one.at[start : start + half]) for start in (0, half)]
    wait(loads)
    stores = [copies.start(slot, slot_out)]
    two_load.wait()
    grad_hidden = dot(slot[:, width:], two[...], COLS)
    one_loads[0].wait()
    both = dot(slot[:, :half], one[:half], PLAIN)
    one_loads[1].wait()
    both = both + dot(slot[:, half:width], one[half:], PLAIN)
    gate, upper = both[:, :wide], both[:, wide:]
    sigma = 1.0 / (1.0 + jnp.exp(-gate))
    silu = gate * sigma
    hidden[...] = (silu * upper).astype(BF16)
    stores.append(copies.start(hidden, hidden_out))
    proj[...] = jnp.concatenate(
        [grad_hidden * upper * sigma * (1.0 + gate * (1.0 - sigma)), grad_hidden * silu], axis=1
    ).astype(BF16)
    stores.append(copies.start(proj, proj_out))
    back[:, :width] = dot(hidden[...], two[...], PLAIN).astype(BF16)
    stores += store_rows(copies, back, outs, slice(0, width))
    back[:, width:] = dot(proj[...], one[...], COLS).astype(BF16)
    stores += store_rows(copies, back, outs, slice(width, 2 * width))
    wait(stores)


def store_rows(copies, source, outs, here):
    cap = outs[0].shape[0]
    return [copies.start(source.at[index * cap : (index + 1) * cap, here], out.at[:, here]) for index, out in enumerate(outs)]


def weight_kernel(end, parts, pieces, number_ref, *refs):
    sources, refs = refs[: 3 * parts], refs[3 * parts :]
    more, refs = refs[: sum(pieces)], refs[sum(pieces) :]
    results, sems = refs[-3 if end else -2 : -1], refs[-1]
    outs, (x, dy, proj, hidden, received) = refs[: -6 - len(results)], refs[-6 - len(results) : -1 - len(results)]
    share, wide = x.shape[1], hidden.shape[1]
    width = sources[0].shape[1] // 2
    first = pl.multiple_of(number_ref[0] * share, share)
    copies = Copies(sems)
    loads = []
    total = 0
    for part in range(parts):
        slot_ref, proj_ref, hidden_ref = sources[3 * part : 3 * part + 3]
        here = slice(total, total + slot_ref.shape[0])
        total = here.stop
        loads.append(copies.start(slot_ref.at[:, pl.ds(first, share)], x.at[here]))
        loads.append(copies.start(slot_ref.at[:, pl.ds(pl.multiple_of(first + width, share), share)], dy.at[here]))
        loads.append(copies.start(proj_ref, proj.at[here]))
        loads.append(copies.start(hidden_ref, hidden.at[here]))
    more_loads = []
    for index, number in enumerate(pieces):
        row = 0
        for ref in more[:number]:
            more_loads.append(copies.start(ref, received.at[index, row : row + ref.shape[0]]))
            row += ref.shape[0]
        more = more[number:]
    wait(loads)
    wait(more_loads)
    step = min(share, 128)
    stores = []
    for start in range(0, share, step):
        here = slice(start, start + step)
        up = dot(x[:, here], proj[...], ROWS)
        for index in range(len(pieces)):
            up = up + received[index, here, : 2 * wide].astype(F32)
        if end:
            results[0][here] = up
            stores.append(copies.start(results[0].at[here], outs[0].at[here]))
            continue
        down = dot(dy[:, here], hidden[...], ROWS)
        for index in range(len(pieces)):
            down = down + received[index, here, 2 * wide : 3 * wide].astype(F32)
        results[0][here, : 2 * wide] = up.astype(BF16)
        results[0][here, 2 * wide : 3 * wide] = down.astype(BF16)
        row = 0
        for out in outs:
            first_row, last_row = max(row, start), min(row + out.shape[0], start + step)
            if first_row < last_row:
                there = out.at[first_row - row : last_row - row]
                stores.append(copies.start(results[0].at[first_row:last_row], there))
            row += out.shape[0]
    if end:
        down = dot(hidden[...], dy[...], ROWS)
        row = lax.broadcasted_iota(jnp.int32, (share, share), 0)
        unit = (row == lax.broadcasted_iota(jnp.int32, (share, share), 1)).astype(BF16)
        for index in range(len(pieces)):
            down = down + dot(received[index, :, 2 * wide : 3 * wide], unit, ROWS)
        results[1][...] = down
        stores.append(copies.start(results[1], outs[1]))
    wait(stores)


def combine_kernel(start, cap, ids_ref, tokens_ref, grad_ref, *refs):
    blocks, (mixed_out, grad_out, ids, data, back, sems) = refs[:-6], refs[-6:]
    copies = Copies(sems)
    ids_load = copies.start(ids_ref, ids)
    pieces = pieces_of(tokens_ref, grad_ref)
    loads = []
    for ref, there, here in pieces:
        loads.append([copies.start(ref.at[:, there], data.at[:, here])])
        for index, block in enumerate(blocks):
            loads[-1].append(copies.start(block.at[:, here], back.at[index * cap : (index + 1) * cap, here]))
    ids_load.wait()
    placing = placing_of(ids[...], len(blocks), start, cap)
    stores = []
    for load, (_, there, here), (out, _, _) in zip(loads, pieces, pieces_of(mixed_out, grad_out)):
        wait(load)
        data[:, here] = (data[:, here].astype(F32) + dot(placing, back[:, here], ROWS)).astype(BF16)
        stores.append(copies.start(data.at[:, here], out.at[:, there]))
    wait(stores)


def after(value, *earlier):
    if not earlier:
        return value
    return lax.optimization_barrier((value, *earlier))[0]


class Lane:
    def __init__(self, window):
        self.window = window
        self.done = []

    def send(self, value, axis, pairs, *earlier):
        if len(self.done) >= self.window:
            earlier = (self.done[-self.window], *earlier)
        self.done.append(lax.ppermute(after(value, *earlier), axis, pairs))
        return self.done[-1]


def rounds_of(experts):
    rounds = [[0] * experts for _ in range(experts)]
    for place in range(experts):
        for mask in range(experts):
            rounds[round_of(place, mask, experts)][place] = place ^ mask
    return rounds


def round_of(place, mask, experts):
    half = experts // 2
    near = mask % half
    if near == 0:
        return experts - 1 if mask else 0
    units = [unit for unit in range(1, half) if bin(unit & near).count("1") % 2 == 0]
    turn = 0
    for bit in range(half.bit_length() if units else 0):
        if units[0] >> bit & 1:
            turn = turn ^ ((place >> bit) & 1)
    return 2 * near - 1 + (turn if mask >= half else 1 - turn)


def exchange(blocks, rounds, lane, numbers, *earlier):
    moved = []
    for number in numbers:
        more = earlier if number == numbers[-1] else ()
        moved.append(lane.send(blocks[number], "exp", list(enumerate(rounds[number])), *more))
    return moved


def body(tokens, expert_ids, gate_up_weight, down_weight, grad_out):
    rows, width = tokens.shape
    experts = lax.axis_size("exp")
    groups = lax.axis_size("grp")
    capacity = 2 * rows // experts
    parts = 2 if capacity % 32 == 0 else 1
    cuts = [(part * capacity // parts, capacity // parts) for part in range(parts)]
    weight_one = gate_up_weight[0]
    weight_two = down_weight[0]
    wide = weight_two.shape[0]
    share = width // groups
    sems = pltpu.SemaphoreType.DMA
    ids_here = pltpu.VMEM((1, rows), jnp.int32)

    def halves(cap):
        return [pltpu.VMEM((count, 2 * width), BF16) for count in (rows, experts * cap)]

    lane = Lane(4)
    numbers = range(1, experts)
    ids = expert_ids.reshape(1, rows)
    rounds = rounds_of(experts)
    group = lax.axis_index("grp").astype(jnp.int32)

    def place(start, cap):
        return call(
            lambda *refs: place_kernel(start, cap, *refs),
            "place",
            [like((cap, 2 * width))] * experts,
            [ids_here, *halves(cap), sems((1 + PIECES * (1 + experts),))],
            [ids, tokens, grad_out],
        )

    def expert(blocks):
        slots = experts * blocks[0].shape[0]
        shapes = [(slots, 2 * width), (slots, 2 * wide), (slots, wide)]
        back = [pltpu.VMEM(shape, BF16) for shape in shapes]
        scratch = [back[0], pltpu.VMEM(weight_one.shape, BF16), pltpu.VMEM(weight_two.shape, BF16)]
        outs = call(
            expert_kernel,
            "expert",
            [like(blocks[0].shape)] * experts + [like(shape) for shape in shapes],
            scratch + back + [sems((6 + 3 * experts,))],
            [*blocks, weight_one, weight_two],
        )
        return outs[:experts], outs[experts:]

    def weight_part(number, kept, received, end, heads):
        shape = (share, pl.cdiv(3 * wide, 128) * 128)
        finals = [like((share, 2 * wide), F32), like((wide, share), F32)]
        rows_of = [heads, share - heads] if heads else [share]
        outs = finals if end else [like((count, shape[1])) for count in rows_of]
        total = experts * capacity
        scratch = [pltpu.VMEM((total, width), BF16) for width in (share, share, 2 * wide, wide)]
        scratch.append(pltpu.VMEM((max(1, len(received)), *shape), BF16))
        scratch += [pltpu.VMEM(out.shape, out.dtype) for out in (finals if end else [like(shape)])]
        sources = [array for arrays in kept + received for array in arrays]
        scratch.append(sems((len(sources) + parts + len(outs) + 4 * groups,)))
        pieces = [len(arrays) for arrays in received]
        return call(
            lambda *refs: weight_kernel(end, parts, pieces, *refs),
            "weight_part",
            outs,
            scratch,
            sources,
            scalars=[number[None]],
        )

    def combine(start, cap, first, second, blocks):
        return call(
            lambda *refs: combine_kernel(start, cap, *refs),
            "combine",
            [like((rows, width))] * 2,
            [ids_here, *halves(cap), sems((1 + PIECES * (2 + experts),))],
            [ids, first, second, *blocks],
        )

    sent = [place(*cut) for cut in cuts]
    results = []
    for part in range(parts):
        earlier = [results[-1][0][0]] if results else []
        results.append(expert([sent[part][0]] + exchange(sent[part], rounds, lane, numbers, *earlier)))
    kept = [result[1] for result in results]

    count = len(lane.done)
    mixed, grad = tokens, grad_out
    back = []
    for part in range(parts):
        if back:
            mixed, grad = combine(*cuts[part - 1], mixed, grad, back)
        blocks = results[part][0]
        lane.window = 3 if part else 5
        back = [blocks[0]] + exchange(blocks, rounds, lane, numbers if part < parts - 1 else numbers[:-1])
    done = lane.done[count:]

    received = {q: [] for q in range(groups)}
    sums = kept[0][0]
    held = {groups - 1: done[:4], 2: done[4:6]}
    for q in sorted(range(1, groups), key=lambda q: (q & -q, -q)):
        low = q & -q
        sent = weight_part(group ^ q, [[sums, *kept[0][1:]], *kept[1:]], received[q], False, 16 if q in held else 0)
        sums = after(sums, sent[0])
        pairs = [(i, i ^ low) for i in range(groups)]
        short = Lane(1)
        received[q ^ low].append([short.send(sent[0], "grp", pairs)])
        received[q ^ low][-1] += [short.send(piece, "grp", pairs, *held[q]) for piece in sent[1:]]

    grad_gate_up, grad_down = weight_part(group, [[sums, *kept[0][1:]], *kept[1:]], received[0], True, 0)
    back += exchange(blocks, rounds, lane, numbers[-1:], mixed, lane.done[-3])
    back[0] = after(back[0], grad_gate_up)
    mixed, grad = combine(*cuts[-1], mixed, grad, back)
    return (mixed, grad, grad_gate_up[None], grad_down[None])


def solution(mesh):
    in_specs = (
        P(("grp", "exp"), None),
        P(("grp", "exp"), None),
        P("exp", None, None),
        P("exp", None, None),
        P(("grp", "exp"), None),
    )
    out_specs = (
        P(("grp", "exp"), None),
        P(("grp", "exp"), None),
        P("exp", "grp", None),
        P("exp", None, "grp"),
    )
    return jax.shard_map(body, mesh=mesh, in_specs=in_specs, out_specs=out_specs, check_vma=False)
```

```python
import jax
import jax.numpy as jnp
from jax import lax
from jax.experimental import pallas as pl
from jax.experimental.pallas import tpu as pltpu
from jax.sharding import PartitionSpec as P

VMEM_BYTES = 64 * 1024 * 1024
PIECES = 2
SMALL = pl.CostEstimate(flops=1024, bytes_accessed=1024, transcendentals=0)
BF16 = jnp.bfloat16
F32 = jnp.float32
ROWS = ((0,), (0,))
COLS = ((1,), (1,))
PLAIN = ((1,), (0,))


def dot(left, right, dims):
    return lax.dot_general(left, right, (dims, ((), ())), preferred_element_type=F32)


def like(shape, dtype=BF16):
    return jax.ShapeDtypeStruct(shape, dtype)


def call(kernel, name, outs, scratch, arrays, scalars=()):
    hbm = pl.BlockSpec(memory_space=pltpu.HBM)
    return pl.pallas_call(
        kernel,
        in_specs=[pl.BlockSpec(memory_space=pltpu.SMEM)] * len(scalars) + [hbm] * len(arrays),
        out_specs=[hbm] * len(outs),
        out_shape=outs,
        scratch_shapes=scratch,
        compiler_params=pltpu.CompilerParams(vmem_limit_bytes=VMEM_BYTES),
        cost_estimate=SMALL,
        name=name,
    )(*scalars, *arrays)


class Copies:
    def __init__(self, sems):
        self.sems = sems
        self.used = 0

    def start(self, source, target):
        copy = pltpu.make_async_copy(source, target, self.sems.at[self.used])
        self.used += 1
        copy.start()
        return copy


def wait(copies):
    for copy in copies:
        copy.wait()


def place_kernel(start, cap, ids_ref, tokens_ref, grad_ref, *refs):
    blocks, (ids, data, moved, sems) = refs[:-4], refs[-4:]
    copies = Copies(sems)
    ids_load = copies.start(ids_ref, ids)
    pieces = pieces_of(tokens_ref, grad_ref)
    loads = [copies.start(ref.at[:, there], data.at[:, here]) for ref, there, here in pieces]
    ids_load.wait()
    placing = placing_of(ids[...], len(blocks), start, cap)
    stores = []
    for load, (_, _, here) in zip(loads, pieces):
        load.wait()
        moved[:, here] = dot(placing, data[:, here], PLAIN).astype(BF16)
        stores += store_rows(copies, moved, blocks, here)
    wait(stores)


def pieces_of(first_ref, second_ref):
    width = first_ref.shape[1]
    step = width // (PIECES // 2)
    return [
        (ref, slice(start, start + step), slice(side * width + start, side * width + start + step))
        for side, ref in enumerate((first_ref, second_ref))
        for start in range(0, width, step)
    ]


def placing_of(ids, experts, start, cap):
    rows = ids.shape[1]
    rel = jnp.zeros((1, rows), jnp.int32)
    me = lax.axis_index("exp").astype(jnp.int32)
    for mask in range(1, experts):
        rel = jnp.where(ids == (me ^ mask), round_of(me, mask, experts), rel)
    onehot = lax.broadcasted_iota(jnp.int32, (max(experts, 16), rows), 0) == rel
    before = lax.broadcasted_iota(jnp.int32, (rows, rows), 0) < lax.broadcasted_iota(jnp.int32, (rows, rows), 1)
    ranks = dot(onehot.astype(BF16), before.astype(BF16), PLAIN)
    rank = jnp.sum(jnp.where(onehot, ranks, 0.0), axis=0, keepdims=True).astype(jnp.int32) - start
    target = jnp.where((rank >= 0) & (rank < cap), rel * cap + rank, -1)
    return (lax.broadcasted_iota(jnp.int32, (experts * cap, rows), 0) == target).astype(BF16)


def expert_kernel(*refs):
    count = (len(refs) - 12) // 2
    blocks, (one_ref, two_ref), outs = refs[:count], refs[count : count + 2], refs[count + 2 : 2 * count + 2]
    slot_out, proj_out, hidden_out, slot, one, two, back, proj, hidden, sems = refs[2 * count + 2 :]
    cap = blocks[0].shape[0]
    wide, width = two.shape
    copies = Copies(sems)
    loads = [copies.start(block, slot.at[index * cap : (index + 1) * cap]) for index, block in enumerate(blocks)]
    two_load = copies.start(two_ref, two)
    half = width // 2
    one_loads = [copies.start(one_ref.at[start : start + half], one.at[start : start + half]) for start in (0, half)]
    wait(loads)
    stores = [copies.start(slot, slot_out)]
    two_load.wait()
    grad_hidden = dot(slot[:, width:], two[...], COLS)
    one_loads[0].wait()
    both = dot(slot[:, :half], one[:half], PLAIN)
    one_loads[1].wait()
    both = both + dot(slot[:, half:width], one[half:], PLAIN)
    gate, upper = both[:, :wide], both[:, wide:]
    sigma = 1.0 / (1.0 + jnp.exp(-gate))
    silu = gate * sigma
    hidden[...] = (silu * upper).astype(BF16)
    stores.append(copies.start(hidden, hidden_out))
    proj[...] = jnp.concatenate(
        [grad_hidden * upper * sigma * (1.0 + gate * (1.0 - sigma)), grad_hidden * silu], axis=1
    ).astype(BF16)
    stores.append(copies.start(proj, proj_out))
    back[:, :width] = dot(hidden[...], two[...], PLAIN).astype(BF16)
    stores += store_rows(copies, back, outs, slice(0, width))
    back[:, width:] = dot(proj[...], one[...], COLS).astype(BF16)
    stores += store_rows(copies, back, outs, slice(width, 2 * width))
    wait(stores)


def store_rows(copies, source, outs, here):
    cap = outs[0].shape[0]
    return [copies.start(source.at[index * cap : (index + 1) * cap, here], out.at[:, here]) for index, out in enumerate(outs)]


def weight_kernel(end, parts, pieces, number_ref, *refs):
    sources, refs = refs[: 3 * parts], refs[3 * parts :]
    more, refs = refs[: sum(pieces)], refs[sum(pieces) :]
    results, sems = refs[-3 if end else -2 : -1], refs[-1]
    outs, (x, dy, proj, hidden, received) = refs[: -6 - len(results)], refs[-6 - len(results) : -1 - len(results)]
    share, wide = x.shape[1], hidden.shape[1]
    width = sources[0].shape[1] // 2
    first = pl.multiple_of(number_ref[0] * share, share)
    copies = Copies(sems)
    loads = []
    total = 0
    for part in range(parts):
        slot_ref, proj_ref, hidden_ref = sources[3 * part : 3 * part + 3]
        here = slice(total, total + slot_ref.shape[0])
        total = here.stop
        loads.append(copies.start(slot_ref.at[:, pl.ds(first, share)], x.at[here]))
        loads.append(copies.start(slot_ref.at[:, pl.ds(pl.multiple_of(first + width, share), share)], dy.at[here]))
        loads.append(copies.start(proj_ref, proj.at[here]))
        loads.append(copies.start(hidden_ref, hidden.at[here]))
    more_loads = []
    for index, number in enumerate(pieces):
        row = 0
        for ref in more[:number]:
            more_loads.append(copies.start(ref, received.at[index, row : row + ref.shape[0]]))
            row += ref.shape[0]
        more = more[number:]
    wait(loads)
    wait(more_loads)
    step = min(share, 128)
    stores = []
    for start in range(0, share, step):
        here = slice(start, start + step)
        up = dot(x[:, here], proj[...], ROWS)
        for index in range(len(pieces)):
            up = up + received[index, here, : 2 * wide].astype(F32)
        if end:
            results[0][here] = up
            stores.append(copies.start(results[0].at[here], outs[0].at[here]))
            continue
        down = dot(dy[:, here], hidden[...], ROWS)
        for index in range(len(pieces)):
            down = down + received[index, here, 2 * wide : 3 * wide].astype(F32)
        results[0][here, : 2 * wide] = up.astype(BF16)
        results[0][here, 2 * wide : 3 * wide] = down.astype(BF16)
        row = 0
        for out in outs:
            first_row, last_row = max(row, start), min(row + out.shape[0], start + step)
            if first_row < last_row:
                there = out.at[first_row - row : last_row - row]
                stores.append(copies.start(results[0].at[first_row:last_row], there))
            row += out.shape[0]
    if end:
        down = dot(hidden[...], dy[...], ROWS)
        row = lax.broadcasted_iota(jnp.int32, (share, share), 0)
        unit = (row == lax.broadcasted_iota(jnp.int32, (share, share), 1)).astype(BF16)
        for index in range(len(pieces)):
            down = down + dot(received[index, :, 2 * wide : 3 * wide], unit, ROWS)
        results[1][...] = down
        stores.append(copies.start(results[1], outs[1]))
    wait(stores)


def combine_kernel(start, cap, ids_ref, tokens_ref, grad_ref, *refs):
    blocks, (mixed_out, grad_out, ids, data, back, sems) = refs[:-6], refs[-6:]
    copies = Copies(sems)
    ids_load = copies.start(ids_ref, ids)
    pieces = pieces_of(tokens_ref, grad_ref)
    loads = []
    for ref, there, here in pieces:
        loads.append([copies.start(ref.at[:, there], data.at[:, here])])
        for index, block in enumerate(blocks):
            loads[-1].append(copies.start(block.at[:, here], back.at[index * cap : (index + 1) * cap, here]))
    ids_load.wait()
    placing = placing_of(ids[...], len(blocks), start, cap)
    stores = []
    for load, (_, there, here), (out, _, _) in zip(loads, pieces, pieces_of(mixed_out, grad_out)):
        wait(load)
        data[:, here] = (data[:, here].astype(F32) + dot(placing, back[:, here], ROWS)).astype(BF16)
        stores.append(copies.start(data.at[:, here], out.at[:, there]))
    wait(stores)


def after(value, *earlier):
    if not earlier:
        return value
    return lax.optimization_barrier((value, *earlier))[0]


class Lane:
    def __init__(self, window):
        self.window = window
        self.done = []

    def send(self, value, axis, pairs, *earlier):
        if len(self.done) >= self.window:
            earlier = (self.done[-self.window], *earlier)
        self.done.append(lax.ppermute(after(value, *earlier), axis, pairs))
        return self.done[-1]


def rounds_of(experts):
    rounds = [[0] * experts for _ in range(experts)]
    for place in range(experts):
        for mask in range(experts):
            rounds[round_of(place, mask, experts)][place] = place ^ mask
    return rounds


def round_of(place, mask, experts):
    half = experts // 2
    near = mask % half
    if near == 0:
        return experts - 1 if mask else 0
    units = [unit for unit in range(1, half) if bin(unit & near).count("1") % 2 == 0]
    turn = 0
    for bit in range(half.bit_length() if units else 0):
        if units[0] >> bit & 1:
            turn = turn ^ ((place >> bit) & 1)
    return 2 * near - 1 + (turn if mask >= half else 1 - turn)


def exchange(blocks, rounds, lane, numbers, *earlier):
    moved = []
    for number in numbers:
        more = earlier if number == numbers[-1] else ()
        moved.append(lane.send(blocks[number], "exp", list(enumerate(rounds[number])), *more))
    return moved


def body(tokens, expert_ids, gate_up_weight, down_weight, grad_out):
    rows, width = tokens.shape
    experts = lax.axis_size("exp")
    groups = lax.axis_size("grp")
    capacity = 2 * rows // experts
    parts = 2 if capacity % 32 == 0 else 1
    cuts = [(part * capacity // parts, capacity // parts) for part in range(parts)]
    weight_one = gate_up_weight[0]
    weight_two = down_weight[0]
    wide = weight_two.shape[0]
    share = width // groups
    sems = pltpu.SemaphoreType.DMA
    ids_here = pltpu.VMEM((1, rows), jnp.int32)

    def halves(cap):
        return [pltpu.VMEM((count, 2 * width), BF16) for count in (rows, experts * cap)]

    lane = Lane(4)
    numbers = range(1, experts)
    ids = expert_ids.reshape(1, rows)
    rounds = rounds_of(experts)
    group = lax.axis_index("grp").astype(jnp.int32)

    def place(start, cap):
        return call(
            lambda *refs: place_kernel(start, cap, *refs),
            "place",
            [like((cap, 2 * width))] * experts,
            [ids_here, *halves(cap), sems((1 + PIECES * (1 + experts),))],
            [ids, tokens, grad_out],
        )

    def expert(blocks):
        slots = experts * blocks[0].shape[0]
        shapes = [(slots, 2 * width), (slots, 2 * wide), (slots, wide)]
        back = [pltpu.VMEM(shape, BF16) for shape in shapes]
        scratch = [back[0], pltpu.VMEM(weight_one.shape, BF16), pltpu.VMEM(weight_two.shape, BF16)]
        outs = call(
            expert_kernel,
            "expert",
            [like(blocks[0].shape)] * experts + [like(shape) for shape in shapes],
            scratch + back + [sems((6 + 3 * experts,))],
            [*blocks, weight_one, weight_two],
        )
        return outs[:experts], outs[experts:]

    def weight_part(number, kept, received, end, heads):
        shape = (share, pl.cdiv(3 * wide, 128) * 128)
        finals = [like((share, 2 * wide), F32), like((wide, share), F32)]
        rows_of = [heads, share - heads] if heads else [share]
        outs = finals if end else [like((count, shape[1])) for count in rows_of]
        total = experts * capacity
        scratch = [pltpu.VMEM((total, width), BF16) for width in (share, share, 2 * wide, wide)]
        scratch.append(pltpu.VMEM((max(1, len(received)), *shape), BF16))
        scratch += [pltpu.VMEM(out.shape, out.dtype) for out in (finals if end else [like(shape)])]
        sources = [array for arrays in kept + received for array in arrays]
        scratch.append(sems((len(sources) + parts + len(outs) + 4 * groups,)))
        pieces = [len(arrays) for arrays in received]
        return call(
            lambda *refs: weight_kernel(end, parts, pieces, *refs),
            "weight_part",
            outs,
            scratch,
            sources,
            scalars=[number[None]],
        )

    def combine(start, cap, first, second, blocks):
        return call(
            lambda *refs: combine_kernel(start, cap, *refs),
            "combine",
            [like((rows, width))] * 2,
            [ids_here, *halves(cap), sems((1 + PIECES * (2 + experts),))],
            [ids, first, second, *blocks],
        )

    sent = [place(*cut) for cut in cuts]
    results = []
    for part in range(parts):
        earlier = [results[-1][0][0]] if results else []
        results.append(expert([sent[part][0]] + exchange(sent[part], rounds, lane, numbers, *earlier)))
    kept = [result[1] for result in results]

    count = len(lane.done)
    mixed, grad = tokens, grad_out
    back = []
    for part in range(parts):
        if back:
            mixed, grad = combine(*cuts[part - 1], mixed, grad, back)
        blocks = results[part][0]
        lane.window = 4 if part else 5
        back = [blocks[0]] + exchange(blocks, rounds, lane, numbers if part < parts - 1 else numbers[:-1])
    done = lane.done[count:]

    received = {q: [] for q in range(groups)}
    sums = kept[0][0]
    held = {groups - 1: done[:4], 2: done[4:6]}
    for q in sorted(range(1, groups), key=lambda q: (q & -q, -q)):
        low = q & -q
        sent = weight_part(group ^ q, [[sums, *kept[0][1:]], *kept[1:]], received[q], False, 16 if q in held else 0)
        sums = after(sums, sent[0])
        pairs = [(i, i ^ low) for i in range(groups)]
        short = Lane(1)
        received[q ^ low].append([short.send(sent[0], "grp", pairs)])
        received[q ^ low][-1] += [short.send(piece, "grp", pairs, *held[q]) for piece in sent[1:]]

    grad_gate_up, grad_down = weight_part(group, [[sums, *kept[0][1:]], *kept[1:]], received[0], True, 0)
    back += exchange(blocks, rounds, lane, numbers[-1:], mixed, lane.done[-3])
    back[0] = after(back[0], grad_gate_up)
    mixed, grad = combine(*cuts[-1], mixed, grad, back)
    return (mixed, grad, grad_gate_up[None], grad_down[None])


def solution(mesh):
    in_specs = (
        P(("grp", "exp"), None),
        P(("grp", "exp"), None),
        P("exp", None, None),
        P("exp", None, None),
        P(("grp", "exp"), None),
    )
    out_specs = (
        P(("grp", "exp"), None),
        P(("grp", "exp"), None),
        P("exp", "grp", None),
        P("exp", None, "grp"),
    )
    return jax.shard_map(body, mesh=mesh, in_specs=in_specs, out_specs=out_specs, check_vma=False)
```
